32 devices in a mesh: lon: 8 (over z, y), lat: 2 (over x), section: 2 (over core).
Axes of the slice: x: 2, y: 2, z: 4, core: 2. Of those that a mesh axis runs over, the one named last changes fastest.
Arguments:
- upper_fields: bfloat16 [5, 6, 48, 384], P(None, None, 'lat', 'lon'), may hold values from -6 to 6
- surface_fields: bfloat16 [4, 48, 384], P(None, 'lat', 'lon'), may hold values from -6 to 6
- upper_embed: bfloat16 [160, 192], replicated, may hold values from -0.5 to 0.5
- surface_embed: bfloat16 [64, 192], replicated, may hold values from -0.75 to 0.75
- norm_gains: float32 [2, 2, 192], replicated, may hold values from 0.1 to 1.9
- qkv_weight: bfloat16 [2, 192, 576], replicated, may hold values from -0.4375 to 0.4375
- proj_weight: bfloat16 [2, 192, 192], replicated, may hold values from -0.4375 to 0.4375
- up_weight: bfloat16 [2, 192, 768], replicated, may hold values from -0.4375 to 0.4375
- down_weight: bfloat16 [2, 768, 192], replicated, may hold values from -0.21875 to 0.21875
- earth_bias: float32 [2, 2, 2, 6, 3312], P(None, 'lat', 'section'), may hold values from -4 to 402
- out_grad: bfloat16 [4, 12, 96, 192], P('section', 'lat', 'lon'), may hold values from -6 to 6
Outputs:
- latent_grad: bfloat16 [4, 12, 96, 192], P('section', 'lat', 'lon')
- upper_embed_grad: float32 [160, 192], replicated
- surface_embed_grad: float32 [64, 192], replicated
The draws below stay inside these ranges and needn't reach their ends.
All inputs are finite; a program needn't handle non-finite values.
Results may differ from the reference program's by a relative error of at most 0.024.
Values may be sent and summed in bfloat16 or wider, within the bound.
No kernel may reach another device: no remote copies, remote signals or barrier semaphores. Data moves between devices by JAX's collectives and lax.ppermute only.
A program may use at most 64 MiB of HBM per device.

```python
import jax
import jax.numpy as jnp
import numpy as np
from jax import lax

D = 192
HEADS = 6
FF = 768
LZ = 4
UV = 5
SV = 4
BLOCKS = 2
LAT = 12
LON = 96
LATR = 48
LONR = 384
PL = 6
LATW = 2
ZW = 2
NPOS = 3312
UP_IN = 160
SF_IN = 64


def draw_earth_bias(key, part):
    shape = (BLOCKS, LATW, ZW, HEADS, NPOS)
    subkeys = jax.random.split(key, 1)
    table = jnp.clip(jax.random.normal(subkeys[0], shape, jnp.float32), -4.0, 4.0)
    return table.astype(jnp.float32)


def level_of(stream_key, extent, cuts, smallest, largest):
    loudness, own = 1.0, jax.random.fold_in(stream_key, 6)
    for dim, shards_of in cuts:
        heights = jnp.exp(jax.random.uniform(jax.random.fold_in(own, dim), (shards_of,), jnp.float32, smallest / len(cuts), largest / len(cuts)))
        loudness = loudness * jnp.repeat(heights, extent[dim] // shards_of).reshape([-1 if axis == dim else 1 for axis in range(len(extent))])
    return loudness


def scatter_about(stream_key, shape, scale, bound, pieces=(), held_as=jnp.bfloat16):
    level = level_of(stream_key, shape, pieces, -0.22, 0.18) if pieces else 1.0
    drawn = jax.random.normal(stream_key, shape, jnp.float32) * scale * level
    return jnp.minimum(jnp.maximum(drawn, -bound), bound).astype(held_as)


def setup_inputs(seed: int = 0) -> dict:
    arg_keys = jax.random.split(jax.random.key(seed), 12)
    return {
        "upper_fields": scatter_about(arg_keys[0], (UV, PL, LATR, LONR), 1.0, 6.0, ((2, 2), (3, 8))),
        "surface_fields": scatter_about(arg_keys[1], (SV, LATR, LONR), 1.0, 6.0, ((1, 2), (2, 8))),
        "upper_embed": scatter_about(arg_keys[2], (UP_IN, D), UP_IN ** -0.5, 0.5),
        "surface_embed": scatter_about(arg_keys[3], (SF_IN, D), SF_IN ** -0.5, 0.75),
        "norm_gains": jnp.clip(1.0 + 0.18 * jax.random.normal(arg_keys[4], (BLOCKS, 2, D), jnp.float32), 0.1, 1.9),
        "qkv_weight": scatter_about(arg_keys[5], (BLOCKS, D, 3 * D), D ** -0.5, 0.4375),
        "proj_weight": scatter_about(arg_keys[6], (BLOCKS, D, D), D ** -0.5, 0.4375),
        "up_weight": scatter_about(arg_keys[7], (BLOCKS, D, FF), D ** -0.5, 0.4375),
        "down_weight": scatter_about(arg_keys[8], (BLOCKS, FF, D), FF ** -0.5, 0.21875),
        "earth_bias": draw_earth_bias(jax.random.fold_in(arg_keys[11], 71), 0),
        "out_grad": scatter_about(arg_keys[10], (LZ, LAT, LON, D), 1.0, 6.0, ((0, 2), (1, 2), (2, 8))),
    }


neg_fill = -1e+30
norm_eps = 1e-05

def layer_norm(values, gain):
    average = lax.optimization_barrier(jnp.mean(values, -1, keepdims=True))
    centred = values - average
    variance = lax.optimization_barrier(jnp.mean(centred * centred, -1, keepdims=True))
    return centred * lax.rsqrt(variance + norm_eps) * gain

def pinned(values):
    return lax.optimization_barrier(values.astype(jnp.bfloat16))

def bias_index():
    token = np.arange(144)
    level_part = token // 72
    row_part = token // 12 % 6
    col_part = token % 12
    pair = (level_part[:, None] * 2 + level_part[None, :]) * 36 + row_part[:, None] * 6 + row_part[None, :]
    return pair * 23 + col_part[:, None] - col_part[None, :] + 11

def make_patches(upper_fields, surface_fields):
    up_vars, raw_levels, raw_rows, raw_cols = upper_fields.shape
    upper_patch = upper_fields.reshape(up_vars, raw_levels // 2, 2, raw_rows // 4, 4, raw_cols // 4, 4)
    upper_patch = upper_patch.transpose(1, 3, 5, 0, 2, 4, 6).reshape(raw_levels // 2, raw_rows // 4, raw_cols // 4, up_vars * 32)
    sf_vars = surface_fields.shape[0]
    surface_patch = surface_fields.reshape(sf_vars, raw_rows // 4, 4, raw_cols // 4, 4)
    surface_patch = surface_patch.transpose(1, 3, 0, 2, 4).reshape(raw_rows // 4, raw_cols // 4, sf_vars * 16)
    return (upper_patch, surface_patch)

def region_valid(levels_total, rows_total, group, shifted):
    token = jnp.arange(144, dtype=jnp.int32)
    level = jnp.arange(levels_total // 2, dtype=jnp.int32)[:, None] * 2 + token[None, :] // 72
    row = group * 6 + token // 12 % 6
    zone_level = (level >= levels_total - 2).astype(jnp.int32) + (level >= levels_total - 1).astype(jnp.int32)
    zone_row = (row >= rows_total - 6).astype(jnp.int32) + (row >= rows_total - 3).astype(jnp.int32)
    labels = zone_level * 3 + zone_row[None, :]
    same = labels[:, :, None] == labels[:, None, :]
    if shifted:
        return same
    return jnp.ones_like(same)

def window_group(block_in, bias, allowed, params):
    gains, w_qkv, w_proj, w_up, w_down = params
    levels, rows, cols, width = block_in.shape
    head_count = bias.shape[1]
    head_size = width // head_count
    inputs = block_in.astype(jnp.float32)
    hidden = pinned(layer_norm(inputs, gains[0]))
    qkv = pinned(jnp.einsum('zycd,de->zyce', hidden.astype(jnp.float32), w_qkv.astype(jnp.float32)))
    wins = qkv.reshape(levels // 2, 2, rows, cols // 12, 12, 3, head_count, head_size)
    wins = wins.transpose(0, 3, 5, 6, 1, 2, 4, 7).reshape(levels // 2, cols // 12, 3, head_count, 144, head_size)
    wins = wins.astype(jnp.float32)
    query = wins[:, :, 0]
    keys_all = wins[:, :, 1]
    values_all = wins[:, :, 2]
    score = jnp.einsum('zwhqd,zwhkd->zwhqk', query, keys_all) * head_size ** (-0.5) + bias[:, None]
    score = jnp.where(allowed[:, None, None], score, neg_fill)
    highest = lax.stop_gradient(lax.optimization_barrier(jnp.max(score, -1, keepdims=True)))
    expo = jnp.exp(score - highest)
    weights = pinned(expo / lax.optimization_barrier(jnp.sum(expo, -1, keepdims=True)))
    mixed = pinned(jnp.einsum('zwhqk,zwhkd->zwhqd', weights.astype(jnp.float32), values_all))
    mixed = mixed.reshape(levels // 2, cols // 12, head_count, 2, rows, 12, head_size)
    mixed = mixed.transpose(0, 3, 4, 1, 5, 2, 6).reshape(levels, rows, cols, width)
    resid = inputs + jnp.einsum('zyxc,cd->zyxd', mixed.astype(jnp.float32), w_proj.astype(jnp.float32))
    normed = pinned(layer_norm(resid, gains[1]))
    upward = jnp.einsum('zyxc,cf->zyxf', normed.astype(jnp.float32), w_up.astype(jnp.float32))
    active = pinned(jax.nn.gelu(upward, approximate=False))
    return pinned(resid + jnp.einsum('zyxf,fc->zyxc', active.astype(jnp.float32), w_down.astype(jnp.float32)))

def run_block(volume, shifted, params, table):
    levels, rows_total, cols_total, width = volume.shape
    bias_all = table[..., bias_index()]
    groups = volume.reshape(levels, rows_total // 6, 6, cols_total, width).transpose(1, 0, 2, 3, 4)
    group_ids = jnp.arange(rows_total // 6, dtype=jnp.int32)

    def step(items):
        allowed = region_valid(levels, rows_total, items[2], shifted)
        return window_group(items[0], items[1], allowed, params)
    outputs = lax.map(jax.checkpoint(step), (groups, bias_all, group_ids))
    return outputs.transpose(1, 0, 2, 3, 4).reshape(levels, rows_total, cols_total, width)

def processor(latent, norm_gains, qkv_weight, proj_weight, up_weight, down_weight, earth_bias):
    first = (norm_gains[0], qkv_weight[0], proj_weight[0], up_weight[0], down_weight[0])
    second = (norm_gains[1], qkv_weight[1], proj_weight[1], up_weight[1], down_weight[1])
    volume = run_block(latent, False, first, earth_bias[0])
    volume = jnp.roll(volume, (-1, -3, -6), (0, 1, 2))
    volume = run_block(volume, True, second, earth_bias[1])
    return jnp.roll(volume, (1, 3, 6), (0, 1, 2))

def reference(upper_fields, surface_fields, upper_embed, surface_embed, norm_gains, qkv_weight, proj_weight, up_weight, down_weight, earth_bias, out_grad):
    upper_patch, surface_patch = make_patches(upper_fields, surface_fields)
    upper_latent = jnp.einsum('zyxp,pc->zyxc', upper_patch.astype(jnp.float32), upper_embed.astype(jnp.float32))
    surface_latent = jnp.einsum('yxp,pc->yxc', surface_patch.astype(jnp.float32), surface_embed.astype(jnp.float32))
    latent = pinned(jnp.concatenate((surface_latent[None], upper_latent), 0))

    def forward(volume):
        return processor(volume, norm_gains, qkv_weight, proj_weight, up_weight, down_weight, earth_bias)
    _, pullback = jax.vjp(forward, latent)
    latent_grad = pullback(out_grad)[0]
    grad_float = lax.optimization_barrier(latent_grad).astype(jnp.float32)
    scale = float(np.prod(latent.shape[:3])) ** (-0.5)
    upper_grad = jnp.einsum('zyxp,zyxc->pc', upper_patch.astype(jnp.float32), grad_float[1:]) * scale
    surface_grad = jnp.einsum('yxp,yxc->pc', surface_patch.astype(jnp.float32), grad_float[0]) * scale
    return (latent_grad, upper_grad, surface_grad)
```

```python
import jax
import jax.numpy as jnp
import ml_dtypes
import numpy as np
from jax import lax
from jax.experimental import pallas as pl
from jax.experimental.pallas import tpu as pltpu
from jax.sharding import PartitionSpec as P

neg_fill = -1e30
norm_eps = 1e-05
HEADS = 6
HEAD = 32
CELLS = 144
WIDTH = 192
FULL = jnp.float32
HALF = jnp.bfloat16


def inner_row(z, a, o):
    return o * 12 + z * 6 + a


def octant_of(z, a, o):
    return (z * 4 + (a // 3) * 2 + o // 6, (a % 3) * 6 + o % 6)


def as_half(array):
    return array.astype(ml_dtypes.bfloat16)


def patch_select():
    sel = np.zeros((512, 512), np.float32)
    for c in range(4):
        for b in range(4):
            base = c * 128 + b * 32
            for z in range(2):
                for a in range(2):
                    for v in range(5):
                        sel[base + (z * 2 + a) * 5 + v, z * 256 + v * 32 + a * 16 + b * 4 + c] = 1
            for v in range(4):
                sel[base + 20 + v, 160 + v * 16 + b * 4 + c] = 1
    return as_half(sel)


def cells():
    return [(z, a, o) for z in range(2) for a in range(6) for o in range(12)]


def natural_to_inner():
    move = np.zeros((CELLS, CELLS), np.float32)
    for z, a, o in cells():
        move[inner_row(z, a, o), (z * 6 + a) * 12 + o] = 1
    return as_half(move)


def inner_to_padded():
    move = np.zeros((192, CELLS), np.float32)
    for z, a, o in cells():
        move[(z * 6 + a) * 16 + o, inner_row(z, a, o)] = 1
    return as_half(move)


def octants_out(pitch, first, padded_source):
    move = np.zeros((8 * pitch, 192 if padded_source else CELLS), np.float32)
    for z, a, o in cells():
        part, place = octant_of(z, a, o)
        source = (z * 6 + a) * 16 + o if padded_source else inner_row(z, a, o)
        move[part * pitch + first + place, source] = 1
    return as_half(move)


def octants_in(pitch, first):
    move = np.zeros((CELLS, 8 * pitch), np.float32)
    for z, a, o in cells():
        part, place = octant_of(z, a, o)
        move[inner_row(z, a, o), part * pitch + first + place] = 1
    return as_half(move)


def bias_columns():
    move = np.zeros((2, 256, 384), np.float32)
    for z in range(2):
        for a in range(6):
            for k in range(23):
                move[z, a * 23 + k, (22 - k) * 12 + z * 6 + a] = 1
    return as_half(move)


def dot(a, b):
    return jnp.dot(a, b, preferred_element_type=FULL)


def dot_nt(a, b):
    return lax.dot_general(a, b, (((1,), (1,)), ((), ())), preferred_element_type=FULL)


def dot_tn(a, b):
    return lax.dot_general(a, b, (((0,), (0,)), ((), ())), preferred_element_type=FULL)


def normalise(v):
    mean = jnp.mean(v, -1, keepdims=True)
    centred = v - mean
    spread = lax.rsqrt(jnp.mean(centred * centred, -1, keepdims=True) + norm_eps)
    return centred * spread, spread


def normalise_back(dy, unit, spread, gain):
    dunit = dy * gain
    inner = jnp.mean(dunit * unit, -1, keepdims=True)
    return spread * (dunit - jnp.mean(dunit, -1, keepdims=True) - unit * inner)


def head_lanes(h):
    lane = lax.broadcasted_iota(jnp.int32, (1, WIDTH), 1)
    return (lane >= h * HEAD) & (lane < (h + 1) * HEAD)


def head_mask(h):
    return jnp.where(head_lanes(h), 1.0, 0.0).astype(HALF)


def build_bias(tbl, block, cols, xs, bias, edges):
    for z in range(2):
        for a in range(6):
            for zu in range(2):
                start = ((z * 2 + zu) * 6 + a) * 138
                piece = tbl[block, :, start : start + 138]
                piece = jnp.concatenate((piece, jnp.zeros((HEADS, 118), FULL)), 1)
                for p in range(2):
                    for half in range(2):
                        xs[zu * 2 + half, pl.ds(p * 12 + z * 6 + a, HEADS, stride=24), :] = piece[
                            :, half * 128 : half * 128 + 128
                        ]
    total = None
    for zu in range(2):
        x = jnp.concatenate((xs[zu * 2], xs[zu * 2 + 1]), 1)
        high = x.astype(HALF)
        left = x - high.astype(FULL)
        mid = left.astype(HALF)
        low = (left - mid.astype(FULL)).astype(HALF)
        term = dot(jnp.concatenate((high, mid, low), 0), cols[zu])
        total = term if total is None else total + term
    table = total[:CELLS] + total[CELLS : 2 * CELLS] + total[2 * CELLS :]
    row = lax.broadcasted_iota(jnp.int32, (CELLS, 1), 0).astype(FULL)
    lane = lax.broadcasted_iota(jnp.int32, (1, CELLS), 1).astype(FULL)

    def part(v, size):
        return jnp.floor((v + 0.5) * (1.0 / size))

    even = part(row, 12) - 2.0 * part(part(row, 12), 2) == 0.0
    table = jnp.where(even, pltpu.roll(table, 384 - 12, 1), table)
    if edges is not None:
        last_section, last_band = edges
        row12, lane12 = row - 12.0 * part(row, 12), lane - 12.0 * part(lane, 12)
        row_z, lane_z = part(row12, 6), part(lane12, 6)
        row_a, lane_a = part(row12 - 6.0 * row_z, 3), part(lane12 - 6.0 * lane_z, 3)
        apart = jnp.abs(row_z - lane_z) * last_section + jnp.abs(row_a - lane_a) * last_band
        blocked = apart > 0.5
    for j in range(6):
        shift = (10 - 2 * j) * 12
        moved = pltpu.roll(table, 384 - shift, 1) if shift else table
        moved = moved[:, :CELLS]
        if edges is not None:
            moved = jnp.where(blocked, neg_fill, moved)
        for h in range(HEADS):
            bias[h * CELLS + j * 24 : h * CELLS + j * 24 + 24, :] = moved[h * 24 : h * 24 + 24, :]


def attend(q, k, v, bias, prob):
    mixed = jnp.zeros((CELLS, WIDTH), FULL)
    for h in range(HEADS):
        rows = slice(h * CELLS, (h + 1) * CELLS)
        score = dot_nt(q * head_mask(h), k) * HEAD ** (-0.5) + bias[rows, :]
        expo = jnp.exp(score - jnp.max(score, -1, keepdims=True))
        weights = (expo * (1.0 / jnp.sum(expo, -1, keepdims=True))).astype(HALF)
        prob[rows, :] = weights
        mixed = jnp.where(head_lanes(h), dot(weights, v), mixed)
    return mixed.astype(HALF)


def attend_back(dmixed, q, k, v, prob):
    dq = jnp.zeros((CELLS, WIDTH), FULL)
    dk = jnp.zeros((CELLS, WIDTH), FULL)
    dv = jnp.zeros((CELLS, WIDTH), FULL)
    for h in range(HEADS):
        rows = slice(h * CELLS, (h + 1) * CELLS)
        weights = prob[rows, :]
        dhead = dmixed * head_mask(h)
        full = weights.astype(FULL)
        dweights = dot_nt(dhead, v)
        inner = jnp.sum(dweights * full, -1, keepdims=True)
        dscore = (full * (dweights - inner) * HEAD ** (-0.5)).astype(HALF)
        dv = dv + dot_tn(weights, dhead)
        dq = jnp.where(head_lanes(h), dot(dscore, k), dq)
        dk = dk + dot_tn(dscore, q * head_mask(h))
    return dq.astype(HALF), dk.astype(HALF), dv.astype(HALF)


def gelu_parts(u):
    below = 0.5 * (1.0 + lax.erf(u * (0.5**0.5)))
    slope = below + u * (jnp.exp(-0.5 * u * u) * (2.0 * np.pi) ** (-0.5))
    return below, slope


def forward_half(x, block, gains, wqkv, wproj, bias, prob):
    unit, spread = normalise(x)
    hidden = (unit * gains[block, 0:1, :]).astype(HALF)
    qkv = dot(hidden, wqkv[block]).astype(HALF)
    q, k, v = (qkv[:, n * WIDTH : (n + 1) * WIDTH] for n in range(3))
    mixed = attend(q, k, v, bias, prob)
    return (q, k, v), x + dot(mixed, wproj[block])


def backward(dflat, block, x, qkv, prob, resid, slope, gains, wqkv, wproj, wup, wdown):
    q, k, v = qkv
    dactive = dot_nt(dflat, wdown[block])
    dupward = (dactive * slope).astype(HALF)
    dnormed = dot_nt(dupward, wup[block])
    unit, spread = normalise(resid)
    dresid = dflat.astype(FULL) + normalise_back(dnormed, unit, spread, gains[block, 1:2, :])
    dmixed = dot_nt(dresid.astype(HALF), wproj[block]).astype(HALF)
    dq, dk, dv = attend_back(dmixed, q, k, v, prob)
    weight = wqkv[block]
    dhidden = dot_nt(dq, weight[:, :WIDTH])
    dhidden = dhidden + dot_nt(dk, weight[:, WIDTH : 2 * WIDTH])
    dhidden = dhidden + dot_nt(dv, weight[:, 2 * WIDTH :])
    unit, spread = normalise(x)
    return dresid + normalise_back(dhidden, unit, spread, gains[block, 0:1, :])


def gather_patches(upper, surface, section, sections, select, ff, ft):
    base = 4 * section - 2
    for z in range(2):
        for a in range(2):
            level = jnp.maximum(base + 2 * z + a, 0)
            for v in range(5):
                field = upper[v, level].astype(FULL)
                if z == 0:
                    field = jnp.where(section == 0, 0.0, field)
                slot = (z * 2 + a) * 5 + v
                ff[slot * 24 : slot * 24 + 24, 0:48] = field
    for v in range(4):
        field = jnp.where(section == 0, surface[v].astype(FULL), 0.0)
        ff[(20 + v) * 24 : (21 + v) * 24, 0:48] = field
    pad = jnp.zeros((8, 128), FULL)
    for i in range(6):
        pieces = []
        for b in range(4):
            pieces += [ff[pl.ds(4 * i + b, 24, stride=24), :], pad]
        ft[i * 48 : i * 48 + 48, :] = jnp.concatenate(pieces, 0).T[:48]
    raw = [ft[pl.ds(c, 72, stride=4), :].astype(HALF) for c in range(4)]
    both = dot(jnp.concatenate(raw, 1), select[...])
    return jnp.concatenate((both[:, :256], both[:, 256:]), 0).astype(HALF)


def first_kernel(
    flags, upper, surface, cot, uembed, sembed, gains, wqkv, wproj, wup, wdown, tbl,
    select, to_inner, out_first, out_cot, cols, *rest
):
    octants, rest = rest[:8], rest[8:]
    patch_o, x_o, qkv_o, prob, resid_o, slope_o, ff, ft, emb, cots, xs, bias = rest
    section = flags[0]
    emb[0:160, :] = uembed[...]
    emb[160:224, :] = sembed[...]
    emb[224:256, :] = jnp.zeros((32, WIDTH), HALF)
    cots[...] = jnp.zeros_like(cots)
    for z in range(2):
        for a in range(6):
            cots[(z * 6 + a) * 16 : (z * 6 + a) * 16 + 12, :] = cot[z, a]
    build_bias(tbl, 0, cols, xs, bias, None)
    patch = gather_patches(upper, surface, section, None, select, ff, ft)
    patch = dot(to_inner[...], patch).astype(HALF)
    patch_o[...] = patch
    latent = dot(patch, emb[...]).astype(HALF)
    x_o[...] = latent
    x = latent.astype(FULL)
    qkv, resid = forward_half(x, 0, gains, wqkv, wproj, bias, prob)
    for n in range(3):
        qkv_o[n] = qkv[n]
    resid_o[...] = resid
    unit, spread = normalise(resid)
    normed = (unit * gains[0, 1:2, :]).astype(HALF)
    upward = dot(normed, wup[0])
    below, slope = gelu_parts(upward)
    slope_o[...] = slope.astype(HALF)
    active = (upward * below).astype(HALF)
    result = (resid + dot(active, wdown[0])).astype(HALF)
    moved = (dot(out_first[...], result) + dot(out_cot[...], cots[...])).astype(HALF)
    for n in range(8):
        octants[n][...] = moved[n * 48 : n * 48 + 48]


def second_kernel(flags, *rest):
    parts, rest = rest[:8], rest[8:]
    gains, wqkv, wproj, wup, wdown, tbl, cols, into, out_of = rest[:9]
    octants, rest = rest[9:17], rest[17:]
    stack, xs, bias, prob = rest
    build_bias(tbl, 1, cols, xs, bias, (flags[1].astype(FULL), flags[2].astype(FULL)))
    for n in range(8):
        stack[n * 48 : n * 48 + 48, :] = parts[n][...]
    both = dot(into[...], stack[...])
    x, dflat = both[:CELLS], both[CELLS:].astype(HALF)
    qkv, resid = forward_half(x, 1, gains, wqkv, wproj, bias, prob)
    unit, spread = normalise(resid)
    normed = (unit * gains[1, 1:2, :]).astype(HALF)
    upward = dot(normed, wup[1])
    slope = gelu_parts(upward)[1]
    dx = backward(dflat, 1, x, qkv, prob, resid, slope, gains, wqkv, wproj, wup, wdown)
    moved = dot(out_of[...], dx.astype(HALF)).astype(HALF)
    for n in range(8):
        octants[n][...] = moved[n * 32 : n * 32 + 32]


def third_kernel(*rest):
    parts, rest = rest[:8], rest[8:]
    gains, wqkv, wproj, wup, wdown, patch, x_i, qkv_i, prob, resid, slope, into, out_of = rest[:13]
    grad_o, terms_o, stack = rest[13:]
    for n in range(8):
        stack[n * 32 : n * 32 + 32, :] = parts[n][...]
    dflat = dot(into[...], stack[...]).astype(HALF)
    qkv = tuple(qkv_i[n] for n in range(3))
    dx = backward(
        dflat, 0, x_i[...].astype(FULL), qkv, prob, resid[...], slope[...].astype(FULL),
        gains, wqkv, wproj, wup, wdown,
    )
    grad = dx.astype(HALF)
    moved = dot(out_of[...], grad).astype(HALF)
    for z in range(2):
        for a in range(6):
            grad_o[z, a] = moved[(z * 6 + a) * 16 : (z * 6 + a) * 16 + 12]
    terms_o[...] = dot_tn(patch[...], grad)[:224].astype(HALF)


def call(kernel, outs, scratch, *args):
    vmem = pl.BlockSpec(memory_space=pltpu.VMEM)
    smem = pl.BlockSpec(memory_space=pltpu.SMEM)
    return pl.pallas_call(
        kernel,
        out_shape=outs,
        in_specs=[smem if a.dtype == jnp.int32 else vmem for a in args],
        out_specs=jax.tree.map(lambda _: vmem, outs),
        scratch_shapes=scratch,
        compiler_params=pltpu.CompilerParams(vmem_limit_bytes=30 * 2**20),
    )(*args)


def shape(dims, dtype=HALF):
    return jax.ShapeDtypeStruct(dims, dtype)


def move_octant(block, step):
    names, step = ("lon", "lat", "section"), step[::-1]
    if not any(step):
        return block
    sizes = [lax.axis_size(name) for name in names]
    pairs = []
    for place in np.ndindex(*sizes):
        source = [(p + s) % n for p, s, n in zip(place, step, sizes)]
        pairs.append((int(np.ravel_multi_index(source, sizes)), int(np.ravel_multi_index(place, sizes))))
    return lax.ppermute(block, names, pairs)


def add_up(terms):
    for name in ("section", "lat", "lon"):
        size = lax.axis_size(name)
        if size & (size - 1):
            terms = lax.psum(terms.astype(FULL), name).astype(HALF)
            continue
        step = 1
        while step < size:
            other = lax.ppermute(terms, name, [(i, i ^ step) for i in range(size)])
            terms = (terms.astype(FULL) + other.astype(FULL)).astype(HALF)
            step *= 2
    return terms.astype(FULL)


def on_device(
    upper_fields,
    surface_fields,
    upper_embed,
    surface_embed,
    norm_gains,
    qkv_weight,
    proj_weight,
    up_weight,
    down_weight,
    earth_bias,
    out_grad,
):
    section, band = lax.axis_index("section"), lax.axis_index("lat")
    sections, bands = lax.axis_size("section"), lax.axis_size("lat")
    levels, rows, columns, width = out_grad.shape
    flags = jnp.stack((section, section == sections - 1, band == bands - 1)).astype(jnp.int32)
    table = earth_bias.reshape(2, HEADS, earth_bias.shape[-1])
    weights = (norm_gains, qkv_weight, proj_weight, up_weight, down_weight)
    cols = jnp.asarray(bias_columns())
    scratch_bias = [pltpu.VMEM((4, CELLS, 128), FULL), pltpu.VMEM((HEADS * CELLS, CELLS), FULL)]
    results = call(
        first_kernel,
        [shape((48, WIDTH))] * 8
        + [
            shape((CELLS, 256)),
            shape((CELLS, WIDTH)),
            shape((3, CELLS, WIDTH)),
            shape((HEADS * CELLS, CELLS)),
            shape((CELLS, WIDTH), FULL),
            shape((CELLS, 4 * WIDTH)),
        ],
        [
            pltpu.VMEM((576, 128), FULL),
            pltpu.VMEM((288, 128), FULL),
            pltpu.VMEM((256, WIDTH), HALF),
            pltpu.VMEM((192, WIDTH), HALF),
        ]
        + scratch_bias,
        flags, upper_fields, surface_fields, out_grad, upper_embed, surface_embed, *weights, table,
        jnp.asarray(patch_select()), jnp.asarray(natural_to_inner()),
        jnp.asarray(octants_out(48, 0, False)), jnp.asarray(octants_out(48, 18, True)), cols,
    )
    octants, (patch, x, qkv, prob, resid, slope) = results[:8], results[8:]
    steps = list(np.ndindex(2, 2, 2))
    shifted = [move_octant(octants[7 - n], steps[n]) for n in range(8)]
    into = np.concatenate((octants_in(48, 0), octants_in(48, 18)), 0)
    back = call(
        second_kernel,
        [shape((32, WIDTH))] * 8,
        [pltpu.VMEM((8 * 48, WIDTH), HALF)]
        + scratch_bias
        + [pltpu.VMEM((HEADS * CELLS, CELLS), HALF)],
        flags, *shifted, *weights, table, cols,
        jnp.asarray(into), jnp.asarray(octants_out(32, 0, False)),
    )
    returned = [move_octant(back[n], tuple(-s for s in steps[n])) for n in range(8)][::-1]
    latent_grad, terms = call(
        third_kernel,
        [shape((2, 6, 12, WIDTH)), shape((224, WIDTH))],
        [pltpu.VMEM((8 * 32, WIDTH), HALF)],
        *returned, *weights, patch, x, qkv, prob, resid, slope,
        jnp.asarray(octants_in(32, 0)), jnp.asarray(inner_to_padded()),
    )
    total = add_up(terms)
    scale = float(levels * sections * rows * bands * columns * lax.axis_size("lon")) ** (-0.5)
    return (latent_grad, total[:160] * scale, total[160:] * scale)


def solution(mesh):
    placed = (
        P(None, None, "lat", "lon"),
        P(None, "lat", "lon"),
        P(),
        P(),
        P(),
        P(),
        P(),
        P(),
        P(),
        P(None, "lat", "section", None, None),
        P("section", "lat", "lon", None),
    )
    return jax.shard_map(
        on_device,
        mesh=mesh,
        in_specs=placed,
        out_specs=(P("section", "lat", "lon", None), P(), P()),
        check_vma=False,
    )
```

```python
import jax
import jax.numpy as jnp
import ml_dtypes
import numpy as np
from jax import lax
from jax.experimental import pallas as pl
from jax.experimental.pallas import tpu as pltpu
from jax.sharding import PartitionSpec as P

neg_fill = -1e30
norm_eps = 1e-05
HEADS = 6
HEAD = 32
CELLS = 144
WIDTH = 192
FULL = jnp.float32
HALF = jnp.bfloat16


def inner_row(z, a, o):
    return o * 12 + z * 6 + a


def octant_of(z, a, o):
    return (z * 4 + (a // 3) * 2 + o // 6, (a % 3) * 6 + o % 6)


def as_half(array):
    return array.astype(ml_dtypes.bfloat16)


def patch_select():
    sel = np.zeros((512, 512), np.float32)
    for c in range(4):
        for b in range(4):
            base = c * 128 + b * 32
            for z in range(2):
                for a in range(2):
                    for v in range(5):
                        sel[base + (z * 2 + a) * 5 + v, z * 256 + v * 32 + a * 16 + b * 4 + c] = 1
            for v in range(4):
                sel[base + 20 + v, 160 + v * 16 + b * 4 + c] = 1
    return as_half(sel)


def cells():
    return [(z, a, o) for z in range(2) for a in range(6) for o in range(12)]


def natural_to_inner():
    move = np.zeros((CELLS, CELLS), np.float32)
    for z, a, o in cells():
        move[inner_row(z, a, o), (z * 6 + a) * 12 + o] = 1
    return as_half(move)


def inner_to_padded():
    move = np.zeros((192, CELLS), np.float32)
    for z, a, o in cells():
        move[(z * 6 + a) * 16 + o, inner_row(z, a, o)] = 1
    return as_half(move)


def octants_out(pitch, first, flip, source):
    move = np.zeros((8 * pitch, CELLS), np.float32)
    for z, a, o in cells():
        part, place = octant_of(z, a, o)
        move[(7 - part if flip else part) * pitch + first + place, source(z, a, o)] = 1
    return as_half(move)


def octants_in(pitch, first, flip):
    move = np.zeros((CELLS, 8 * pitch), np.float32)
    for z, a, o in cells():
        part, place = octant_of(z, a, o)
        part = 7 - part if flip else part
        block = (part % 4) * 2 + part // 4
        move[inner_row(z, a, o), block * pitch + first + place] = 1
    return as_half(move)


def bias_columns():
    move = np.zeros((2, 256, 384), np.float32)
    for z in range(2):
        for a in range(6):
            for k in range(23):
                move[z, a * 23 + k, (22 - k) * 12 + z * 6 + a] = 1
    return as_half(move)


def dot(a, b):
    return jnp.dot(a, b, preferred_element_type=FULL)


def dot_nt(a, b):
    return lax.dot_general(a, b, (((1,), (1,)), ((), ())), preferred_element_type=FULL)


def dot_tn(a, b):
    return lax.dot_general(a, b, (((0,), (0,)), ((), ())), preferred_element_type=FULL)


def normalise(v):
    mean = jnp.mean(v, -1, keepdims=True)
    centred = v - mean
    spread = lax.rsqrt(jnp.mean(centred * centred, -1, keepdims=True) + norm_eps)
    return centred * spread, spread


def normalise_back(dy, unit, spread, gain):
    dunit = dy * gain
    inner = jnp.mean(dunit * unit, -1, keepdims=True)
    return spread * (dunit - jnp.mean(dunit, -1, keepdims=True) - unit * inner)


def head_lanes(h):
    lane = lax.broadcasted_iota(jnp.int32, (1, WIDTH), 1)
    return (lane >= h * HEAD) & (lane < (h + 1) * HEAD)


def head_mask(h):
    return jnp.where(head_lanes(h), 1.0, 0.0).astype(HALF)


def build_bias(tbl, cols, xs, bias, edges):
    for z in range(2):
        for a in range(6):
            for zu in range(2):
                start = ((z * 2 + zu) * 6 + a) * 138
                piece = tbl[0:HEADS, start : start + 138]
                piece = jnp.concatenate((piece, jnp.zeros((HEADS, 118), FULL)), 1)
                for p in range(2):
                    for half in range(2):
                        xs[zu * 2 + half, pl.ds(p * 12 + z * 6 + a, HEADS, stride=24), :] = piece[
                            :, half * 128 : half * 128 + 128
                        ]
    total = None
    for zu in range(2):
        x = jnp.concatenate((xs[zu * 2], xs[zu * 2 + 1]), 1)
        high = x.astype(HALF)
        left = x - high.astype(FULL)
        mid = left.astype(HALF)
        low = (left - mid.astype(FULL)).astype(HALF)
        term = dot(jnp.concatenate((high, mid, low), 0), cols[zu])
        total = term if total is None else total + term
    table = total[:CELLS] + total[CELLS : 2 * CELLS] + total[2 * CELLS :]
    row = lax.broadcasted_iota(jnp.int32, (CELLS, 1), 0).astype(FULL)
    lane = lax.broadcasted_iota(jnp.int32, (1, CELLS), 1).astype(FULL)

    def part(v, size):
        return jnp.floor((v + 0.5) * (1.0 / size))

    even = part(row, 12) - 2.0 * part(part(row, 12), 2) == 0.0
    table = jnp.where(even, pltpu.roll(table, 384 - 12, 1), table)
    if edges is not None:
        last_section, last_band = edges
        row12, lane12 = row - 12.0 * part(row, 12), lane - 12.0 * part(lane, 12)
        row_z, lane_z = part(row12, 6), part(lane12, 6)
        row_a, lane_a = part(row12 - 6.0 * row_z, 3), part(lane12 - 6.0 * lane_z, 3)
        apart = jnp.abs(row_z - lane_z) * last_section + jnp.abs(row_a - lane_a) * last_band
        blocked = apart > 0.5
    for j in range(6):
        shift = (10 - 2 * j) * 12
        moved = pltpu.roll(table, 384 - shift, 1) if shift else table
        moved = moved[:, :CELLS]
        if edges is not None:
            moved = jnp.where(blocked, neg_fill, moved)
        for h in range(HEADS):
            bias[h * CELLS + j * 24 : h * CELLS + j * 24 + 24, :] = moved[h * 24 : h * 24 + 24, :]


def attend(q, k, v, bias, prob):
    mixed = jnp.zeros((CELLS, WIDTH), FULL)
    for h in range(HEADS):
        rows = slice(h * CELLS, (h + 1) * CELLS)
        score = dot_nt(q * head_mask(h), k) * HEAD ** (-0.5) + bias[rows, :]
        expo = jnp.exp(score - jnp.max(score, -1, keepdims=True))
        weights = (expo * (1.0 / jnp.sum(expo, -1, keepdims=True))).astype(HALF)
        prob[rows, :] = weights
        mixed = jnp.where(head_lanes(h), dot(weights, v), mixed)
    return mixed.astype(HALF)


def attend_back(dmixed, q, k, v, prob):
    dq = jnp.zeros((CELLS, WIDTH), FULL)
    dk = jnp.zeros((CELLS, WIDTH), FULL)
    dv = jnp.zeros((CELLS, WIDTH), FULL)
    for h in range(HEADS):
        rows = slice(h * CELLS, (h + 1) * CELLS)
        weights = prob[rows, :]
        dhead = dmixed * head_mask(h)
        full = weights.astype(FULL)
        dweights = dot_nt(dhead, v)
        inner = jnp.sum(dweights * full, -1, keepdims=True)
        dscore = (full * (dweights - inner) * HEAD ** (-0.5)).astype(HALF)
        dv = dv + dot_tn(weights, dhead)
        dq = jnp.where(head_lanes(h), dot(dscore, k), dq)
        dk = dk + dot_tn(dscore, q * head_mask(h))
    return dq.astype(HALF), dk.astype(HALF), dv.astype(HALF)


def gelu_parts(u):
    below = 0.5 * (1.0 + lax.erf(u * (0.5**0.5)))
    slope = below + u * (jnp.exp(-0.5 * u * u) * (2.0 * np.pi) ** (-0.5))
    return below, slope


def forward_half(x, gains, wqkv, wproj, bias, prob):
    unit, spread = normalise(x)
    hidden = (unit * gains[0:1, :]).astype(HALF)
    qkv = dot(hidden, wqkv[...]).astype(HALF)
    q, k, v = (qkv[:, n * WIDTH : (n + 1) * WIDTH] for n in range(3))
    mixed = attend(q, k, v, bias, prob)
    return (q, k, v), x + dot(mixed, wproj[...])


def backward(dflat, x, qkv, prob, resid, slope, gains, wqkv, wproj, wup, wdown):
    q, k, v = qkv
    dactive = dot(dflat, wdown[...])
    dupward = (dactive * slope).astype(HALF)
    dnormed = dot_nt(dupward, wup[...])
    unit, spread = normalise(resid)
    dresid = dflat.astype(FULL) + normalise_back(dnormed, unit, spread, gains[1:2, :])
    dmixed = dot_nt(dresid.astype(HALF), wproj[...]).astype(HALF)
    dq, dk, dv = attend_back(dmixed, q, k, v, prob)
    dhidden = dot_nt(dq, wqkv[:, :WIDTH])
    dhidden = dhidden + dot_nt(dk, wqkv[:, WIDTH : 2 * WIDTH])
    dhidden = dhidden + dot_nt(dv, wqkv[:, 2 * WIDTH :])
    unit, spread = normalise(x)
    return dresid + normalise_back(dhidden, unit, spread, gains[0:1, :])


def gather_patches(upper, surface, section, select, ff, ft):
    base = 4 * section - 2
    for z in range(2):
        for a in range(2):
            level = jnp.maximum(base + 2 * z + a, 0)
            for v in range(5):
                field = upper[v, level].astype(FULL)
                if z == 0:
                    field = jnp.where(section == 0, 0.0, field)
                slot = (z * 2 + a) * 5 + v
                ff[slot * 24 : slot * 24 + 24, 0:48] = field
    for v in range(4):
        field = jnp.where(section == 0, surface[v].astype(FULL), 0.0)
        ff[(20 + v) * 24 : (21 + v) * 24, 0:48] = field
    pad = jnp.zeros((8, 128), FULL)
    for i in range(6):
        pieces = []
        for b in range(4):
            pieces += [ff[pl.ds(4 * i + b, 24, stride=24), :], pad]
        ft[i * 48 : i * 48 + 48, :] = jnp.concatenate(pieces, 0).T[:48]
    raw = [ft[pl.ds(c, 72, stride=4), :].astype(HALF) for c in range(4)]
    both = dot(jnp.concatenate(raw, 1), select[...])
    return jnp.concatenate((both[:, :256], both[:, 256:]), 0).astype(HALF)


def flag(axis):
    last = lax.axis_index(axis) == lax.axis_size(axis) - 1
    return jnp.where(last, 1.0, 0.0)


def table_rows(tbl, block, table):
    for h in range(HEADS):
        table[h : h + 1, 0 : tbl.shape[-1]] = tbl[block * HEADS + h]


def first_kernel(*refs):
    names = (
        "tbl", "cols", "upper", "surface", "select", "to_inner", "uembed", "sembed", "gains",
        "wqkv", "wproj", "wup", "wdown", "cot", "out_first", "out_cot",
    )
    count = len(names)
    source, rest = refs[:count], refs[count:]
    keep_o, send_o, patch_o, x_o, qkv_o, prob, resid_o, slope_o = rest[:8]
    local, rest = rest[8 : 8 + count], rest[8 + count :]
    ff, ft, emb, cots, table, xs, bias, sems = rest
    copies = {}
    for n, name in enumerate(names):
        start = source[n].at[0] if name[0] == "w" else source[n]
        if name == "uembed":
            target = emb.at[pl.ds(0, 160)]
        elif name == "sembed":
            target = emb.at[pl.ds(160, 64)]
        else:
            target = local[n]
        copies[name] = pltpu.make_async_copy(start, target, sems.at[n])
        copies[name].start()
    have = dict(zip(names, local))

    def wait(*which):
        for name in which:
            copies[name].wait()

    emb[224:256, :] = jnp.zeros((32, WIDTH), HALF)
    wait("tbl", "cols")
    table_rows(have["tbl"], 0, table)
    build_bias(table, have["cols"], xs, bias, None)
    wait("upper", "surface", "select", "to_inner", "uembed", "sembed", "gains", "wqkv")
    section = lax.axis_index("section")
    patch = gather_patches(have["upper"], have["surface"], section, have["select"], ff, ft)
    patch = dot(have["to_inner"][...], patch).astype(HALF)
    patch_o[...] = patch
    latent = dot(patch, emb[...]).astype(HALF)
    x_o[...] = latent
    x = latent.astype(FULL)
    gains = have["gains"].at[0]
    wait("wproj", "wup", "wdown", "cot", "out_first", "out_cot")
    cot = have["cot"]
    for a in range(6):
        for o in range(12):
            cots[(a * 12 + o) * 2 : (a * 12 + o) * 2 + 2, :] = cot[a, o].astype(FULL)
    qkv, resid = forward_half(x, gains, have["wqkv"], have["wproj"], bias, prob)
    for n in range(3):
        qkv_o[n] = qkv[n]
    resid_o[...] = resid
    unit, spread = normalise(resid)
    normed = (unit * gains[1:2, :]).astype(HALF)
    upward = dot(normed, have["wup"][...])
    below, slope = gelu_parts(upward)
    slope_o[...] = slope.astype(HALF)
    active = (upward * below).astype(HALF)
    result = (resid + dot_nt(active, have["wdown"][...])).astype(HALF)
    moved = dot(have["out_first"][...], result)
    moved = (moved + dot(have["out_cot"][...], cots[...].astype(HALF))).astype(HALF)
    keep_o[...] = moved[:192]
    send_o[...] = moved[192:]


def bias_kernel(tbl, cols, bias, table, xs):
    table_rows(tbl, 1, table)
    build_bias(table, cols, xs, bias, (flag("section"), flag("lat")))


def second_kernel(*refs):
    parts, rest = refs[:4], refs[4:]
    gains, wqkv, wproj, wup, wdown, bias, into, out_of, keep_o, send_o, stack, prob = rest
    for n in range(4):
        stack[n * 96 : n * 96 + 96, :] = parts[n][...]
    both = dot(into[...], stack[...])
    x, dflat = both[:CELLS], both[CELLS:].astype(HALF)
    gains, wqkv, wproj, wup, wdown = (w.at[1] for w in (gains, wqkv, wproj, wup, wdown))
    qkv, resid = forward_half(x, gains, wqkv, wproj, bias, prob)
    unit, spread = normalise(resid)
    normed = (unit * gains[1:2, :]).astype(HALF)
    upward = dot(normed, wup[...])
    slope = gelu_parts(upward)[1]
    dx = backward(dflat, x, qkv, prob, resid, slope, gains, wqkv, wproj, wup, wdown)
    moved = dot(out_of[...], dx.astype(HALF)).astype(HALF)
    keep_o[...] = moved[:128]
    send_o[...] = moved[128:]


def third_kernel(*refs):
    parts, rest = refs[:4], refs[4:]
    gains, wqkv, wproj, wup, wdown, patch, x_i, qkv_i, prob, resid, slope, into, out_of = rest[:13]
    grad_o, mine_o, other_o, stack, terms = rest[13:]
    for n in range(4):
        stack[n * 64 : n * 64 + 64, :] = parts[n][...]
    dflat = dot(into[...], stack[...]).astype(HALF)
    qkv = tuple(qkv_i[n] for n in range(3))
    gains, wqkv, wproj, wup, wdown = (w.at[0] for w in (gains, wqkv, wproj, wup, wdown))
    dx = backward(
        dflat, x_i[...].astype(FULL), qkv, prob, resid[...], slope[...].astype(FULL),
        gains, wqkv, wproj, wup, wdown,
    )
    grad = dx.astype(HALF)
    moved = dot(out_of[...], grad).astype(HALF)
    for z in range(2):
        for a in range(6):
            grad_o[z, a] = moved[(z * 6 + a) * 16 : (z * 6 + a) * 16 + 12]
    terms[...] = dot_tn(patch[...], grad)
    place = lax.axis_index("section") % 2
    mine_o[...] = terms[pl.ds(pl.multiple_of(place * 112, 16), 112), :].astype(HALF)
    other_o[...] = terms[pl.ds(pl.multiple_of(112 - place * 112, 16), 112), :].astype(HALF)


vmem = pl.BlockSpec(memory_space=pltpu.VMEM)
where_it_lies = pl.BlockSpec(memory_space=pl.ANY)


def call(kernel, outs, scratch, *args, spec=vmem, flops=1000000):
    return pl.pallas_call(
        kernel,
        out_shape=outs,
        in_specs=[spec for a in args],
        out_specs=jax.tree.map(lambda _: vmem, outs),
        scratch_shapes=scratch,
        compiler_params=pltpu.CompilerParams(vmem_limit_bytes=30 * 2**20),
        cost_estimate=pl.CostEstimate(flops=flops, bytes_accessed=1000000, transcendentals=0),
    )(*args)


def shape(dims, dtype=HALF):
    return jax.ShapeDtypeStruct(dims, dtype)


def fetch(block, steps):
    names = ("lon", "lat", "section")
    axes = [name for name in names if steps.get(name, 0)]
    if not axes:
        return block
    sizes = [lax.axis_size(name) for name in axes]
    pairs = []
    for place in np.ndindex(*sizes):
        source = [(p + steps[name]) % n for p, name, n in zip(place, axes, sizes)]
        pairs.append(
            (int(np.ravel_multi_index(source, sizes)), int(np.ravel_multi_index(place, sizes)))
        )
    return lax.ppermute(block, tuple(axes), pairs)


def exchange(keep, send, way):
    pitch = keep.shape[0] // 4
    got = fetch(send, {"section": way})
    blocks = []
    for n in range(4):
        rows = slice(n * pitch, (n + 1) * pitch)
        block = jnp.concatenate((keep[rows], got[rows]), 0)
        blocks.append(fetch(block, {"lat": way * (n // 2), "lon": way * (n % 2)}))
    return blocks


def add_up(mine, other):
    sections = lax.axis_size("section")
    place = lax.axis_index("section") % 2
    if sections % 2:
        raise ValueError("odd sections")
    swap = [(i, i ^ 1) for i in range(sections)]

    def both(a, b):
        return (a.astype(FULL) + b.astype(FULL)).astype(HALF)

    total = both(mine, lax.ppermute(other, "section", swap))
    for name in ("section", "lat", "lon"):
        size = lax.axis_size(name)
        if size & (size - 1):
            raise ValueError("axis size")
        step = 2 if name == "section" else 1
        while step < size:
            pairs = [(i, i ^ step) for i in range(size)]
            total = both(total, lax.ppermute(total, name, pairs))
            step *= 2
    far = lax.ppermute(total, "section", swap)
    first = jnp.where(place == 0, total, far)
    second = jnp.where(place == 0, far, total)
    return jnp.concatenate((first, second), 0).astype(FULL)


def on_device(
    upper_fields,
    surface_fields,
    upper_embed,
    surface_embed,
    norm_gains,
    qkv_weight,
    proj_weight,
    up_weight,
    down_weight,
    earth_bias,
    out_grad,
):
    sections, bands = lax.axis_size("section"), lax.axis_size("lat")
    levels, rows, columns, width = out_grad.shape
    positions = earth_bias.shape[-1]
    table = earth_bias.transpose(0, 1, 3, 2, 4).reshape(2 * HEADS, 1, positions)
    weights = (norm_gains, qkv_weight, proj_weight, up_weight, down_weight.transpose(0, 2, 1))
    cols = jnp.asarray(bias_columns())

    def from_cot(z, a, o):
        return (a * 12 + o) * 2 + z

    operands = (
        table, cols, upper_fields, surface_fields, jnp.asarray(patch_select()),
        jnp.asarray(natural_to_inner()), upper_embed, surface_embed, *weights,
        out_grad.transpose(1, 2, 0, 3),
        jnp.asarray(octants_out(48, 0, True, inner_row)),
        jnp.asarray(octants_out(48, 18, True, from_cot)),
    )
    local = [
        pltpu.VMEM(v.shape[1:] if 9 <= n < 13 else v.shape, v.dtype) for n, v in enumerate(operands)
    ]
    local[6] = local[7] = pltpu.VMEM((16, 128), HALF)
    scratch_bias = [pltpu.VMEM((8, 3328), FULL), pltpu.VMEM((4, CELLS, 128), FULL)]
    keep, send, patch, x, qkv, prob, resid, slope = call(
        first_kernel,
        [
            shape((192, WIDTH)),
            shape((192, WIDTH)),
            shape((CELLS, 256)),
            shape((CELLS, WIDTH)),
            shape((3, CELLS, WIDTH)),
            shape((HEADS * CELLS, CELLS)),
            shape((CELLS, WIDTH), FULL),
            shape((CELLS, 4 * WIDTH)),
        ],
        local
        + [
            pltpu.VMEM((576, 128), FULL),
            pltpu.VMEM((288, 128), FULL),
            pltpu.VMEM((256, WIDTH), HALF),
            pltpu.VMEM((CELLS, WIDTH), FULL),
        ]
        + scratch_bias
        + [
            pltpu.VMEM((HEADS * CELLS, CELLS), FULL),
            pltpu.SemaphoreType.DMA((len(operands),)),
        ],
        *operands,
        spec=where_it_lies,
    )
    bias = call(bias_kernel, shape((HEADS * CELLS, CELLS), FULL), scratch_bias, table, cols)
    into = np.concatenate((octants_in(48, 0, False), octants_in(48, 18, False)), 0)
    keep, send = call(
        second_kernel,
        [shape((128, WIDTH))] * 2,
        [pltpu.VMEM((8 * 48, WIDTH), HALF), pltpu.VMEM((HEADS * CELLS, CELLS), HALF)],
        *exchange(keep, send, 1), *weights, bias,
        jnp.asarray(into), jnp.asarray(octants_out(32, 0, False, inner_row)),
    )
    latent_grad, mine, other = call(
        third_kernel,
        [shape((2, 6, 12, WIDTH)), shape((112, WIDTH)), shape((112, WIDTH))],
        [pltpu.VMEM((8 * 32, WIDTH), HALF), pltpu.VMEM((256, WIDTH), FULL)],
        *exchange(keep, send, -1), *weights, patch, x, qkv, prob, resid, slope,
        jnp.asarray(octants_in(32, 0, True)), jnp.asarray(inner_to_padded()),
    )
    total = add_up(mine, other)
    scale = float(levels * sections * rows * bands * columns * lax.axis_size("lon")) ** (-0.5)
    return (latent_grad, total[:160] * scale, total[160:] * scale)


def solution(mesh):
    placed = (
        P(None, None, "lat", "lon"),
        P(None, "lat", "lon"),
        P(),
        P(),
        P(),
        P(),
        P(),
        P(),
        P(),
        P(None, "lat", "section", None, None),
        P("section", "lat", "lon", None),
    )
    return jax.shard_map(
        on_device,
        mesh=mesh,
        in_specs=placed,
        out_specs=(P("section", "lat", "lon", None), P(), P()),
        check_vma=False,
    )
```

```python
import functools

import jax
import jax.numpy as jnp
import ml_dtypes
import numpy as np
from jax import lax
from jax.experimental import pallas as pl
from jax.experimental.pallas import tpu as pltpu
from jax.sharding import PartitionSpec as P

neg_fill = -1e30
norm_eps = 1e-05
HEADS = 6
HEAD = 32
CELLS = 144
WIDTH = 192
FULL = jnp.float32
HALF = jnp.bfloat16


def inner_row(z, a, o):
    return o * 12 + z * 6 + a


def octant_of(z, a, o):
    return (z * 4 + (a // 3) * 2 + o // 6, (a % 3) * 6 + o % 6)


def as_half(array):
    return array.astype(ml_dtypes.bfloat16)


def patch_select():
    sel = np.zeros((512, 512), np.float32)
    for c in range(4):
        for b in range(4):
            base = c * 128 + b * 32
            for z in range(2):
                for a in range(2):
                    for v in range(5):
                        sel[base + (z * 2 + a) * 5 + v, z * 256 + v * 32 + a * 16 + b * 4 + c] = 1
            for v in range(4):
                sel[base + 20 + v, 160 + v * 16 + b * 4 + c] = 1
    return as_half(sel)


def cells():
    return [(z, a, o) for z in range(2) for a in range(6) for o in range(12)]


def natural_to_inner():
    move = np.zeros((CELLS, CELLS), np.float32)
    for z, a, o in cells():
        move[inner_row(z, a, o), (z * 6 + a) * 12 + o] = 1
    return as_half(move)


def inner_to_padded():
    move = np.zeros((192, CELLS), np.float32)
    for z, a, o in cells():
        move[(z * 6 + a) * 16 + o, inner_row(z, a, o)] = 1
    return as_half(move)


def octants_out(pitch, first, flip, source):
    move = np.zeros((8 * pitch, CELLS), np.float32)
    for z, a, o in cells():
        part, place = octant_of(z, a, o)
        move[(7 - part if flip else part) * pitch + first + place, source(z, a, o)] = 1
    return as_half(move)


def octants_in(pitch, first, flip):
    move = np.zeros((CELLS, 8 * pitch), np.float32)
    for z, a, o in cells():
        part, place = octant_of(z, a, o)
        part = 7 - part if flip else part
        block = (part % 4) * 2 + part // 4
        move[inner_row(z, a, o), block * pitch + first + place] = 1
    return as_half(move)


def bias_columns():
    move = np.zeros((2, 256, 384), np.float32)
    for z in range(2):
        for a in range(6):
            for k in range(23):
                move[z, a * 23 + k, (22 - k) * 12 + z * 6 + a] = 1
    return as_half(move)


def dot(a, b):
    return jnp.dot(a, b, preferred_element_type=FULL)


def dot_nt(a, b):
    return lax.dot_general(a, b, (((1,), (1,)), ((), ())), preferred_element_type=FULL)


def dot_tn(a, b):
    return lax.dot_general(a, b, (((0,), (0,)), ((), ())), preferred_element_type=FULL)


def normalise(v):
    mean = jnp.mean(v, -1, keepdims=True)
    centred = v - mean
    spread = lax.rsqrt(jnp.mean(centred * centred, -1, keepdims=True) + norm_eps)
    return centred * spread, spread


def normalise_back(dy, unit, spread, gain):
    dunit = dy * gain
    inner = jnp.mean(dunit * unit, -1, keepdims=True)
    return spread * (dunit - jnp.mean(dunit, -1, keepdims=True) - unit * inner)


def head_lanes(h):
    lane = lax.broadcasted_iota(jnp.int32, (1, WIDTH), 1)
    return (lane >= h * HEAD) & (lane < (h + 1) * HEAD)


def head_mask(h):
    return jnp.where(head_lanes(h), 1.0, 0.0).astype(HALF)


def build_bias(tbl, cols, xs, bias, edges):
    for z in range(2):
        for a in range(6):
            for zu in range(2):
                start = ((z * 2 + zu) * 6 + a) * 138
                piece = tbl[0:HEADS, start : start + 138]
                piece = jnp.concatenate((piece, jnp.zeros((HEADS, 118), FULL)), 1)
                for p in range(2):
                    for half in range(2):
                        xs[zu * 2 + half, pl.ds(p * 12 + z * 6 + a, HEADS, stride=24), :] = piece[
                            :, half * 128 : half * 128 + 128
                        ]
    total = None
    for zu in range(2):
        x = jnp.concatenate((xs[zu * 2], xs[zu * 2 + 1]), 1)
        high = x.astype(HALF)
        left = x - high.astype(FULL)
        mid = left.astype(HALF)
        low = (left - mid.astype(FULL)).astype(HALF)
        term = dot(jnp.concatenate((high, mid, low), 0), cols[zu])
        total = term if total is None else total + term
    table = total[:CELLS] + total[CELLS : 2 * CELLS] + total[2 * CELLS :]
    row = lax.broadcasted_iota(jnp.int32, (CELLS, 1), 0).astype(FULL)
    lane = lax.broadcasted_iota(jnp.int32, (1, CELLS), 1).astype(FULL)

    def part(v, size):
        return jnp.floor((v + 0.5) * (1.0 / size))

    even = part(row, 12) - 2.0 * part(part(row, 12), 2) == 0.0
    table = jnp.where(even, pltpu.roll(table, 384 - 12, 1), table)
    if edges is not None:
        last_section, last_band = edges
        row12, lane12 = row - 12.0 * part(row, 12), lane - 12.0 * part(lane, 12)
        row_z, lane_z = part(row12, 6), part(lane12, 6)
        row_a, lane_a = part(row12 - 6.0 * row_z, 3), part(lane12 - 6.0 * lane_z, 3)
        apart = jnp.abs(row_z - lane_z) * last_section + jnp.abs(row_a - lane_a) * last_band
        blocked = apart > 0.5
    for j in range(6):
        shift = (10 - 2 * j) * 12
        moved = pltpu.roll(table, 384 - shift, 1) if shift else table
        moved = moved[:, :CELLS]
        if edges is not None:
            moved = jnp.where(blocked, neg_fill, moved)
        for h in range(HEADS):
            bias[h * CELLS + j * 24 : h * CELLS + j * 24 + 24, :] = moved[h * 24 : h * 24 + 24, :]


def attend(q, k, v, bias, prob):
    mixed = jnp.zeros((CELLS, WIDTH), FULL)
    for h in range(HEADS):
        rows = slice(h * CELLS, (h + 1) * CELLS)
        score = dot_nt(q * head_mask(h), k) * HEAD ** (-0.5) + bias[rows, :]
        expo = jnp.exp(score - jnp.max(score, -1, keepdims=True))
        weights = (expo * (1.0 / jnp.sum(expo, -1, keepdims=True))).astype(HALF)
        prob[rows, :] = weights
        mixed = jnp.where(head_lanes(h), dot(weights, v), mixed)
    return mixed.astype(HALF)


def attend_back(dmixed, q, k, v, prob):
    dq = jnp.zeros((CELLS, WIDTH), FULL)
    dk = jnp.zeros((CELLS, WIDTH), FULL)
    dv = jnp.zeros((CELLS, WIDTH), FULL)
    for h in range(HEADS):
        rows = slice(h * CELLS, (h + 1) * CELLS)
        weights = prob[rows, :]
        dhead = dmixed * head_mask(h)
        full = weights.astype(FULL)
        dweights = dot_nt(dhead, v)
        inner = jnp.sum(dweights * full, -1, keepdims=True)
        dscore = (full * (dweights - inner) * HEAD ** (-0.5)).astype(HALF)
        dv = dv + dot_tn(weights, dhead)
        dq = jnp.where(head_lanes(h), dot(dscore, k), dq)
        dk = dk + dot_tn(dscore, q * head_mask(h))
    return dq.astype(HALF), dk.astype(HALF), dv.astype(HALF)


def gelu_parts(u):
    below = 0.5 * (1.0 + lax.erf(u * (0.5**0.5)))
    slope = below + u * (jnp.exp(-0.5 * u * u) * (2.0 * np.pi) ** (-0.5))
    return below, slope


def forward_half(x, gains, wqkv, wproj, bias, prob):
    unit, spread = normalise(x)
    hidden = (unit * gains[0:1, :]).astype(HALF)
    qkv = dot(hidden, wqkv[...]).astype(HALF)
    q, k, v = (qkv[:, n * WIDTH : (n + 1) * WIDTH] for n in range(3))
    mixed = attend(q, k, v, bias, prob)
    return (q, k, v), x + dot(mixed, wproj[...])


def backward(dflat, x, qkv, prob, resid, slope, gains, wqkv, wproj, wup, wdown):
    q, k, v = qkv
    dactive = dot(dflat, wdown[...])
    dupward = (dactive * slope).astype(HALF)
    dnormed = dot_nt(dupward, wup[...])
    unit, spread = normalise(resid)
    dresid = dflat.astype(FULL) + normalise_back(dnormed, unit, spread, gains[1:2, :])
    dmixed = dot_nt(dresid.astype(HALF), wproj[...]).astype(HALF)
    dq, dk, dv = attend_back(dmixed, q, k, v, prob)
    dhidden = dot_nt(dq, wqkv[:, :WIDTH])
    dhidden = dhidden + dot_nt(dk, wqkv[:, WIDTH : 2 * WIDTH])
    dhidden = dhidden + dot_nt(dv, wqkv[:, 2 * WIDTH :])
    unit, spread = normalise(x)
    return dresid + normalise_back(dhidden, unit, spread, gains[0:1, :])


def gather_patches(upper, surface, section, select, ff, ft):
    base = 4 * section - 2
    for z in range(2):
        for a in range(2):
            level = jnp.maximum(base + 2 * z + a, 0)
            for v in range(5):
                field = upper[v, level].astype(FULL)
                if z == 0:
                    field = jnp.where(section == 0, 0.0, field)
                slot = (z * 2 + a) * 5 + v
                ff[slot * 24 : slot * 24 + 24, 0:48] = field
    for v in range(4):
        field = jnp.where(section == 0, surface[v].astype(FULL), 0.0)
        ff[(20 + v) * 24 : (21 + v) * 24, 0:48] = field
    pad = jnp.zeros((8, 128), FULL)
    for i in range(6):
        pieces = []
        for b in range(4):
            pieces += [ff[pl.ds(4 * i + b, 24, stride=24), :], pad]
        ft[i * 48 : i * 48 + 48, :] = jnp.concatenate(pieces, 0).T[:48]
    raw = [ft[pl.ds(c, 72, stride=4), :].astype(HALF) for c in range(4)]
    both = dot(jnp.concatenate(raw, 1), select[...])
    return jnp.concatenate((both[:, :256], both[:, 256:]), 0).astype(HALF)


def flag(axis):
    last = lax.axis_index(axis) == lax.axis_size(axis) - 1
    return jnp.where(last, 1.0, 0.0)


def table_rows(tbl, block, table):
    for h in range(HEADS):
        table[h : h + 1, 0 : tbl.shape[-1]] = tbl[block * HEADS + h]


def first_kernel(*refs):
    names = (
        "tbl", "cols", "upper", "surface", "select", "to_inner", "uembed", "sembed", "gains",
        "wqkv", "wproj", "wup", "wdown", "cot", "out_first", "out_cot",
    )
    count = len(names)
    source, rest = refs[:count], refs[count:]
    keep_o, send_o, patch_o, x_o, qkv_o, prob, resid_o, slope_o = rest[:8]
    local, rest = rest[8 : 8 + count], rest[8 + count :]
    ff, ft, emb, cots, table, xs, bias, sems = rest
    copies = {}
    for n, name in enumerate(names):
        start = source[n].at[0] if name[0] == "w" else source[n]
        if name == "uembed":
            target = emb.at[pl.ds(0, 160)]
        elif name == "sembed":
            target = emb.at[pl.ds(160, 64)]
        else:
            target = local[n]
        copies[name] = pltpu.make_async_copy(start, target, sems.at[n])
        copies[name].start()
    have = dict(zip(names, local))

    def wait(*which):
        for name in which:
            copies[name].wait()

    emb[224:256, :] = jnp.zeros((32, WIDTH), HALF)
    wait("tbl", "cols")
    table_rows(have["tbl"], 0, table)
    build_bias(table, have["cols"], xs, bias, None)
    wait("upper", "surface", "select", "to_inner", "uembed", "sembed", "gains", "wqkv")
    section = lax.axis_index("section")
    patch = gather_patches(have["upper"], have["surface"], section, have["select"], ff, ft)
    patch = dot(have["to_inner"][...], patch).astype(HALF)
    patch_o[...] = patch
    latent = dot(patch, emb[...]).astype(HALF)
    x_o[...] = latent
    x = latent.astype(FULL)
    gains = have["gains"].at[0]
    wait("wproj", "wup", "wdown", "cot", "out_first", "out_cot")
    cot = have["cot"]
    for a in range(6):
        for o in range(12):
            cots[(a * 12 + o) * 2 : (a * 12 + o) * 2 + 2, :] = cot[a, o].astype(FULL)
    qkv, resid = forward_half(x, gains, have["wqkv"], have["wproj"], bias, prob)
    for n in range(3):
        qkv_o[n] = qkv[n]
    resid_o[...] = resid
    unit, spread = normalise(resid)
    normed = (unit * gains[1:2, :]).astype(HALF)
    upward = dot(normed, have["wup"][...])
    below, slope = gelu_parts(upward)
    slope_o[...] = slope.astype(HALF)
    active = (upward * below).astype(HALF)
    result = (resid + dot_nt(active, have["wdown"][...])).astype(HALF)
    moved = dot(have["out_first"][...], result)
    moved = (moved + dot(have["out_cot"][...], cots[...].astype(HALF))).astype(HALF)
    keep_o[...] = moved[:192]
    send_o[...] = moved[192:]


def bias_kernel(tbl, cols, bias, table, xs):
    table_rows(tbl, 1, table)
    build_bias(table, cols, xs, bias, (flag("section"), flag("lat")))


def second_kernel(*refs):
    parts, rest = refs[:4], refs[4:]
    gains, wqkv, wproj, wup, wdown, bias, into, out_of, keep_o, send_o, stack, prob = rest
    for n in range(4):
        stack[n * 96 : n * 96 + 96, :] = parts[n][...]
    both = dot(into[...], stack[...])
    x, dflat = both[:CELLS], both[CELLS:].astype(HALF)
    gains, wqkv, wproj, wup, wdown = (w.at[1] for w in (gains, wqkv, wproj, wup, wdown))
    qkv, resid = forward_half(x, gains, wqkv, wproj, bias, prob)
    unit, spread = normalise(resid)
    normed = (unit * gains[1:2, :]).astype(HALF)
    upward = dot(normed, wup[...])
    slope = gelu_parts(upward)[1]
    dx = backward(dflat, x, qkv, prob, resid, slope, gains, wqkv, wproj, wup, wdown)
    moved = dot(out_of[...], dx.astype(HALF)).astype(HALF)
    keep_o[...] = moved[:128]
    send_o[...] = moved[128:]


def third_kernel(*refs):
    parts, rest = refs[:4], refs[4:]
    gains, wqkv, wproj, wup, wdown, patch, x_i, qkv_i, prob, resid, slope, into, out_of = rest[:13]
    grad_o, mine_o, other_o, stack, terms = rest[13:]
    for n in range(4):
        stack[n * 64 : n * 64 + 64, :] = parts[n][...]
    dflat = dot(into[...], stack[...]).astype(HALF)
    qkv = tuple(qkv_i[n] for n in range(3))
    gains, wqkv, wproj, wup, wdown = (w.at[0] for w in (gains, wqkv, wproj, wup, wdown))
    dx = backward(
        dflat, x_i[...].astype(FULL), qkv, prob, resid[...], slope[...].astype(FULL),
        gains, wqkv, wproj, wup, wdown,
    )
    grad = dx.astype(HALF)
    moved = dot(out_of[...], grad).astype(HALF)
    for z in range(2):
        for a in range(6):
            grad_o[z, a] = moved[(z * 6 + a) * 16 : (z * 6 + a) * 16 + 12]
    terms[...] = dot_tn(patch[...], grad)
    place = lax.axis_index("section") % 2
    mine_o[...] = terms[pl.ds(pl.multiple_of(place * 112, 16), 112), :].astype(HALF)
    other_o[...] = terms[pl.ds(pl.multiple_of(112 - place * 112, 16), 112), :].astype(HALF)


vmem = pl.BlockSpec(memory_space=pltpu.VMEM)
hbm = pl.BlockSpec(memory_space=pltpu.HBM)


def call(kernel, outs, scratch, *args, spec=vmem, out=vmem, room=30):
    return pl.pallas_call(
        kernel,
        out_shape=outs,
        in_specs=[spec for a in args],
        out_specs=jax.tree.map(lambda _: out, outs),
        scratch_shapes=scratch,
        compiler_params=pltpu.CompilerParams(vmem_limit_bytes=room * 2**20),
        cost_estimate=pl.CostEstimate(flops=1000000, bytes_accessed=1000000, transcendentals=0),
    )(*args)


def shape(dims, dtype=HALF):
    return jax.ShapeDtypeStruct(dims, dtype)


def fetch(block, steps):
    names = ("lon", "lat", "section")
    axes = [name for name in names if steps.get(name, 0)]
    if not axes:
        return block
    sizes = [lax.axis_size(name) for name in axes]
    pairs = []
    for place in np.ndindex(*sizes):
        source = [(p + steps[name]) % n for p, name, n in zip(place, axes, sizes)]
        pairs.append(
            (int(np.ravel_multi_index(source, sizes)), int(np.ravel_multi_index(place, sizes)))
        )
    return lax.ppermute(block, tuple(axes), pairs)


def exchange(keep, send, way):
    pitch = keep.shape[0] // 4
    got = fetch(send, {"section": way})
    blocks = []
    for n in range(4):
        rows = slice(n * pitch, (n + 1) * pitch)
        block = jnp.concatenate((keep[rows], got[rows]), 0)
        blocks.append(fetch(block, {"lat": way * (n // 2), "lon": way * (n % 2)}))
    return blocks


def swap(block, flips):
    names = ("lon", "lat", "section")
    axes = [name for name in names if flips.get(name, 0)]
    sizes = [lax.axis_size(name) for name in axes]
    pairs = []
    for place in np.ndindex(*sizes):
        source = [p ^ flips[name] for p, name in zip(place, axes)]
        pairs.append(
            (int(np.ravel_multi_index(source, sizes)), int(np.ravel_multi_index(place, sizes)))
        )
    return lax.ppermute(block, tuple(axes), pairs)


def add_up(mine, other):
    total = (mine.astype(FULL) + swap(other, {"section": 1}).astype(FULL)).astype(HALF)
    bits = []
    for name in ("section", "lat", "lon"):
        size = lax.axis_size(name)
        if size & (size - 1) or size < 2:
            raise ValueError("axis size")
        bits += [(name, 1 << n) for n in range(name == "section", size.bit_length() - 1)]
    for n in range(0, len(bits), 2):
        pair = [{name: bit} for name, bit in bits[n : n + 2]]
        if len(pair) == 1:
            total = total.astype(FULL) + swap(total, pair[0]).astype(FULL)
        else:
            one, two = pair
            three = dict(one)
            for name, bit in two.items():
                three[name] = three.get(name, 0) | bit
            near, far, last = (swap(total, step).astype(FULL) for step in (one, two, three))
            total = (total.astype(FULL) + near) + (far + last)
        total = total.astype(HALF)
    return total, swap(total, {"section": 1})


def last_kernel(scale, mine, other, upper_o, surface_o, both, sems):
    place = lax.axis_index("section") % 2
    both[pl.ds(pl.multiple_of(place * 112, 16), 112), :] = mine[...].astype(FULL) * scale
    both[pl.ds(pl.multiple_of(112 - place * 112, 16), 112), :] = other[...].astype(FULL) * scale
    copies = [
        pltpu.make_async_copy(both.at[pl.ds(0, 160)], upper_o, sems.at[0]),
        pltpu.make_async_copy(both.at[pl.ds(160, 64)], surface_o, sems.at[1]),
    ]
    for copy in copies:
        copy.start()
    for copy in copies:
        copy.wait()


def on_device(
    upper_fields,
    surface_fields,
    upper_embed,
    surface_embed,
    norm_gains,
    qkv_weight,
    proj_weight,
    up_weight,
    down_weight,
    earth_bias,
    out_grad,
):
    sections, bands = lax.axis_size("section"), lax.axis_size("lat")
    levels, rows, columns, width = out_grad.shape
    positions = earth_bias.shape[-1]
    table = earth_bias.transpose(0, 1, 3, 2, 4).reshape(2 * HEADS, 1, positions)
    weights = (norm_gains, qkv_weight, proj_weight, up_weight, down_weight.transpose(0, 2, 1))
    cols = jnp.asarray(bias_columns())

    def from_cot(z, a, o):
        return (a * 12 + o) * 2 + z

    operands = (
        table, cols, upper_fields, surface_fields, jnp.asarray(patch_select()),
        jnp.asarray(natural_to_inner()), upper_embed, surface_embed, *weights,
        out_grad.transpose(1, 2, 0, 3),
        jnp.asarray(octants_out(48, 0, True, inner_row)),
        jnp.asarray(octants_out(48, 18, True, from_cot)),
    )
    local = [
        pltpu.VMEM(v.shape[1:] if 9 <= n < 13 else v.shape, v.dtype) for n, v in enumerate(operands)
    ]
    local[6] = local[7] = pltpu.VMEM((16, 128), HALF)
    scratch_bias = [pltpu.VMEM((8, 3328), FULL), pltpu.VMEM((4, CELLS, 128), FULL)]
    keep, send, patch, x, qkv, prob, resid, slope = call(
        first_kernel,
        [
            shape((192, WIDTH)),
            shape((192, WIDTH)),
            shape((CELLS, 256)),
            shape((CELLS, WIDTH)),
            shape((3, CELLS, WIDTH)),
            shape((HEADS * CELLS, CELLS)),
            shape((CELLS, WIDTH), FULL),
            shape((CELLS, 4 * WIDTH)),
        ],
        local
        + [
            pltpu.VMEM((576, 128), FULL),
            pltpu.VMEM((288, 128), FULL),
            pltpu.VMEM((256, WIDTH), HALF),
            pltpu.VMEM((CELLS, WIDTH), FULL),
        ]
        + scratch_bias
        + [
            pltpu.VMEM((HEADS * CELLS, CELLS), FULL),
            pltpu.SemaphoreType.DMA((len(operands),)),
        ],
        *operands,
        spec=hbm,
        room=60,
    )
    bias = call(bias_kernel, shape((HEADS * CELLS, CELLS), FULL), scratch_bias, table, cols)
    into = np.concatenate((octants_in(48, 0, False), octants_in(48, 18, False)), 0)
    keep, send = call(
        second_kernel,
        [shape((128, WIDTH))] * 2,
        [pltpu.VMEM((8 * 48, WIDTH), HALF), pltpu.VMEM((HEADS * CELLS, CELLS), HALF)],
        *exchange(keep, send, 1), *weights, bias,
        jnp.asarray(into), jnp.asarray(octants_out(32, 0, False, inner_row)),
    )
    latent_grad, mine, other = call(
        third_kernel,
        [shape((2, 6, 12, WIDTH)), shape((112, WIDTH)), shape((112, WIDTH))],
        [pltpu.VMEM((8 * 32, WIDTH), HALF), pltpu.VMEM((256, WIDTH), FULL)],
        *exchange(keep, send, -1), *weights, patch, x, qkv, prob, resid, slope,
        jnp.asarray(octants_in(32, 0, True)), jnp.asarray(inner_to_padded()),
    )
    scale = float(levels * sections * rows * bands * columns * lax.axis_size("lon")) ** (-0.5)
    upper_grad, surface_grad = call(
        functools.partial(last_kernel, scale),
        [shape((160, WIDTH), FULL), shape((64, WIDTH), FULL)],
        [pltpu.VMEM((224, WIDTH), FULL), pltpu.SemaphoreType.DMA((2,))],
        *add_up(mine, other),
        out=hbm,
    )
    return (latent_grad, upper_grad, surface_grad)


def solution(mesh):
    placed = (
        P(None, None, "lat", "lon"),
        P(None, "lat", "lon"),
        P(),
        P(),
        P(),
        P(),
        P(),
        P(),
        P(),
        P(None, "lat", "section", None, None),
        P("section", "lat", "lon", None),
    )
    return jax.shard_map(
        on_device,
        mesh=mesh,
        in_specs=placed,
        out_specs=(P("section", "lat", "lon", None), P(), P()),
        check_vma=False,
    )
```

```python
import functools

import jax
import jax.numpy as jnp
import ml_dtypes
import numpy as np
from jax import lax
from jax.experimental import pallas as pl
from jax.experimental.pallas import tpu as pltpu
from jax.sharding import PartitionSpec as P

neg_fill = -1e30
norm_eps = 1e-05
HEADS = 6
HEAD = 32
CELLS = 144
WIDTH = 192
FULL = jnp.float32
HALF = jnp.bfloat16


def inner_row(z, a, o):
    return o * 12 + z * 6 + a


def octant_of(z, a, o):
    return (z * 4 + (a // 3) * 2 + o // 6, (a % 3) * 6 + o % 6)


def as_half(array):
    return array.astype(ml_dtypes.bfloat16)


def patch_select():
    sel = np.zeros((512, 512), np.float32)
    for c in range(4):
        for b in range(4):
            base = c * 128 + b * 32
            for z in range(2):
                for a in range(2):
                    for v in range(5):
                        sel[base + (z * 2 + a) * 5 + v, z * 256 + v * 32 + a * 16 + b * 4 + c] = 1
            for v in range(4):
                sel[base + 20 + v, 160 + v * 16 + b * 4 + c] = 1
    return as_half(sel)


def cells():
    return [(z, a, o) for z in range(2) for a in range(6) for o in range(12)]


def natural_to_inner():
    move = np.zeros((CELLS, CELLS), np.float32)
    for z, a, o in cells():
        move[inner_row(z, a, o), (z * 6 + a) * 12 + o] = 1
    return as_half(move)


def inner_to_padded():
    move = np.zeros((192, CELLS), np.float32)
    for z, a, o in cells():
        move[(z * 6 + a) * 16 + o, inner_row(z, a, o)] = 1
    return as_half(move)


def octants_out(pitch, first, flip, source):
    move = np.zeros((8 * pitch, CELLS), np.float32)
    for z, a, o in cells():
        part, place = octant_of(z, a, o)
        move[(7 - part if flip else part) * pitch + first + place, source(z, a, o)] = 1
    return as_half(move)


def octants_in(pitch, first, flip):
    move = np.zeros((CELLS, 8 * pitch), np.float32)
    for z, a, o in cells():
        part, place = octant_of(z, a, o)
        part = 7 - part if flip else part
        block = (part % 4) * 2 + part // 4
        move[inner_row(z, a, o), block * pitch + first + place] = 1
    return as_half(move)


def bias_columns():
    move = np.zeros((2, 256, 384), np.float32)
    for z in range(2):
        for a in range(6):
            for k in range(23):
                move[z, a * 23 + k, (22 - k) * 12 + z * 6 + a] = 1
    return as_half(move)


def dot(a, b):
    return jnp.dot(a, b, preferred_element_type=FULL)


def dot_nt(a, b):
    return lax.dot_general(a, b, (((1,), (1,)), ((), ())), preferred_element_type=FULL)


def dot_tn(a, b):
    return lax.dot_general(a, b, (((0,), (0,)), ((), ())), preferred_element_type=FULL)


def normalise(v):
    mean = jnp.mean(v, -1, keepdims=True)
    centred = v - mean
    spread = lax.rsqrt(jnp.mean(centred * centred, -1, keepdims=True) + norm_eps)
    return centred * spread, spread


def normalise_back(dy, unit, spread, gain):
    dunit = dy * gain
    inner = jnp.mean(dunit * unit, -1, keepdims=True)
    return spread * (dunit - jnp.mean(dunit, -1, keepdims=True) - unit * inner)


def head_lanes(h):
    lane = lax.broadcasted_iota(jnp.int32, (1, WIDTH), 1)
    return (lane >= h * HEAD) & (lane < (h + 1) * HEAD)


def head_mask(h):
    return jnp.where(head_lanes(h), 1.0, 0.0).astype(HALF)


def build_bias(tbl, cols, xs, bias, edges):
    for z in range(2):
        for a in range(6):
            for zu in range(2):
                start = ((z * 2 + zu) * 6 + a) * 138
                piece = tbl[0:HEADS, start : start + 138]
                piece = jnp.concatenate((piece, jnp.zeros((HEADS, 118), FULL)), 1)
                for p in range(2):
                    for half in range(2):
                        xs[zu * 2 + half, pl.ds(p * 12 + z * 6 + a, HEADS, stride=24), :] = piece[
                            :, half * 128 : half * 128 + 128
                        ]
    total = None
    for zu in range(2):
        x = jnp.concatenate((xs[zu * 2], xs[zu * 2 + 1]), 1)
        high = x.astype(HALF)
        left = x - high.astype(FULL)
        mid = left.astype(HALF)
        low = (left - mid.astype(FULL)).astype(HALF)
        term = dot(jnp.concatenate((high, mid, low), 0), cols[zu])
        total = term if total is None else total + term
    table = total[:CELLS] + total[CELLS : 2 * CELLS] + total[2 * CELLS :]
    row = lax.broadcasted_iota(jnp.int32, (CELLS, 1), 0).astype(FULL)
    lane = lax.broadcasted_iota(jnp.int32, (1, CELLS), 1).astype(FULL)

    def part(v, size):
        return jnp.floor((v + 0.5) * (1.0 / size))

    even = part(row, 12) - 2.0 * part(part(row, 12), 2) == 0.0
    table = jnp.where(even, pltpu.roll(table, 384 - 12, 1), table)
    if edges is not None:
        last_section, last_band = edges
        row12, lane12 = row - 12.0 * part(row, 12), lane - 12.0 * part(lane, 12)
        row_z, lane_z = part(row12, 6), part(lane12, 6)
        row_a, lane_a = part(row12 - 6.0 * row_z, 3), part(lane12 - 6.0 * lane_z, 3)
        apart = jnp.abs(row_z - lane_z) * last_section + jnp.abs(row_a - lane_a) * last_band
        blocked = apart > 0.5
    for j in range(6):
        shift = (10 - 2 * j) * 12
        moved = pltpu.roll(table, 384 - shift, 1) if shift else table
        moved = moved[:, :CELLS]
        if edges is not None:
            moved = jnp.where(blocked, neg_fill, moved)
        for h in range(HEADS):
            bias[h * CELLS + j * 24 : h * CELLS + j * 24 + 24, :] = moved[h * 24 : h * 24 + 24, :]


def attend(q, k, v, bias, prob):
    mixed = jnp.zeros((CELLS, WIDTH), FULL)
    for h in range(HEADS):
        rows = slice(h * CELLS, (h + 1) * CELLS)
        score = dot_nt(q * head_mask(h), k) * HEAD ** (-0.5) + bias[rows, :]
        expo = jnp.exp(score - jnp.max(score, -1, keepdims=True))
        weights = (expo * (1.0 / jnp.sum(expo, -1, keepdims=True))).astype(HALF)
        prob[rows, :] = weights
        mixed = jnp.where(head_lanes(h), dot(weights, v), mixed)
    return mixed.astype(HALF)


def attend_back(dmixed, q, k, v, prob):
    dq = jnp.zeros((CELLS, WIDTH), FULL)
    dk = jnp.zeros((CELLS, WIDTH), FULL)
    dv = jnp.zeros((CELLS, WIDTH), FULL)
    for h in range(HEADS):
        rows = slice(h * CELLS, (h + 1) * CELLS)
        weights = prob[rows, :]
        dhead = dmixed * head_mask(h)
        full = weights.astype(FULL)
        dweights = dot_nt(dhead, v)
        inner = jnp.sum(dweights * full, -1, keepdims=True)
        dscore = (full * (dweights - inner) * HEAD ** (-0.5)).astype(HALF)
        dv = dv + dot_tn(weights, dhead)
        dq = jnp.where(head_lanes(h), dot(dscore, k), dq)
        dk = dk + dot_tn(dscore, q * head_mask(h))
    return dq.astype(HALF), dk.astype(HALF), dv.astype(HALF)


def gelu_parts(u):
    below = 0.5 * (1.0 + lax.erf(u * (0.5**0.5)))
    slope = below + u * (jnp.exp(-0.5 * u * u) * (2.0 * np.pi) ** (-0.5))
    return below, slope


def forward_half(x, gains, wqkv, wproj, bias, prob):
    unit, spread = normalise(x)
    hidden = (unit * gains[0:1, :]).astype(HALF)
    qkv = dot(hidden, wqkv[...]).astype(HALF)
    q, k, v = (qkv[:, n * WIDTH : (n + 1) * WIDTH] for n in range(3))
    mixed = attend(q, k, v, bias, prob)
    return (q, k, v), x + dot(mixed, wproj[...])


def backward(dflat, x, qkv, prob, resid, slope, gains, wqkv, wproj, wup, wdown):
    q, k, v = qkv
    dactive = dot(dflat, wdown[...])
    dupward = (dactive * slope).astype(HALF)
    dnormed = dot_nt(dupward, wup[...])
    unit, spread = normalise(resid)
    dresid = dflat.astype(FULL) + normalise_back(dnormed, unit, spread, gains[1:2, :])
    dmixed = dot_nt(dresid.astype(HALF), wproj[...]).astype(HALF)
    dq, dk, dv = attend_back(dmixed, q, k, v, prob)
    dhidden = dot_nt(dq, wqkv[:, :WIDTH])
    dhidden = dhidden + dot_nt(dk, wqkv[:, WIDTH : 2 * WIDTH])
    dhidden = dhidden + dot_nt(dv, wqkv[:, 2 * WIDTH :])
    unit, spread = normalise(x)
    return dresid + normalise_back(dhidden, unit, spread, gains[0:1, :])


def gather_patches(upper, surface, section, select, ff, ft):
    base = 4 * section - 2
    for z in range(2):
        for a in range(2):
            level = jnp.maximum(base + 2 * z + a, 0)
            for v in range(5):
                field = upper[v, level].astype(FULL)
                if z == 0:
                    field = jnp.where(section == 0, 0.0, field)
                slot = (z * 2 + a) * 5 + v
                ff[slot * 24 : slot * 24 + 24, 0:48] = field
    for v in range(4):
        field = jnp.where(section == 0, surface[v].astype(FULL), 0.0)
        ff[(20 + v) * 24 : (21 + v) * 24, 0:48] = field
    pad = jnp.zeros((8, 128), FULL)
    for i in range(6):
        pieces = []
        for b in range(4):
            pieces += [ff[pl.ds(4 * i + b, 24, stride=24), :], pad]
        ft[i * 48 : i * 48 + 48, :] = jnp.concatenate(pieces, 0).T[:48]
    raw = [ft[pl.ds(c, 72, stride=4), :].astype(HALF) for c in range(4)]
    both = dot(jnp.concatenate(raw, 1), select[...])
    return jnp.concatenate((both[:, :256], both[:, 256:]), 0).astype(HALF)


def flag(axis):
    last = lax.axis_index(axis) == lax.axis_size(axis) - 1
    return jnp.where(last, 1.0, 0.0)


def table_rows(tbl, block, table):
    for h in range(HEADS):
        table[h : h + 1, 0 : tbl.shape[-1]] = tbl[block * HEADS + h]


def first_kernel(*refs):
    names = (
        "tbl", "cols", "upper", "surface", "select", "to_inner", "uembed", "sembed", "gains",
        "wqkv", "wproj", "wup", "wdown", "cot", "out_first", "out_cot",
    )
    count = len(names)
    source, rest = refs[:count], refs[count:]
    keep_o, send_o, patch_o, x_o, qkv_o, prob, resid_o, slope_o = rest[:8]
    local, rest = rest[8 : 8 + count], rest[8 + count :]
    ff, ft, emb, cots, table, xs, bias, sems = rest
    copies = {}
    for n, name in enumerate(names):
        start = source[n].at[0] if name[0] == "w" else source[n]
        if name == "uembed":
            target = emb.at[pl.ds(0, 160)]
        elif name == "sembed":
            target = emb.at[pl.ds(160, 64)]
        else:
            target = local[n]
        copies[name] = pltpu.make_async_copy(start, target, sems.at[n])
        copies[name].start()
    have = dict(zip(names, local))

    def wait(*which):
        for name in which:
            copies[name].wait()

    emb[224:256, :] = jnp.zeros((32, WIDTH), HALF)
    wait("tbl", "cols")
    table_rows(have["tbl"], 0, table)
    build_bias(table, have["cols"], xs, bias, None)
    wait("upper", "surface", "select", "to_inner", "uembed", "sembed", "gains", "wqkv")
    section = lax.axis_index("section")
    patch = gather_patches(have["upper"], have["surface"], section, have["select"], ff, ft)
    patch = dot(have["to_inner"][...], patch).astype(HALF)
    patch_o[...] = patch
    latent = dot(patch, emb[...]).astype(HALF)
    x_o[...] = latent
    x = latent.astype(FULL)
    gains = have["gains"].at[0]
    wait("wproj", "wup", "wdown", "cot", "out_first", "out_cot")
    cot = have["cot"]
    for a in range(6):
        for o in range(12):
            cots[(a * 12 + o) * 2 : (a * 12 + o) * 2 + 2, :] = cot[a, o].astype(FULL)
    qkv, resid = forward_half(x, gains, have["wqkv"], have["wproj"], bias, prob)
    for n in range(3):
        qkv_o[n] = qkv[n]
    resid_o[...] = resid
    unit, spread = normalise(resid)
    normed = (unit * gains[1:2, :]).astype(HALF)
    upward = dot(normed, have["wup"][...])
    below, slope = gelu_parts(upward)
    slope_o[...] = slope.astype(HALF)
    active = (upward * below).astype(HALF)
    result = (resid + dot_nt(active, have["wdown"][...])).astype(HALF)
    moved = dot(have["out_first"][...], result)
    moved = (moved + dot(have["out_cot"][...], cots[...].astype(HALF))).astype(HALF)
    keep_o[...] = moved[:192]
    send_o[...] = moved[192:]


def bias_kernel(tbl, cols, bias, table, xs):
    table_rows(tbl, 1, table)
    build_bias(table, cols, xs, bias, (flag("section"), flag("lat")))


def second_kernel(*refs):
    parts, rest = refs[:4], refs[4:]
    gains, wqkv, wproj, wup, wdown, bias, into, out_of, keep_o, send_o, stack, prob = rest
    for n in range(4):
        stack[n * 96 : n * 96 + 96, :] = parts[n][...]
    both = dot(into[...], stack[...])
    x, dflat = both[:CELLS], both[CELLS:].astype(HALF)
    gains, wqkv, wproj, wup, wdown = (w.at[1] for w in (gains, wqkv, wproj, wup, wdown))
    qkv, resid = forward_half(x, gains, wqkv, wproj, bias, prob)
    unit, spread = normalise(resid)
    normed = (unit * gains[1:2, :]).astype(HALF)
    upward = dot(normed, wup[...])
    slope = gelu_parts(upward)[1]
    dx = backward(dflat, x, qkv, prob, resid, slope, gains, wqkv, wproj, wup, wdown)
    moved = dot(out_of[...], dx.astype(HALF)).astype(HALF)
    keep_o[...] = moved[:128]
    send_o[...] = moved[128:]


def third_kernel(*refs):
    parts, rest = refs[:4], refs[4:]
    gains, wqkv, wproj, wup, wdown, patch, x_i, qkv_i, prob, resid, slope, into, out_of = rest[:13]
    grad_o, chunks_o, stack, terms = rest[13:]
    for n in range(4):
        stack[n * 64 : n * 64 + 64, :] = parts[n][...]
    dflat = dot(into[...], stack[...]).astype(HALF)
    qkv = tuple(qkv_i[n] for n in range(3))
    gains, wqkv, wproj, wup, wdown = (w.at[0] for w in (gains, wqkv, wproj, wup, wdown))
    dx = backward(
        dflat, x_i[...].astype(FULL), qkv, prob, resid[...], slope[...].astype(FULL),
        gains, wqkv, wproj, wup, wdown,
    )
    grad = dx.astype(HALF)
    moved = dot(out_of[...], grad).astype(HALF)
    for z in range(2):
        for a in range(6):
            grad_o[z, a] = moved[(z * 6 + a) * 16 : (z * 6 + a) * 16 + 12]
    terms[...] = dot_tn(patch[...], grad)
    count = chunks_o.shape[1]
    for n in range(chunks_o.shape[0]):
        if n * count < 224:
            chunks_o[n] = terms[n * count : (n + 1) * count, :].astype(HALF)
        else:
            chunks_o[n] = jnp.zeros(chunks_o.shape[1:], HALF)


vmem = pl.BlockSpec(memory_space=pltpu.VMEM)
hbm = pl.BlockSpec(memory_space=pltpu.HBM)


def call(kernel, outs, scratch, *args, spec=vmem, out=vmem, room=30):
    return pl.pallas_call(
        kernel,
        out_shape=outs,
        in_specs=[spec for a in args],
        out_specs=jax.tree.map(lambda _: out, outs),
        scratch_shapes=scratch,
        compiler_params=pltpu.CompilerParams(vmem_limit_bytes=room * 2**20),
        cost_estimate=pl.CostEstimate(flops=1000000, bytes_accessed=1000000, transcendentals=0),
    )(*args)


def shape(dims, dtype=HALF):
    return jax.ShapeDtypeStruct(dims, dtype)


def fetch(block, steps):
    names = ("lon", "lat", "section")
    axes = [name for name in names if steps.get(name, 0)]
    if not axes:
        return block
    sizes = [lax.axis_size(name) for name in axes]
    pairs = []
    for place in np.ndindex(*sizes):
        source = [(p + steps[name]) % n for p, name, n in zip(place, axes, sizes)]
        pairs.append(
            (int(np.ravel_multi_index(source, sizes)), int(np.ravel_multi_index(place, sizes)))
        )
    return lax.ppermute(block, tuple(axes), pairs)


def exchange(keep, send, way):
    pitch = keep.shape[0] // 4
    got = fetch(send, {"section": way})
    blocks = []
    for n in range(4):
        rows = slice(n * pitch, (n + 1) * pitch)
        block = jnp.concatenate((keep[rows], got[rows]), 0)
        blocks.append(fetch(block, {"lat": way * (n // 2), "lon": way * (n % 2)}))
    return blocks


def swap(block, flips):
    names = ("lon", "lat", "section")
    axes = [name for name in names if flips.get(name, 0)]
    sizes = [lax.axis_size(name) for name in axes]
    pairs = []
    for place in np.ndindex(*sizes):
        source = [p ^ flips[name] for p, name in zip(place, axes)]
        pairs.append(
            (int(np.ravel_multi_index(source, sizes)), int(np.ravel_multi_index(place, sizes)))
        )
    return lax.ppermute(block, tuple(axes), pairs)


def add_up(chunks):
    axes = ("lon", "lat", "section")
    mine = lax.all_to_all(chunks, axes, 0, 0, tiled=True)
    mine = jnp.sum(mine.astype(FULL), 0, keepdims=True).astype(HALF)
    return lax.all_to_all(jnp.broadcast_to(mine, chunks.shape), axes, 0, 0, tiled=True)


def last_kernel(scale, chunks, upper_o, surface_o, both, sems):
    count = chunks.shape[1]
    for n in range(224 // count):
        both[n * count : (n + 1) * count, :] = chunks[n].astype(FULL) * scale
    copies = [
        pltpu.make_async_copy(both.at[pl.ds(0, 160)], upper_o, sems.at[0]),
        pltpu.make_async_copy(both.at[pl.ds(160, 64)], surface_o, sems.at[1]),
    ]
    for copy in copies:
        copy.start()
    for copy in copies:
        copy.wait()


def on_device(
    upper_fields,
    surface_fields,
    upper_embed,
    surface_embed,
    norm_gains,
    qkv_weight,
    proj_weight,
    up_weight,
    down_weight,
    earth_bias,
    out_grad,
):
    sections, bands = lax.axis_size("section"), lax.axis_size("lat")
    levels, rows, columns, width = out_grad.shape
    positions = earth_bias.shape[-1]
    table = earth_bias.transpose(0, 1, 3, 2, 4).reshape(2 * HEADS, 1, positions)
    weights = (norm_gains, qkv_weight, proj_weight, up_weight, down_weight.transpose(0, 2, 1))
    cols = jnp.asarray(bias_columns())

    def from_cot(z, a, o):
        return (a * 12 + o) * 2 + z

    operands = (
        table, cols, upper_fields, surface_fields, jnp.asarray(patch_select()),
        jnp.asarray(natural_to_inner()), upper_embed, surface_embed, *weights,
        out_grad.transpose(1, 2, 0, 3),
        jnp.asarray(octants_out(48, 0, True, inner_row)),
        jnp.asarray(octants_out(48, 18, True, from_cot)),
    )
    local = [
        pltpu.VMEM(v.shape[1:] if 9 <= n < 13 else v.shape, v.dtype) for n, v in enumerate(operands)
    ]
    local[6] = local[7] = pltpu.VMEM((16, 128), HALF)
    scratch_bias = [pltpu.VMEM((8, 3328), FULL), pltpu.VMEM((4, CELLS, 128), FULL)]
    keep, send, patch, x, qkv, prob, resid, slope = call(
        first_kernel,
        [
            shape((192, WIDTH)),
            shape((192, WIDTH)),
            shape((CELLS, 256)),
            shape((CELLS, WIDTH)),
            shape((3, CELLS, WIDTH)),
            shape((HEADS * CELLS, CELLS)),
            shape((CELLS, WIDTH), FULL),
            shape((CELLS, 4 * WIDTH)),
        ],
        local
        + [
            pltpu.VMEM((576, 128), FULL),
            pltpu.VMEM((288, 128), FULL),
            pltpu.VMEM((256, WIDTH), HALF),
            pltpu.VMEM((CELLS, WIDTH), FULL),
        ]
        + scratch_bias
        + [
            pltpu.VMEM((HEADS * CELLS, CELLS), FULL),
            pltpu.SemaphoreType.DMA((len(operands),)),
        ],
        *operands,
        spec=hbm,
        room=60,
    )
    bias = call(bias_kernel, shape((HEADS * CELLS, CELLS), FULL), scratch_bias, table, cols)
    into = np.concatenate((octants_in(48, 0, False), octants_in(48, 18, False)), 0)
    keep, send = call(
        second_kernel,
        [shape((128, WIDTH))] * 2,
        [pltpu.VMEM((8 * 48, WIDTH), HALF), pltpu.VMEM((HEADS * CELLS, CELLS), HALF)],
        *exchange(keep, send, 1), *weights, bias,
        jnp.asarray(into), jnp.asarray(octants_out(32, 0, False, inner_row)),
    )
    devices = sections * bands * lax.axis_size("lon")
    latent_grad, chunks = call(
        third_kernel,
        [shape((2, 6, 12, WIDTH)), shape((devices, -(-224 // devices), WIDTH))],
        [pltpu.VMEM((8 * 32, WIDTH), HALF), pltpu.VMEM((256, WIDTH), FULL)],
        *exchange(keep, send, -1), *weights, patch, x, qkv, prob, resid, slope,
        jnp.asarray(octants_in(32, 0, True)), jnp.asarray(inner_to_padded()),
    )
    scale = float(levels * sections * rows * bands * columns * lax.axis_size("lon")) ** (-0.5)
    upper_grad, surface_grad = call(
        functools.partial(last_kernel, scale),
        [shape((160, WIDTH), FULL), shape((64, WIDTH), FULL)],
        [pltpu.VMEM((224, WIDTH), FULL), pltpu.SemaphoreType.DMA((2,))],
        add_up(chunks),
        out=hbm,
    )
    return (latent_grad, upper_grad, surface_grad)


def solution(mesh):
    placed = (
        P(None, None, "lat", "lon"),
        P(None, "lat", "lon"),
        P(),
        P(),
        P(),
        P(),
        P(),
        P(),
        P(),
        P(None, "lat", "section", None, None),
        P("section", "lat", "lon", None),
    )
    return jax.shard_map(
        on_device,
        mesh=mesh,
        in_specs=placed,
        out_specs=(P("section", "lat", "lon", None), P(), P()),
        check_vma=False,
    )
```

```python
import functools

import jax
import jax.numpy as jnp
import ml_dtypes
import numpy as np
from jax import lax
from jax.experimental import pallas as pl
from jax.experimental.pallas import tpu as pltpu
from jax.sharding import PartitionSpec as P

neg_fill = -1e30
norm_eps = 1e-05
HEADS = 6
HEAD = 32
CELLS = 144
WIDTH = 192
FULL = jnp.float32
HALF = jnp.bfloat16


def inner_row(z, a, o):
    return o * 12 + z * 6 + a


def octant_of(z, a, o):
    return (z * 4 + (a // 3) * 2 + o // 6, (a % 3) * 6 + o % 6)


def as_half(array):
    return array.astype(ml_dtypes.bfloat16)


def cells():
    return [(z, a, o) for z in range(2) for a in range(6) for o in range(12)]


def natural_to_inner():
    move = np.zeros((CELLS, CELLS), np.float32)
    for z, a, o in cells():
        move[inner_row(z, a, o), (z * 6 + a) * 12 + o] = 1
    return as_half(move)


def inner_to_padded():
    move = np.zeros((192, CELLS), np.float32)
    for z, a, o in cells():
        move[(z * 6 + a) * 16 + o, inner_row(z, a, o)] = 1
    return as_half(move)


def pair_out():
    move = np.zeros((512, 3 * CELLS), np.float32)
    for z, a, o in cells():
        part, place = octant_of(z, a, o)
        for n in range(3):
            slot = (7 - part) % 4 * 2 + (7 - part) // 4
            move[slot * 64 + n * 18 + place, n * CELLS + inner_row(z, a, o)] = 1
    return as_half(move)


def pair_in():
    move = np.zeros((3 * CELLS, 512), np.float32)
    for z, a, o in cells():
        part, place = octant_of(z, a, o)
        for n in range(3):
            move[n * CELLS + inner_row(z, a, o), part * 64 + n * 18 + place] = 1
    return as_half(move)


def single_place(place):
    return place, 1 + place // 9, 18 + place % 9


def single_out():
    move = np.zeros((256, 3 * CELLS), np.float32)
    for z, a, o in cells():
        part, place = octant_of(z, a, o)
        first, group, last = single_place(place)
        slot = part % 4 * 2 + part // 4
        move[slot * 32 + first, inner_row(z, a, o)] = 1
        move[slot * 32 + last, group * CELLS + inner_row(z, a, o)] = 1
    return as_half(move)


def single_in():
    move = np.zeros((3 * CELLS, 256), np.float32)
    for z, a, o in cells():
        part, place = octant_of(z, a, o)
        first, group, last = single_place(place)
        move[inner_row(z, a, o), (7 - part) * 32 + first] = 1
        move[group * CELLS + inner_row(z, a, o), (7 - part) * 32 + last] = 1
    return as_half(move)


def whole_part(v, size):
    return jnp.floor((v + 0.5) * (1.0 / size))


def one_hot(target, lanes):
    lane = lax.broadcasted_iota(jnp.int32, (1, lanes), 1).astype(FULL)
    return jnp.where(lane == target, 1.0, 0.0).astype(HALF)


def fill_columns(cols):
    row = lax.broadcasted_iota(jnp.int32, (256, 1), 0).astype(FULL)
    a = whole_part(row, 23)
    k = row - 23.0 * a
    for z in range(2):
        target = (22.0 - k) * 12.0 + (z * 6.0) + a
        cols[z] = one_hot(jnp.where(row < 138.0, target, -1.0), 384)


def fill_select(select):
    row = lax.broadcasted_iota(jnp.int32, (128, 1), 0).astype(FULL)
    b = whole_part(row, 32)
    slot = row - 32.0 * b
    layer = whole_part(slot, 5)
    z = whole_part(layer, 2)
    upper = z * 256.0 + (slot - 5.0 * layer) * 32.0 + (layer - 2.0 * z) * 16.0
    surface = 160.0 + (slot - 20.0) * 16.0
    target = jnp.where(slot < 20.0, upper, surface) + b * 4.0
    for c in range(4):
        select[c * 128 : c * 128 + 128, :] = one_hot(
            jnp.where(slot < 24.0, target + float(c), -1.0), 512
        )


def dot(a, b):
    return jnp.dot(a, b, preferred_element_type=FULL)


def dot_nt(a, b):
    return lax.dot_general(a, b, (((1,), (1,)), ((), ())), preferred_element_type=FULL)


def dot_tn(a, b):
    return lax.dot_general(a, b, (((0,), (0,)), ((), ())), preferred_element_type=FULL)


def normalise(v):
    mean = jnp.mean(v, -1, keepdims=True)
    centred = v - mean
    spread = lax.rsqrt(jnp.mean(centred * centred, -1, keepdims=True) + norm_eps)
    return centred * spread, spread


def normalise_back(dy, unit, spread, gain):
    dunit = dy * gain
    inner = jnp.mean(dunit * unit, -1, keepdims=True)
    return spread * (dunit - jnp.mean(dunit, -1, keepdims=True) - unit * inner)


def head_lanes(h):
    lane = lax.broadcasted_iota(jnp.int32, (1, WIDTH), 1)
    return (lane >= h * HEAD) & (lane < (h + 1) * HEAD)


def head_mask(h):
    return jnp.where(head_lanes(h), 1.0, 0.0).astype(HALF)


def build_bias(tbl, cols, xs, bias, edges):
    for z in range(2):
        for a in range(6):
            for zu in range(2):
                start = ((z * 2 + zu) * 6 + a) * 138
                piece = tbl[0:HEADS, start : start + 138]
                piece = jnp.concatenate((piece, jnp.zeros((HEADS, 118), FULL)), 1)
                for p in range(2):
                    for half in range(2):
                        xs[zu * 2 + half, pl.ds(p * 12 + z * 6 + a, HEADS, stride=24), :] = piece[
                            :, half * 128 : half * 128 + 128
                        ]
    total = None
    for zu in range(2):
        x = jnp.concatenate((xs[zu * 2], xs[zu * 2 + 1]), 1)
        high = x.astype(HALF)
        left = x - high.astype(FULL)
        mid = left.astype(HALF)
        low = (left - mid.astype(FULL)).astype(HALF)
        term = dot(jnp.concatenate((high, mid, low), 0), cols[zu])
        total = term if total is None else total + term
    table = total[:CELLS] + total[CELLS : 2 * CELLS] + total[2 * CELLS :]
    row = lax.broadcasted_iota(jnp.int32, (CELLS, 1), 0).astype(FULL)
    lane = lax.broadcasted_iota(jnp.int32, (1, CELLS), 1).astype(FULL)

    part = whole_part
    even = part(row, 12) - 2.0 * part(part(row, 12), 2) == 0.0
    table = jnp.where(even, pltpu.roll(table, 384 - 12, 1), table)
    if edges is not None:
        last_section, last_band = edges
        row12, lane12 = row - 12.0 * part(row, 12), lane - 12.0 * part(lane, 12)
        row_z, lane_z = part(row12, 6), part(lane12, 6)
        row_a, lane_a = part(row12 - 6.0 * row_z, 3), part(lane12 - 6.0 * lane_z, 3)
        apart = jnp.abs(row_z - lane_z) * last_section + jnp.abs(row_a - lane_a) * last_band
        blocked = apart > 0.5
    for j in range(6):
        shift = (10 - 2 * j) * 12
        moved = pltpu.roll(table, 384 - shift, 1) if shift else table
        moved = moved[:, :CELLS]
        if edges is not None:
            moved = jnp.where(blocked, neg_fill, moved)
        for h in range(HEADS):
            bias[h * CELLS + j * 24 : h * CELLS + j * 24 + 24, :] = moved[h * 24 : h * 24 + 24, :]


def attend(q, k, v, bias, prob):
    mixed = jnp.zeros((CELLS, WIDTH), FULL)
    for h in range(HEADS):
        rows = slice(h * CELLS, (h + 1) * CELLS)
        score = dot_nt(q * head_mask(h), k) * HEAD ** (-0.5) + bias[rows, :]
        expo = jnp.exp(score - jnp.max(score, -1, keepdims=True))
        weights = (expo * (1.0 / jnp.sum(expo, -1, keepdims=True))).astype(HALF)
        prob[rows, :] = weights
        mixed = jnp.where(head_lanes(h), dot(weights, v), mixed)
    return mixed.astype(HALF)


def attend_back(dmixed, q, k, v, prob):
    dq = jnp.zeros((CELLS, WIDTH), FULL)
    dk = jnp.zeros((CELLS, WIDTH), FULL)
    dv = jnp.zeros((CELLS, WIDTH), FULL)
    for h in range(HEADS):
        rows = slice(h * CELLS, (h + 1) * CELLS)
        weights = prob[rows, :]
        dhead = dmixed * head_mask(h)
        full = weights.astype(FULL)
        dweights = dot_nt(dhead, v)
        inner = jnp.sum(dweights * full, -1, keepdims=True)
        dscore = (full * (dweights - inner) * HEAD ** (-0.5)).astype(HALF)
        dv = dv + dot_tn(weights, dhead)
        dq = jnp.where(head_lanes(h), dot(dscore, k), dq)
        dk = dk + dot_tn(dscore, q * head_mask(h))
    return dq.astype(HALF), dk.astype(HALF), dv.astype(HALF)


def gelu_parts(u):
    below = 0.5 * (1.0 + lax.erf(u * (0.5**0.5)))
    slope = below + u * (jnp.exp(-0.5 * u * u) * (2.0 * np.pi) ** (-0.5))
    return below, slope


def forward_half(x, gains, wqkv, wproj, bias, prob):
    unit, spread = normalise(x)
    hidden = (unit * gains[0:1, :]).astype(HALF)
    qkv = dot(hidden, wqkv[...]).astype(HALF)
    q, k, v = (qkv[:, n * WIDTH : (n + 1) * WIDTH] for n in range(3))
    mixed = attend(q, k, v, bias, prob)
    return (q, k, v), x + dot(mixed, wproj[...])


def backward(dflat, x, qkv, prob, resid, slope, gains, wqkv, wproj, wup, wdown):
    q, k, v = qkv
    dactive = dot(dflat, wdown[...])
    dupward = (dactive * slope).astype(HALF)
    dnormed = dot_nt(dupward, wup[...])
    unit, spread = normalise(resid)
    dresid = dflat.astype(FULL) + normalise_back(dnormed, unit, spread, gains[1:2, :])
    dmixed = dot_nt(dresid.astype(HALF), wproj[...]).astype(HALF)
    dq, dk, dv = attend_back(dmixed, q, k, v, prob)
    dhidden = dot_nt(dq, wqkv[:, :WIDTH])
    dhidden = dhidden + dot_nt(dk, wqkv[:, WIDTH : 2 * WIDTH])
    dhidden = dhidden + dot_nt(dv, wqkv[:, 2 * WIDTH :])
    unit, spread = normalise(x)
    return dresid + normalise_back(dhidden, unit, spread, gains[0:1, :])


def gather_patches(upper, surface, section, select, ff, ft):
    base = 4 * section - 2
    for z in range(2):
        for a in range(2):
            level = jnp.maximum(base + 2 * z + a, 0)
            for v in range(5):
                field = upper[v, level].astype(FULL)
                if z == 0:
                    field = jnp.where(section == 0, 0.0, field)
                slot = (z * 2 + a) * 5 + v
                ff[slot * 24 : slot * 24 + 24, 0:48] = field
    for v in range(4):
        field = jnp.where(section == 0, surface[v].astype(FULL), 0.0)
        ff[(20 + v) * 24 : (21 + v) * 24, 0:48] = field
    pad = jnp.zeros((8, 128), FULL)
    for i in range(6):
        pieces = []
        for b in range(4):
            pieces += [ff[pl.ds(4 * i + b, 24, stride=24), :], pad]
        ft[i * 48 : i * 48 + 48, :] = jnp.concatenate(pieces, 0).T[:48]
    raw = [ft[pl.ds(c, 72, stride=4), :].astype(HALF) for c in range(4)]
    both = dot(jnp.concatenate(raw, 1), select[...])
    return jnp.concatenate((both[:, :256], both[:, 256:]), 0).astype(HALF)


def flag(axis):
    last = lax.axis_index(axis) == lax.axis_size(axis) - 1
    return jnp.where(last, 1.0, 0.0)


def table_rows(tbl, block, table):
    for h in range(HEADS):
        table[h : h + 1, 0 : tbl.shape[-1]] = tbl[block * HEADS + h]


def first_kernel(*refs):
    names = (
        "tbl", "upper", "surface", "to_inner", "uembed", "sembed", "gains",
        "wqkv", "wproj", "wup", "wdown", "cot", "out",
    )
    count = len(names)
    source, refs = refs[:count], refs[count:]
    results = ("patch", "x", "qkv", "prob", "resid", "slope", "block0", "block1", "block2", "block3")
    target, refs = refs[: len(results)], refs[len(results) :]
    local, refs = refs[:count], refs[count:]
    patch_s, x_s, qkv_s, prob, resid_s, slope_s, blocks = refs[:7]
    ff, ft, emb, cots, table, xs, bias, cols, select, sems = refs[7:]
    copies = {}
    for n, name in enumerate(names):
        start, end = source[n], local[n]
        if name[0] == "w":
            start = start.at[0]
        elif name == "tbl":
            start = start.at[pl.ds(0, HEADS)]
        elif name == "uembed":
            end = emb.at[pl.ds(0, 160)]
        elif name == "sembed":
            end = emb.at[pl.ds(160, 64)]
        copies[name] = pltpu.make_async_copy(start, end, sems.at[n])
        copies[name].start()
    have = dict(zip(names, local))
    sent = []

    def wait(*which):
        for name in which:
            copies[name].wait()

    def send(name, held):
        n = results.index(name)
        sent.append(pltpu.make_async_copy(held, target[n], sems.at[count + n]))
        sent[-1].start()

    emb[224:256, :] = jnp.zeros((32, WIDTH), HALF)
    fill_columns(cols)
    fill_select(select)
    wait("tbl")
    table_rows(have["tbl"], 0, table)
    build_bias(table, cols, xs, bias, None)
    wait("upper", "surface", "to_inner", "uembed", "sembed", "gains", "wqkv")
    section = lax.axis_index("section")
    patch = gather_patches(have["upper"], have["surface"], section, select, ff, ft)
    patch = dot(have["to_inner"][...], patch).astype(HALF)
    patch_s[...] = patch
    send("patch", patch_s)
    latent = dot(patch, emb[...]).astype(HALF)
    x_s[...] = latent
    send("x", x_s)
    x = latent.astype(FULL)
    gains = have["gains"].at[0]
    wait("wproj", "wup", "wdown", "cot", "out")
    cot = have["cot"]
    gap = jnp.zeros((2, 64), FULL)
    for a in range(6):
        for o in range(12):
            pair = cot[a, o].astype(FULL)
            cots[0, pl.ds(o * 12 + a, 2, stride=6), :] = pair[:, :128]
            cots[1, pl.ds(o * 12 + a, 2, stride=6), :] = jnp.concatenate((gap, pair[:, 128:]), 1)
    qkv, resid = forward_half(x, gains, have["wqkv"], have["wproj"], bias, prob)
    send("prob", prob)
    for n in range(3):
        qkv_s[n] = qkv[n]
    send("qkv", qkv_s)
    resid_s[...] = resid
    send("resid", resid_s)
    unit, spread = normalise(resid)
    normed = (unit * gains[1:2, :]).astype(HALF)
    upward = dot(normed, have["wup"][...])
    below, slope = gelu_parts(upward)
    slope_s[...] = slope.astype(HALF)
    send("slope", slope_s)
    active = (upward * below).astype(HALF)
    result = (resid + dot_nt(active, have["wdown"][...])).astype(HALF)
    last = jnp.concatenate((result[:, 128:], jnp.zeros((CELLS, 64), HALF)), 1)
    last = last + cots[1].astype(HALF)
    both = jnp.concatenate((result[:, :128], cots[0].astype(HALF), last), 0)
    moved = dot(have["out"][...], both).astype(HALF)
    for n in range(4):
        blocks[n] = moved[n * 128 : n * 128 + 128]
        send("block" + str(n), blocks.at[n])
    for copy in sent:
        copy.wait()


def bias_kernel(tbl, bias, table, xs, cols):
    fill_columns(cols)
    table_rows(tbl, 1, table)
    build_bias(table, cols, xs, bias, (flag("section"), flag("lat")))


def stacked(parts, stack):
    pitch = stack.shape[0] // 8
    for n in range(4):
        stack[n * pitch : (n + 1) * pitch, :] = parts[n][0:pitch, :]
    stack[4 * pitch :, :] = parts[4][...]


def second_kernel(*refs):
    parts, rest = refs[:5], refs[5:]
    gains, wqkv, wproj, wup, wdown, bias, into, out_of = rest[:8]
    blocks, stack, prob = rest[8:12], rest[12], rest[13]
    stacked(parts, stack)
    both = dot(into[...], stack[...])
    last = both[2 * CELLS :]
    x = jnp.concatenate((both[:CELLS], last[:, :64]), 1)
    dflat = jnp.concatenate((both[CELLS : 2 * CELLS], last[:, 64:]), 1).astype(HALF)
    gains, wqkv, wproj, wup, wdown = (w.at[1] for w in (gains, wqkv, wproj, wup, wdown))
    qkv, resid = forward_half(x, gains, wqkv, wproj, bias, prob)
    unit, spread = normalise(resid)
    normed = (unit * gains[1:2, :]).astype(HALF)
    upward = dot(normed, wup[...])
    slope = gelu_parts(upward)[1]
    dx = backward(dflat, x, qkv, prob, resid, slope, gains, wqkv, wproj, wup, wdown)
    dx = dx.astype(HALF)
    gap = jnp.zeros((CELLS, 64), HALF)
    left = jnp.concatenate((dx[:, 128:], gap), 1)
    right = jnp.concatenate((gap, dx[:, 128:]), 1)
    moved = dot(out_of[...], jnp.concatenate((dx[:, :128], left, right), 0)).astype(HALF)
    for n in range(4):
        blocks[n][...] = moved[n * 64 : n * 64 + 64]


def third_kernel(*refs):
    parts, rest = refs[:5], refs[5:]
    gains, wqkv, wproj, wup, wdown, patch, x_i, qkv_i, prob, resid, slope, into, out_of = rest[:13]
    grad_o, mine_o, other_o, stack, terms = rest[13:]
    stacked(parts, stack)
    moved = dot(into[...], stack[...])
    last = moved[CELLS : 2 * CELLS, :64] + moved[2 * CELLS :, 64:]
    dflat = jnp.concatenate((moved[:CELLS], last), 1).astype(HALF)
    qkv = tuple(qkv_i[n] for n in range(3))
    gains, wqkv, wproj, wup, wdown = (w.at[0] for w in (gains, wqkv, wproj, wup, wdown))
    dx = backward(
        dflat, x_i[...].astype(FULL), qkv, prob, resid[...], slope[...].astype(FULL),
        gains, wqkv, wproj, wup, wdown,
    )
    grad = dx.astype(HALF)
    total = dot_tn(patch[...], grad)
    terms[0:224, :] = total[:224, :128]
    terms[224:336, :] = jnp.concatenate((total[:112, 128:], total[112:224, 128:]), 1)
    place = lax.axis_index("section") % 2
    mine_o[...] = terms[pl.ds(pl.multiple_of(place * 168, 8), 168), :].astype(HALF)
    other_o[...] = terms[pl.ds(pl.multiple_of(168 - place * 168, 8), 168), :].astype(HALF)
    moved = dot(out_of[...], grad).astype(HALF)
    for z in range(2):
        for a in range(6):
            grad_o[z, a] = moved[(z * 6 + a) * 16 : (z * 6 + a) * 16 + 12]


vmem = pl.BlockSpec(memory_space=pltpu.VMEM)
hbm = pl.BlockSpec(memory_space=pltpu.HBM)


def call(kernel, outs, scratch, *args, spec=vmem, out=vmem, room=30):
    return pl.pallas_call(
        kernel,
        out_shape=outs,
        in_specs=[spec for a in args],
        out_specs=jax.tree.map(lambda _: out, outs),
        scratch_shapes=scratch,
        compiler_params=pltpu.CompilerParams(vmem_limit_bytes=room * 2**20),
        cost_estimate=pl.CostEstimate(flops=1000000, bytes_accessed=1000000, transcendentals=0),
    )(*args)


def shape(dims, dtype=HALF):
    return jax.ShapeDtypeStruct(dims, dtype)


def fetch(block, steps):
    names = ("lon", "lat", "section")
    axes = [name for name in names if steps.get(name, 0)]
    if not axes:
        return block
    sizes = [lax.axis_size(name) for name in axes]
    pairs = []
    for place in np.ndindex(*sizes):
        source = [(p + steps[name]) % n for p, name, n in zip(place, axes, sizes)]
        pairs.append(
            (int(np.ravel_multi_index(source, sizes)), int(np.ravel_multi_index(place, sizes)))
        )
    return lax.ppermute(block, tuple(axes), pairs)


def exchange(blocks, way):
    moved = [fetch(b, {"lat": way * (n // 2), "lon": way * (n % 2)}) for n, b in enumerate(blocks)]
    half = blocks[0].shape[0] // 2
    second = jnp.concatenate([block[half:] for block in moved], 0)
    return (*moved, fetch(second, {"section": way}))


def swap(block, flips):
    names = ("lon", "lat", "section")
    axes = [name for name in names if flips.get(name, 0)]
    sizes = [lax.axis_size(name) for name in axes]
    pairs = []
    for place in np.ndindex(*sizes):
        source = [p ^ flips[name] for p, name in zip(place, axes)]
        pairs.append(
            (int(np.ravel_multi_index(source, sizes)), int(np.ravel_multi_index(place, sizes)))
        )
    return lax.ppermute(block, tuple(axes), pairs)


def add_up(mine, other):
    total = (mine.astype(FULL) + swap(other, {"section": 1}).astype(FULL)).astype(HALF)
    bits = []
    for name in ("section", "lat", "lon"):
        size = lax.axis_size(name)
        if size & (size - 1) or size < 2:
            raise ValueError("axis size")
        bits += [(name, 1 << n) for n in range(name == "section", size.bit_length() - 1)]
    for n in range(0, len(bits), 2):
        pair = [{name: bit} for name, bit in bits[n : n + 2]]
        if len(pair) == 1:
            total = total.astype(FULL) + swap(total, pair[0]).astype(FULL)
        else:
            one, two = pair
            three = dict(one)
            for name, bit in two.items():
                three[name] = three.get(name, 0) | bit
            near, far, last = (swap(total, step).astype(FULL) for step in (one, two, three))
            total = (total.astype(FULL) + near) + (far + last)
        total = total.astype(HALF)
    return total, swap(total, {"section": 1})


def last_kernel(scale, mine, other, upper_o, surface_o, halves, both, sems):
    place = lax.axis_index("section") % 2
    halves[pl.ds(pl.multiple_of(place * 168, 8), 168), :] = mine[...].astype(FULL) * scale
    halves[pl.ds(pl.multiple_of(168 - place * 168, 8), 168), :] = other[...].astype(FULL) * scale
    both[:, 0:128] = halves[0:224, :]
    last = halves[224:336, :]
    both[0:112, 128:192] = last[:, :64]
    both[112:224, 128:192] = last[:, 64:]
    copies = [
        pltpu.make_async_copy(both.at[pl.ds(0, 160)], upper_o, sems.at[0]),
        pltpu.make_async_copy(both.at[pl.ds(160, 64)], surface_o, sems.at[1]),
    ]
    for copy in copies:
        copy.start()
    for copy in copies:
        copy.wait()


def on_device(
    upper_fields,
    surface_fields,
    upper_embed,
    surface_embed,
    norm_gains,
    qkv_weight,
    proj_weight,
    up_weight,
    down_weight,
    earth_bias,
    out_grad,
):
    sections, bands = lax.axis_size("section"), lax.axis_size("lat")
    levels, rows, columns, width = out_grad.shape
    positions = earth_bias.shape[-1]
    table = earth_bias.transpose(0, 1, 3, 2, 4).reshape(2 * HEADS, 1, positions)
    weights = (norm_gains, qkv_weight, proj_weight, up_weight, down_weight.transpose(0, 2, 1))
    operands = (
        table, upper_fields, surface_fields, jnp.asarray(natural_to_inner()), upper_embed,
        surface_embed, *weights, out_grad.transpose(1, 2, 0, 3), jnp.asarray(pair_out()),
    )
    local = [
        pltpu.VMEM(v.shape[1:] if 7 <= n < 11 else v.shape, v.dtype) for n, v in enumerate(operands)
    ]
    local[0] = pltpu.VMEM((HEADS, 1, positions), FULL)
    local[4] = local[5] = pltpu.VMEM((16, 128), HALF)
    scratch_bias = [pltpu.VMEM((8, 3328), FULL), pltpu.VMEM((4, CELLS, 128), FULL)]
    scratch_cols = pltpu.VMEM((2, 256, 384), HALF)
    held = [
        shape((CELLS, 256)),
        shape((CELLS, WIDTH)),
        shape((3, CELLS, WIDTH)),
        shape((HEADS * CELLS, CELLS)),
        shape((CELLS, WIDTH), FULL),
        shape((CELLS, 4 * WIDTH)),
    ]
    patch, x, qkv, prob, resid, slope, *blocks = call(
        first_kernel,
        held + [shape((128, 128))] * 4,
        local
        + [pltpu.VMEM(v.shape, v.dtype) for v in held]
        + [
            pltpu.VMEM((4, 128, 128), HALF),
            pltpu.VMEM((576, 128), FULL),
            pltpu.VMEM((288, 128), FULL),
            pltpu.VMEM((256, WIDTH), HALF),
            pltpu.VMEM((2, CELLS, 128), FULL),
        ]
        + scratch_bias
        + [
            pltpu.VMEM((HEADS * CELLS, CELLS), FULL),
            scratch_cols,
            pltpu.VMEM((512, 512), HALF),
            pltpu.SemaphoreType.DMA((len(operands) + 10,)),
        ],
        *operands,
        spec=hbm,
        out=hbm,
        room=60,
    )
    bias = call(
        bias_kernel, shape((HEADS * CELLS, CELLS), FULL), [*scratch_bias, scratch_cols], table
    )
    blocks = call(
        second_kernel,
        [shape((64, 128))] * 4,
        [pltpu.VMEM((512, 128), HALF), pltpu.VMEM((HEADS * CELLS, CELLS), HALF)],
        *exchange(blocks, 1), *weights, bias,
        jnp.asarray(pair_in()), jnp.asarray(single_out()),
    )
    latent_grad, mine, other = call(
        third_kernel,
        [shape((2, 6, 12, WIDTH)), shape((168, 128)), shape((168, 128))],
        [pltpu.VMEM((256, 128), HALF), pltpu.VMEM((336, 128), FULL)],
        *exchange(blocks, -1), *weights, patch, x, qkv, prob, resid, slope,
        jnp.asarray(single_in()), jnp.asarray(inner_to_padded()),
    )
    scale = float(levels * sections * rows * bands * columns * lax.axis_size("lon")) ** (-0.5)
    upper_grad, surface_grad = call(
        functools.partial(last_kernel, scale),
        [shape((160, WIDTH), FULL), shape((64, WIDTH), FULL)],
        [
            pltpu.VMEM((336, 128), FULL),
            pltpu.VMEM((224, WIDTH), FULL),
            pltpu.SemaphoreType.DMA((2,)),
        ],
        *add_up(mine, other),
        out=hbm,
    )
    return (latent_grad, upper_grad, surface_grad)


def solution(mesh):
    placed = (
        P(None, None, "lat", "lon"),
        P(None, "lat", "lon"),
        P(),
        P(),
        P(),
        P(),
        P(),
        P(),
        P(),
        P(None, "lat", "section", None, None),
        P("section", "lat", "lon", None),
    )
    return jax.shard_map(
        on_device,
        mesh=mesh,
        in_specs=placed,
        out_specs=(P("section", "lat", "lon", None), P(), P()),
        check_vma=False,
    )
```

```python
import functools

import jax
import jax.numpy as jnp
import ml_dtypes
import numpy as np
from jax import lax
from jax.experimental import pallas as pl
from jax.experimental.pallas import tpu as pltpu
from jax.sharding import PartitionSpec as P

neg_fill = -1e30
norm_eps = 1e-05
HEADS = 6
HEAD = 32
CELLS = 144
WIDTH = 192
FULL = jnp.float32
HALF = jnp.bfloat16


def inner_row(z, a, o):
    return o * 12 + z * 6 + a


def octant_of(z, a, o):
    return (z * 4 + (a // 3) * 2 + o // 6, (a % 3) * 6 + o % 6)


def as_half(array):
    return array.astype(ml_dtypes.bfloat16)


def cells():
    return [(z, a, o) for z in range(2) for a in range(6) for o in range(12)]


def natural_to_inner():
    move = np.zeros((CELLS, CELLS), np.float32)
    for z, a, o in cells():
        move[inner_row(z, a, o), (z * 6 + a) * 12 + o] = 1
    return as_half(move)


def inner_to_padded():
    move = np.zeros((192, CELLS), np.float32)
    for z, a, o in cells():
        move[(z * 6 + a) * 16 + o, inner_row(z, a, o)] = 1
    return as_half(move)


def octants_out(pitch, first, flip, source):
    move = np.zeros((8 * pitch, CELLS), np.float32)
    for z, a, o in cells():
        part, place = octant_of(z, a, o)
        part = 7 - part if flip else part
        move[(part % 4 * 2 + part // 4) * pitch + first + place, source(z, a, o)] = 1
    return as_half(move)


def octants_in(pitch, first, flip):
    move = np.zeros((CELLS, 8 * pitch), np.float32)
    for z, a, o in cells():
        part, place = octant_of(z, a, o)
        part = 7 - part if flip else part
        move[inner_row(z, a, o), part * pitch + first + place] = 1
    return as_half(move)


def whole_part(v, size):
    return jnp.floor((v + 0.5) * (1.0 / size))


def one_hot(target, lanes):
    lane = lax.broadcasted_iota(jnp.int32, (1, lanes), 1).astype(FULL)
    return jnp.where(lane == target, 1.0, 0.0).astype(HALF)


def fill_columns(cols):
    row = lax.broadcasted_iota(jnp.int32, (256, 1), 0).astype(FULL)
    a = whole_part(row, 23)
    k = row - 23.0 * a
    for z in range(2):
        target = (22.0 - k) * 12.0 + (z * 6.0) + a
        cols[z] = one_hot(jnp.where(row < 138.0, target, -1.0), 384)


def fill_select(select):
    row = lax.broadcasted_iota(jnp.int32, (128, 1), 0).astype(FULL)
    b = whole_part(row, 32)
    slot = row - 32.0 * b
    layer = whole_part(slot, 5)
    z = whole_part(layer, 2)
    upper = z * 256.0 + (slot - 5.0 * layer) * 32.0 + (layer - 2.0 * z) * 16.0
    surface = 160.0 + (slot - 20.0) * 16.0
    target = jnp.where(slot < 20.0, upper, surface) + b * 4.0
    for c in range(4):
        select[c * 128 : c * 128 + 128, :] = one_hot(
            jnp.where(slot < 24.0, target + float(c), -1.0), 512
        )


def dot(a, b):
    return jnp.dot(a, b, preferred_element_type=FULL)


def dot_nt(a, b):
    return lax.dot_general(a, b, (((1,), (1,)), ((), ())), preferred_element_type=FULL)


def dot_tn(a, b):
    return lax.dot_general(a, b, (((0,), (0,)), ((), ())), preferred_element_type=FULL)


def normalise(v):
    mean = jnp.mean(v, -1, keepdims=True)
    centred = v - mean
    spread = lax.rsqrt(jnp.mean(centred * centred, -1, keepdims=True) + norm_eps)
    return centred * spread, spread


def normalise_back(dy, unit, spread, gain):
    dunit = dy * gain
    inner = jnp.mean(dunit * unit, -1, keepdims=True)
    return spread * (dunit - jnp.mean(dunit, -1, keepdims=True) - unit * inner)


def head_lanes(h):
    lane = lax.broadcasted_iota(jnp.int32, (1, WIDTH), 1)
    return (lane >= h * HEAD) & (lane < (h + 1) * HEAD)


def head_mask(h):
    return jnp.where(head_lanes(h), 1.0, 0.0).astype(HALF)


def build_bias(tbl, cols, xs, bias, edges):
    for z in range(2):
        for a in range(6):
            for zu in range(2):
                start = ((z * 2 + zu) * 6 + a) * 138
                piece = tbl[0:HEADS, start : start + 138]
                piece = jnp.concatenate((piece, jnp.zeros((HEADS, 118), FULL)), 1)
                for p in range(2):
                    for half in range(2):
                        xs[zu * 2 + half, pl.ds(p * 12 + z * 6 + a, HEADS, stride=24), :] = piece[
                            :, half * 128 : half * 128 + 128
                        ]
    total = None
    for zu in range(2):
        x = jnp.concatenate((xs[zu * 2], xs[zu * 2 + 1]), 1)
        high = x.astype(HALF)
        left = x - high.astype(FULL)
        mid = left.astype(HALF)
        low = (left - mid.astype(FULL)).astype(HALF)
        term = dot(jnp.concatenate((high, mid, low), 0), cols[zu])
        total = term if total is None else total + term
    table = total[:CELLS] + total[CELLS : 2 * CELLS] + total[2 * CELLS :]
    row = lax.broadcasted_iota(jnp.int32, (CELLS, 1), 0).astype(FULL)
    lane = lax.broadcasted_iota(jnp.int32, (1, CELLS), 1).astype(FULL)

    part = whole_part
    even = part(row, 12) - 2.0 * part(part(row, 12), 2) == 0.0
    table = jnp.where(even, pltpu.roll(table, 384 - 12, 1), table)
    if edges is not None:
        last_section, last_band = edges
        row12, lane12 = row - 12.0 * part(row, 12), lane - 12.0 * part(lane, 12)
        row_z, lane_z = part(row12, 6), part(lane12, 6)
        row_a, lane_a = part(row12 - 6.0 * row_z, 3), part(lane12 - 6.0 * lane_z, 3)
        apart = jnp.abs(row_z - lane_z) * last_section + jnp.abs(row_a - lane_a) * last_band
        blocked = apart > 0.5
    for j in range(6):
        shift = (10 - 2 * j) * 12
        moved = pltpu.roll(table, 384 - shift, 1) if shift else table
        moved = moved[:, :CELLS]
        if edges is not None:
            moved = jnp.where(blocked, neg_fill, moved)
        for h in range(HEADS):
            bias[h * CELLS + j * 24 : h * CELLS + j * 24 + 24, :] = moved[h * 24 : h * 24 + 24, :]


def attend(q, k, v, bias, prob):
    mixed = jnp.zeros((CELLS, WIDTH), FULL)
    for h in range(HEADS):
        rows = slice(h * CELLS, (h + 1) * CELLS)
        score = dot_nt(q * head_mask(h), k) * HEAD ** (-0.5) + bias[rows, :]
        expo = jnp.exp(score - jnp.max(score, -1, keepdims=True))
        weights = (expo * (1.0 / jnp.sum(expo, -1, keepdims=True))).astype(HALF)
        prob[rows, :] = weights
        mixed = jnp.where(head_lanes(h), dot(weights, v), mixed)
    return mixed.astype(HALF)


def attend_back(dmixed, q, k, v, prob):
    dq = jnp.zeros((CELLS, WIDTH), FULL)
    dk = jnp.zeros((CELLS, WIDTH), FULL)
    dv = jnp.zeros((CELLS, WIDTH), FULL)
    for h in range(HEADS):
        rows = slice(h * CELLS, (h + 1) * CELLS)
        weights = prob[rows, :]
        dhead = dmixed * head_mask(h)
        full = weights.astype(FULL)
        dweights = dot_nt(dhead, v)
        inner = jnp.sum(dweights * full, -1, keepdims=True)
        dscore = (full * (dweights - inner) * HEAD ** (-0.5)).astype(HALF)
        dv = dv + dot_tn(weights, dhead)
        dq = jnp.where(head_lanes(h), dot(dscore, k), dq)
        dk = dk + dot_tn(dscore, q * head_mask(h))
    return dq.astype(HALF), dk.astype(HALF), dv.astype(HALF)


def gelu_parts(u):
    below = 0.5 * (1.0 + lax.erf(u * (0.5**0.5)))
    slope = below + u * (jnp.exp(-0.5 * u * u) * (2.0 * np.pi) ** (-0.5))
    return below, slope


def forward_half(x, gains, wqkv, wproj, bias, prob):
    unit, spread = normalise(x)
    hidden = (unit * gains[0:1, :]).astype(HALF)
    qkv = dot(hidden, wqkv[...]).astype(HALF)
    q, k, v = (qkv[:, n * WIDTH : (n + 1) * WIDTH] for n in range(3))
    mixed = attend(q, k, v, bias, prob)
    return (q, k, v), x + dot(mixed, wproj[...])


def backward(dflat, x, qkv, prob, resid, slope, gains, wqkv, wproj, wup, wdown):
    q, k, v = qkv
    dactive = dot(dflat, wdown[...])
    dupward = (dactive * slope).astype(HALF)
    dnormed = dot_nt(dupward, wup[...])
    unit, spread = normalise(resid)
    dresid = dflat.astype(FULL) + normalise_back(dnormed, unit, spread, gains[1:2, :])
    dmixed = dot_nt(dresid.astype(HALF), wproj[...]).astype(HALF)
    dq, dk, dv = attend_back(dmixed, q, k, v, prob)
    dhidden = dot_nt(dq, wqkv[:, :WIDTH])
    dhidden = dhidden + dot_nt(dk, wqkv[:, WIDTH : 2 * WIDTH])
    dhidden = dhidden + dot_nt(dv, wqkv[:, 2 * WIDTH :])
    unit, spread = normalise(x)
    return dresid + normalise_back(dhidden, unit, spread, gains[0:1, :])


def gather_patches(upper, surface, section, select, ff, ft):
    base = 4 * section - 2
    for z in range(2):
        for a in range(2):
            level = jnp.maximum(base + 2 * z + a, 0)
            for v in range(5):
                field = upper[v, level].astype(FULL)
                if z == 0:
                    field = jnp.where(section == 0, 0.0, field)
                slot = (z * 2 + a) * 5 + v
                ff[slot * 24 : slot * 24 + 24, 0:48] = field
    for v in range(4):
        field = jnp.where(section == 0, surface[v].astype(FULL), 0.0)
        ff[(20 + v) * 24 : (21 + v) * 24, 0:48] = field
    pad = jnp.zeros((8, 128), FULL)
    for i in range(6):
        pieces = []
        for b in range(4):
            pieces += [ff[pl.ds(4 * i + b, 24, stride=24), :], pad]
        ft[i * 48 : i * 48 + 48, :] = jnp.concatenate(pieces, 0).T[:48]
    raw = [ft[pl.ds(c, 72, stride=4), :].astype(HALF) for c in range(4)]
    both = dot(jnp.concatenate(raw, 1), select[...])
    return jnp.concatenate((both[:, :256], both[:, 256:]), 0).astype(HALF)


def flag(axis):
    last = lax.axis_index(axis) == lax.axis_size(axis) - 1
    return jnp.where(last, 1.0, 0.0)


def table_rows(tbl, block, table):
    for h in range(HEADS):
        table[h : h + 1, 0 : tbl.shape[-1]] = tbl[block * HEADS + h]


def first_kernel(*refs):
    names = (
        "tbl", "upper", "surface", "to_inner", "uembed", "sembed", "gains",
        "wqkv", "wproj", "wup", "wdown", "cot", "out_first", "out_cot",
    )
    count = len(names)
    source, refs = refs[:count], refs[count:]
    results = ("patch", "x", "qkv", "prob", "resid", "slope", "keep", "give", "one", "two", "three")
    target, refs = refs[: len(results)], refs[len(results) :]
    local, refs = refs[:count], refs[count:]
    patch_s, x_s, qkv_s, prob, resid_s, slope_s, blocks = refs[:7]
    ff, ft, emb, cots, table, xs, bias, cols, select, sems = refs[7:]
    copies = {}
    for n, name in enumerate(names):
        start, end = source[n], local[n]
        if name[0] == "w":
            start = start.at[0]
        elif name == "tbl":
            start = start.at[pl.ds(0, HEADS)]
        elif name == "uembed":
            end = emb.at[pl.ds(0, 160)]
        elif name == "sembed":
            end = emb.at[pl.ds(160, 64)]
        copies[name] = pltpu.make_async_copy(start, end, sems.at[n])
        copies[name].start()
    have = dict(zip(names, local))
    sent = []

    def wait(*which):
        for name in which:
            copies[name].wait()

    def send(name, held):
        n = results.index(name)
        sent.append(pltpu.make_async_copy(held, target[n], sems.at[len(names) + n]))
        sent[-1].start()

    emb[224:256, :] = jnp.zeros((32, WIDTH), HALF)
    fill_columns(cols)
    fill_select(select)
    wait("tbl")
    table_rows(have["tbl"], 0, table)
    build_bias(table, cols, xs, bias, None)
    wait("upper", "surface", "to_inner", "uembed", "sembed", "gains", "wqkv")
    section = lax.axis_index("section")
    patch = gather_patches(have["upper"], have["surface"], section, select, ff, ft)
    patch = dot(have["to_inner"][...], patch).astype(HALF)
    patch_s[...] = patch
    send("patch", patch_s)
    latent = dot(patch, emb[...]).astype(HALF)
    x_s[...] = latent
    send("x", x_s)
    x = latent.astype(FULL)
    gains = have["gains"].at[0]
    wait("wproj", "wup", "wdown", "cot", "out_first", "out_cot")
    cot = have["cot"]
    for a in range(6):
        for o in range(12):
            cots[(a * 12 + o) * 2 : (a * 12 + o) * 2 + 2, :] = cot[a, o].astype(FULL)
    ready = dot(have["out_cot"][...], cots[...].astype(HALF))
    qkv, resid = forward_half(x, gains, have["wqkv"], have["wproj"], bias, prob)
    send("prob", prob)
    for n in range(3):
        qkv_s[n] = qkv[n]
    send("qkv", qkv_s)
    resid_s[...] = resid
    send("resid", resid_s)
    unit, spread = normalise(resid)
    normed = (unit * gains[1:2, :]).astype(HALF)
    upward = dot(normed, have["wup"][...])
    below, slope = gelu_parts(upward)
    slope_s[...] = slope.astype(HALF)
    send("slope", slope_s)
    active = (upward * below).astype(HALF)
    result = (resid + dot_nt(active, have["wdown"][...])).astype(HALF)
    blocks[...] = (dot(have["out_first"][...], result) + ready).astype(HALF)
    for name, first, count in (("give", 48, 48), ("one", 96, 96), ("two", 192, 96), ("three", 288, 96), ("keep", 0, 48)):
        send(name, blocks.at[pl.ds(first, count)])
    for copy in sent:
        copy.wait()


def bias_kernel(tbl, bias, done, table, xs, cols):
    done[...] = jnp.zeros_like(done)
    fill_columns(cols)
    table_rows(tbl, 1, table)
    build_bias(table, cols, xs, bias, (flag("section"), flag("lat")))


def stacked(parts, stack):
    keep, one, two, three, own, others = parts
    pitch = keep.shape[0]
    for n, part in enumerate((keep, one, two, three, own)):
        stack[n * pitch : (n + 1) * pitch, :] = part[0:pitch, :]
    stack[5 * pitch :, :] = others[...]


def second_kernel(*refs):
    parts, rest = refs[:6], refs[6:]
    gains, wqkv, wproj, wup, wdown, bias, into, out_of = rest[:8]
    keep, give, one, two, three, stack, prob = rest[8:]
    stacked(parts, stack)
    both = dot(into[...], stack[...])
    x, dflat = both[:CELLS], both[CELLS:].astype(HALF)
    gains, wqkv, wproj, wup, wdown = (w.at[1] for w in (gains, wqkv, wproj, wup, wdown))
    qkv, resid = forward_half(x, gains, wqkv, wproj, bias, prob)
    unit, spread = normalise(resid)
    normed = (unit * gains[1:2, :]).astype(HALF)
    upward = dot(normed, wup[...])
    slope = gelu_parts(upward)[1]
    dx = backward(dflat, x, qkv, prob, resid, slope, gains, wqkv, wproj, wup, wdown)
    moved = dot(out_of[...], dx.astype(HALF)).astype(HALF)
    keep[...] = moved[:32]
    give[...] = moved[32:64]
    for n, block in enumerate((one, two, three)):
        block[...] = moved[n * 64 + 64 : n * 64 + 128]


def third_kernel(*refs):
    parts, rest = refs[:6], refs[6:]
    gains, wqkv, wproj, wup, wdown, patch, x_i, qkv_i, prob, resid, slope, into, out_of = rest[:13]
    grad_o, terms_o, stack = rest[13:]
    stacked(parts, stack)
    dflat = dot(into[...], stack[...]).astype(HALF)
    qkv = tuple(qkv_i[n] for n in range(3))
    gains, wqkv, wproj, wup, wdown = (w.at[0] for w in (gains, wqkv, wproj, wup, wdown))
    dx = backward(
        dflat, x_i[...].astype(FULL), qkv, prob, resid[...], slope[...].astype(FULL),
        gains, wqkv, wproj, wup, wdown,
    )
    grad = dx.astype(HALF)
    total = dot_tn(patch[...], grad)
    terms_o[0:224, :] = total[:224, :128].astype(HALF)
    last = jnp.concatenate((total[:112, 128:], total[112:224, 128:]), 1)
    terms_o[224:336, :] = last.astype(HALF)
    moved = dot(out_of[...], grad).astype(HALF)
    for z in range(2):
        for a in range(6):
            grad_o[z, a] = moved[(z * 6 + a) * 16 : (z * 6 + a) * 16 + 12]


vmem = pl.BlockSpec(memory_space=pltpu.VMEM)
hbm = pl.BlockSpec(memory_space=pltpu.HBM)


def call(kernel, outs, scratch, *args, spec=vmem, out=vmem, room=30):
    return pl.pallas_call(
        kernel,
        out_shape=outs,
        in_specs=[spec for a in args],
        out_specs=jax.tree.map(lambda _: out, outs),
        scratch_shapes=scratch,
        compiler_params=pltpu.CompilerParams(vmem_limit_bytes=room * 2**20),
        cost_estimate=pl.CostEstimate(flops=1000000, bytes_accessed=1000000, transcendentals=0),
    )(*args)


def shape(dims, dtype=HALF):
    return jax.ShapeDtypeStruct(dims, dtype)


def fetch(block, steps):
    names = ("lon", "lat", "section")
    axes = [name for name in names if steps.get(name, 0)]
    if not axes:
        return block
    sizes = [lax.axis_size(name) for name in axes]
    pairs = []
    for place in np.ndindex(*sizes):
        source = [(p + steps[name]) % n for p, name, n in zip(place, axes, sizes)]
        pairs.append(
            (int(np.ravel_multi_index(source, sizes)), int(np.ravel_multi_index(place, sizes)))
        )
    return lax.ppermute(block, tuple(axes), pairs)


def exchange(keep, give, others, way, wait=None):
    own = fetch(give, {"section": way})
    moved = [
        fetch(b, {"lat": way * (n // 2), "lon": way * (n % 2)}) for n, b in enumerate(others, 1)
    ]
    second = jnp.concatenate([block[keep.shape[0] :] for block in moved], 0)
    if wait is not None:
        second = second + wait[0, 0].astype(HALF)
    return (keep, *moved, own, fetch(second, {"section": way}))


def swap(block, flips):
    axes = ("lon", "lat", "section")
    sizes = [lax.axis_size(name) for name in axes]
    pairs = []
    for place in np.ndindex(*sizes):
        source = [p ^ flips.get(name, 0) for p, name in zip(place, axes)]
        if place[2] % 2:
            pairs.append(
                (int(np.ravel_multi_index(source, sizes)), int(np.ravel_multi_index(place, sizes)))
            )
    return lax.ppermute(block, axes, pairs)


def add_up(terms):
    total = (terms.astype(FULL) + swap(terms, {"section": 1}).astype(FULL)).astype(HALF)
    bits = []
    for name in ("section", "lat", "lon"):
        size = lax.axis_size(name)
        if size & (size - 1) or size < 2:
            raise ValueError("axis size")
        bits += [(name, 1 << n) for n in range(name == "section", size.bit_length() - 1)]
    for n in range(0, len(bits), 2):
        pair = [{name: bit} for name, bit in bits[n : n + 2]]
        if len(pair) == 1:
            total = total.astype(FULL) + swap(total, pair[0]).astype(FULL)
        else:
            one, two = pair
            three = dict(one)
            for name, bit in two.items():
                three[name] = three.get(name, 0) | bit
            near, far, last = (swap(total, step).astype(FULL) for step in (one, two, three))
            total = (total.astype(FULL) + near) + (far + last)
        total = total.astype(HALF)
    sections = range(0, lax.axis_size("section"), 2)
    return total, lax.ppermute(total, "section", [(i + 1, i) for i in sections])


def last_kernel(scale, own, given, upper_o, surface_o, both, sems):
    odd = lax.axis_index("section") % 2 == 1
    total = jnp.where(odd, own[...].astype(FULL), given[...].astype(FULL)) * scale
    both[:, 0:128] = total[:224]
    both[0:112, 128:192] = total[224:, :64]
    both[112:224, 128:192] = total[224:, 64:]
    copies = [
        pltpu.make_async_copy(both.at[pl.ds(0, 160)], upper_o, sems.at[0]),
        pltpu.make_async_copy(both.at[pl.ds(160, 64)], surface_o, sems.at[1]),
    ]
    for copy in copies:
        copy.start()
    for copy in copies:
        copy.wait()


def on_device(
    upper_fields,
    surface_fields,
    upper_embed,
    surface_embed,
    norm_gains,
    qkv_weight,
    proj_weight,
    up_weight,
    down_weight,
    earth_bias,
    out_grad,
):
    sections, bands = lax.axis_size("section"), lax.axis_size("lat")
    levels, rows, columns, width = out_grad.shape
    positions = earth_bias.shape[-1]
    table = earth_bias.transpose(0, 1, 3, 2, 4).reshape(2 * HEADS, 1, positions)
    weights = (norm_gains, qkv_weight, proj_weight, up_weight, down_weight.transpose(0, 2, 1))
    def from_cot(z, a, o):
        return (a * 12 + o) * 2 + z

    operands = (
        table, upper_fields, surface_fields, jnp.asarray(natural_to_inner()), upper_embed,
        surface_embed, *weights, out_grad.transpose(1, 2, 0, 3),
        jnp.asarray(octants_out(48, 0, True, inner_row)),
        jnp.asarray(octants_out(48, 18, True, from_cot)),
    )
    local = [
        pltpu.VMEM(v.shape[1:] if 7 <= n < 11 else v.shape, v.dtype) for n, v in enumerate(operands)
    ]
    local[0] = pltpu.VMEM((HEADS, 1, positions), FULL)
    local[4] = local[5] = pltpu.VMEM((16, 128), HALF)
    scratch_bias = [pltpu.VMEM((8, 3328), FULL), pltpu.VMEM((4, CELLS, 128), FULL)]
    scratch_cols = pltpu.VMEM((2, 256, 384), HALF)
    held = [
        shape((CELLS, 256)),
        shape((CELLS, WIDTH)),
        shape((3, CELLS, WIDTH)),
        shape((HEADS * CELLS, CELLS)),
        shape((CELLS, WIDTH), FULL),
        shape((CELLS, 4 * WIDTH)),
    ]
    patch, x, qkv, prob, resid, slope, keep, give, *others = call(
        first_kernel,
        held + [shape((48, WIDTH))] * 2 + [shape((96, WIDTH))] * 3,
        local
        + [pltpu.VMEM(v.shape, v.dtype) for v in held]
        + [
            pltpu.VMEM((384, WIDTH), HALF),
            pltpu.VMEM((576, 128), FULL),
            pltpu.VMEM((288, 128), FULL),
            pltpu.VMEM((256, WIDTH), HALF),
            pltpu.VMEM((CELLS, WIDTH), FULL),
        ]
        + scratch_bias
        + [
            pltpu.VMEM((HEADS * CELLS, CELLS), FULL),
            scratch_cols,
            pltpu.VMEM((512, 512), HALF),
            pltpu.SemaphoreType.DMA((len(operands) + 11,)),
        ],
        *operands,
        spec=hbm,
        out=hbm,
        room=60,
    )
    bias, done = call(
        bias_kernel,
        [shape((HEADS * CELLS, CELLS), FULL), shape((8, 128), FULL)],
        [*scratch_bias, scratch_cols],
        table,
    )
    into = np.concatenate((octants_in(48, 0, False), octants_in(48, 18, False)), 0)
    keep, give, *others = call(
        second_kernel,
        [shape((32, WIDTH))] * 2 + [shape((64, WIDTH))] * 3,
        [pltpu.VMEM((384, WIDTH), HALF), pltpu.VMEM((HEADS * CELLS, CELLS), HALF)],
        *exchange(keep, give, others, 1, done), *weights, bias,
        jnp.asarray(into), jnp.asarray(octants_out(32, 0, False, inner_row)),
    )
    latent_grad, terms = call(
        third_kernel,
        [shape((2, 6, 12, WIDTH)), shape((336, 128))],
        [pltpu.VMEM((256, WIDTH), HALF)],
        *exchange(keep, give, others, -1), *weights, patch, x, qkv, prob, resid, slope,
        jnp.asarray(octants_in(32, 0, True)), jnp.asarray(inner_to_padded()),
    )
    scale = float(levels * sections * rows * bands * columns * lax.axis_size("lon")) ** (-0.5)
    upper_grad, surface_grad = call(
        functools.partial(last_kernel, scale),
        [shape((160, WIDTH), FULL), shape((64, WIDTH), FULL)],
        [
            pltpu.VMEM((224, WIDTH), FULL),
            pltpu.SemaphoreType.DMA((2,)),
        ],
        *add_up(terms),
        out=hbm,
    )
    return (latent_grad, upper_grad, surface_grad)


def solution(mesh):
    placed = (
        P(None, None, "lat", "lon"),
        P(None, "lat", "lon"),
        P(),
        P(),
        P(),
        P(),
        P(),
        P(),
        P(),
        P(None, "lat", "section", None, None),
        P("section", "lat", "lon", None),
    )
    return jax.shard_map(
        on_device,
        mesh=mesh,
        in_specs=placed,
        out_specs=(P("section", "lat", "lon", None), P(), P()),
        check_vma=False,
    )
```

```python
import functools

import jax
import jax.numpy as jnp
import ml_dtypes
import numpy as np
from jax import lax
from jax.experimental import pallas as pl
from jax.experimental.pallas import tpu as pltpu
from jax.sharding import PartitionSpec as P

neg_fill = -1e30
norm_eps = 1e-05
HEADS = 6
HEAD = 32
CELLS = 144
WIDTH = 192
FULL = jnp.float32
HALF = jnp.bfloat16


def inner_row(z, a, o):
    return o * 12 + z * 6 + a


def octant_of(z, a, o):
    return (z * 4 + (a // 3) * 2 + o // 6, (a % 3) * 6 + o % 6)


def as_half(array):
    return array.astype(ml_dtypes.bfloat16)


def cells():
    return [(z, a, o) for z in range(2) for a in range(6) for o in range(12)]


def natural_to_inner():
    move = np.zeros((CELLS, CELLS), np.float32)
    for z, a, o in cells():
        move[inner_row(z, a, o), (z * 6 + a) * 12 + o] = 1
    return as_half(move)


def inner_to_padded():
    move = np.zeros((192, CELLS), np.float32)
    for z, a, o in cells():
        move[(z * 6 + a) * 16 + o, inner_row(z, a, o)] = 1
    return as_half(move)


def octants_out(pitch, first, flip, source):
    move = np.zeros((8 * pitch, CELLS), np.float32)
    for z, a, o in cells():
        part, place = octant_of(z, a, o)
        move[(7 - part if flip else part) * pitch + first + place, source(z, a, o)] = 1
    return as_half(move)


def octants_in(pitch, first, flip):
    move = np.zeros((CELLS, 8 * pitch), np.float32)
    for z, a, o in cells():
        part, place = octant_of(z, a, o)
        part = 7 - part if flip else part
        block = (part % 4) * 2 + part // 4
        move[inner_row(z, a, o), block * pitch + first + place] = 1
    return as_half(move)


def whole_part(v, size):
    return jnp.floor((v + 0.5) * (1.0 / size))


def one_hot(target, lanes):
    lane = lax.broadcasted_iota(jnp.int32, (1, lanes), 1).astype(FULL)
    return jnp.where(lane == target, 1.0, 0.0).astype(HALF)


def fill_columns(cols):
    row = lax.broadcasted_iota(jnp.int32, (256, 1), 0).astype(FULL)
    a = whole_part(row, 23)
    k = row - 23.0 * a
    for z in range(2):
        target = (22.0 - k) * 12.0 + (z * 6.0) + a
        cols[z] = one_hot(jnp.where(row < 138.0, target, -1.0), 384)


def fill_select(select):
    row = lax.broadcasted_iota(jnp.int32, (128, 1), 0).astype(FULL)
    b = whole_part(row, 32)
    slot = row - 32.0 * b
    layer = whole_part(slot, 5)
    z = whole_part(layer, 2)
    upper = z * 256.0 + (slot - 5.0 * layer) * 32.0 + (layer - 2.0 * z) * 16.0
    surface = 160.0 + (slot - 20.0) * 16.0
    target = jnp.where(slot < 20.0, upper, surface) + b * 4.0
    for c in range(4):
        select[c * 128 : c * 128 + 128, :] = one_hot(
            jnp.where(slot < 24.0, target + float(c), -1.0), 512
        )


def dot(a, b):
    return jnp.dot(a, b, preferred_element_type=FULL)


def dot_nt(a, b):
    return lax.dot_general(a, b, (((1,), (1,)), ((), ())), preferred_element_type=FULL)


def dot_tn(a, b):
    return lax.dot_general(a, b, (((0,), (0,)), ((), ())), preferred_element_type=FULL)


def normalise(v):
    mean = jnp.mean(v, -1, keepdims=True)
    centred = v - mean
    spread = lax.rsqrt(jnp.mean(centred * centred, -1, keepdims=True) + norm_eps)
    return centred * spread, spread


def normalise_back(dy, unit, spread, gain):
    dunit = dy * gain
    inner = jnp.mean(dunit * unit, -1, keepdims=True)
    return spread * (dunit - jnp.mean(dunit, -1, keepdims=True) - unit * inner)


def head_lanes(h):
    lane = lax.broadcasted_iota(jnp.int32, (1, WIDTH), 1)
    return (lane >= h * HEAD) & (lane < (h + 1) * HEAD)


def head_mask(h):
    return jnp.where(head_lanes(h), 1.0, 0.0).astype(HALF)


def build_bias(tbl, cols, xs, bias, edges):
    for z in range(2):
        for a in range(6):
            for zu in range(2):
                start = ((z * 2 + zu) * 6 + a) * 138
                piece = tbl[0:HEADS, start : start + 138]
                piece = jnp.concatenate((piece, jnp.zeros((HEADS, 118), FULL)), 1)
                for p in range(2):
                    for half in range(2):
                        xs[zu * 2 + half, pl.ds(p * 12 + z * 6 + a, HEADS, stride=24), :] = piece[
                            :, half * 128 : half * 128 + 128
                        ]
    total = None
    for zu in range(2):
        x = jnp.concatenate((xs[zu * 2], xs[zu * 2 + 1]), 1)
        high = x.astype(HALF)
        left = x - high.astype(FULL)
        mid = left.astype(HALF)
        low = (left - mid.astype(FULL)).astype(HALF)
        term = dot(jnp.concatenate((high, mid, low), 0), cols[zu])
        total = term if total is None else total + term
    table = total[:CELLS] + total[CELLS : 2 * CELLS] + total[2 * CELLS :]
    row = lax.broadcasted_iota(jnp.int32, (CELLS, 1), 0).astype(FULL)
    lane = lax.broadcasted_iota(jnp.int32, (1, CELLS), 1).astype(FULL)

    part = whole_part
    even = part(row, 12) - 2.0 * part(part(row, 12), 2) == 0.0
    table = jnp.where(even, pltpu.roll(table, 384 - 12, 1), table)
    if edges is not None:
        last_section, last_band = edges
        row12, lane12 = row - 12.0 * part(row, 12), lane - 12.0 * part(lane, 12)
        row_z, lane_z = part(row12, 6), part(lane12, 6)
        row_a, lane_a = part(row12 - 6.0 * row_z, 3), part(lane12 - 6.0 * lane_z, 3)
        apart = jnp.abs(row_z - lane_z) * last_section + jnp.abs(row_a - lane_a) * last_band
        blocked = apart > 0.5
    for j in range(6):
        shift = (10 - 2 * j) * 12
        moved = pltpu.roll(table, 384 - shift, 1) if shift else table
        moved = moved[:, :CELLS]
        if edges is not None:
            moved = jnp.where(blocked, neg_fill, moved)
        for h in range(HEADS):
            bias[h * CELLS + j * 24 : h * CELLS + j * 24 + 24, :] = moved[h * 24 : h * 24 + 24, :]


def attend(q, k, v, bias, prob):
    mixed = jnp.zeros((CELLS, WIDTH), FULL)
    for h in range(HEADS):
        rows = slice(h * CELLS, (h + 1) * CELLS)
        score = dot_nt(q * head_mask(h), k) * HEAD ** (-0.5) + bias[rows, :]
        expo = jnp.exp(score - jnp.max(score, -1, keepdims=True))
        weights = (expo * (1.0 / jnp.sum(expo, -1, keepdims=True))).astype(HALF)
        prob[rows, :] = weights
        mixed = jnp.where(head_lanes(h), dot(weights, v), mixed)
    return mixed.astype(HALF)


def attend_back(dmixed, q, k, v, prob):
    dq = jnp.zeros((CELLS, WIDTH), FULL)
    dk = jnp.zeros((CELLS, WIDTH), FULL)
    dv = jnp.zeros((CELLS, WIDTH), FULL)
    for h in range(HEADS):
        rows = slice(h * CELLS, (h + 1) * CELLS)
        weights = prob[rows, :]
        dhead = dmixed * head_mask(h)
        full = weights.astype(FULL)
        dweights = dot_nt(dhead, v)
        inner = jnp.sum(dweights * full, -1, keepdims=True)
        dscore = (full * (dweights - inner) * HEAD ** (-0.5)).astype(HALF)
        dv = dv + dot_tn(weights, dhead)
        dq = jnp.where(head_lanes(h), dot(dscore, k), dq)
        dk = dk + dot_tn(dscore, q * head_mask(h))
    return dq.astype(HALF), dk.astype(HALF), dv.astype(HALF)


def gelu_parts(u):
    below = 0.5 * (1.0 + lax.erf(u * (0.5**0.5)))
    slope = below + u * (jnp.exp(-0.5 * u * u) * (2.0 * np.pi) ** (-0.5))
    return below, slope


def forward_half(x, gains, wqkv, wproj, bias, prob):
    unit, spread = normalise(x)
    hidden = (unit * gains[0:1, :]).astype(HALF)
    qkv = dot(hidden, wqkv[...]).astype(HALF)
    q, k, v = (qkv[:, n * WIDTH : (n + 1) * WIDTH] for n in range(3))
    mixed = attend(q, k, v, bias, prob)
    return (q, k, v), x + dot(mixed, wproj[...])


def backward(dflat, x, qkv, prob, resid, slope, gains, wqkv, wproj, wup, wdown):
    q, k, v = qkv
    dactive = dot(dflat, wdown[...])
    dupward = (dactive * slope).astype(HALF)
    dnormed = dot_nt(dupward, wup[...])
    unit, spread = normalise(resid)
    dresid = dflat.astype(FULL) + normalise_back(dnormed, unit, spread, gains[1:2, :])
    dmixed = dot_nt(dresid.astype(HALF), wproj[...]).astype(HALF)
    dq, dk, dv = attend_back(dmixed, q, k, v, prob)
    dhidden = dot_nt(dq, wqkv[:, :WIDTH])
    dhidden = dhidden + dot_nt(dk, wqkv[:, WIDTH : 2 * WIDTH])
    dhidden = dhidden + dot_nt(dv, wqkv[:, 2 * WIDTH :])
    unit, spread = normalise(x)
    return dresid + normalise_back(dhidden, unit, spread, gains[0:1, :])


def gather_patches(upper, surface, section, select, ff, ft):
    base = 4 * section - 2
    for z in range(2):
        for a in range(2):
            level = jnp.maximum(base + 2 * z + a, 0)
            for v in range(5):
                field = upper[v, level].astype(FULL)
                if z == 0:
                    field = jnp.where(section == 0, 0.0, field)
                slot = (z * 2 + a) * 5 + v
                ff[slot * 24 : slot * 24 + 24, 0:48] = field
    for v in range(4):
        field = jnp.where(section == 0, surface[v].astype(FULL), 0.0)
        ff[(20 + v) * 24 : (21 + v) * 24, 0:48] = field
    pad = jnp.zeros((8, 128), FULL)
    for i in range(6):
        pieces = []
        for b in range(4):
            pieces += [ff[pl.ds(4 * i + b, 24, stride=24), :], pad]
        ft[i * 48 : i * 48 + 48, :] = jnp.concatenate(pieces, 0).T[:48]
    raw = [ft[pl.ds(c, 72, stride=4), :].astype(HALF) for c in range(4)]
    both = dot(jnp.concatenate(raw, 1), select[...])
    return jnp.concatenate((both[:, :256], both[:, 256:]), 0).astype(HALF)


def flag(axis):
    last = lax.axis_index(axis) == lax.axis_size(axis) - 1
    return jnp.where(last, 1.0, 0.0)


def table_rows(tbl, block, table):
    for h in range(HEADS):
        table[h : h + 1, 0 : tbl.shape[-1]] = tbl[block * HEADS + h]


def first_kernel(*refs):
    names = (
        "tbl", "upper", "surface", "to_inner", "uembed", "sembed", "gains",
        "wqkv", "wproj", "wup", "wdown", "cot", "out_first", "out_cot",
    )
    count = len(names)
    source, refs = refs[:count], refs[count:]
    results = ("patch", "x", "qkv", "prob", "resid", "slope", "send", "keep0", "keep1", "keep2", "keep3")
    target, refs = refs[: len(results)], refs[len(results) :]
    local, refs = refs[:count], refs[count:]
    patch_s, x_s, qkv_s, prob, resid_s, slope_s, blocks = refs[:7]
    ff, ft, emb, cots, table, xs, bias, cols, select, sems = refs[7:]
    copies = {}
    for n, name in enumerate(names):
        start, end = source[n], local[n]
        if name[0] == "w":
            start = start.at[0]
        elif name == "tbl":
            start = start.at[pl.ds(0, HEADS)]
        elif name == "uembed":
            end = emb.at[pl.ds(0, 160)]
        elif name == "sembed":
            end = emb.at[pl.ds(160, 64)]
        copies[name] = pltpu.make_async_copy(start, end, sems.at[n])
        copies[name].start()
    have = dict(zip(names, local))
    sent = []

    def wait(*which):
        for name in which:
            copies[name].wait()

    def send(name, held):
        n = results.index(name)
        sent.append(pltpu.make_async_copy(held, target[n], sems.at[len(names) + n]))
        sent[-1].start()

    emb[224:256, :] = jnp.zeros((32, WIDTH), HALF)
    fill_columns(cols)
    fill_select(select)
    wait("tbl")
    table_rows(have["tbl"], 0, table)
    build_bias(table, cols, xs, bias, None)
    wait("upper", "surface", "to_inner", "uembed", "sembed", "gains", "wqkv")
    section = lax.axis_index("section")
    patch = gather_patches(have["upper"], have["surface"], section, select, ff, ft)
    patch = dot(have["to_inner"][...], patch).astype(HALF)
    patch_s[...] = patch
    send("patch", patch_s)
    latent = dot(patch, emb[...]).astype(HALF)
    x_s[...] = latent
    send("x", x_s)
    x = latent.astype(FULL)
    gains = have["gains"].at[0]
    wait("wproj", "wup", "wdown", "cot", "out_first", "out_cot")
    cot = have["cot"]
    for a in range(6):
        for o in range(12):
            cots[(a * 12 + o) * 2 : (a * 12 + o) * 2 + 2, :] = cot[a, o].astype(FULL)
    ready = dot(have["out_cot"][...], cots[...].astype(HALF))
    qkv, resid = forward_half(x, gains, have["wqkv"], have["wproj"], bias, prob)
    send("prob", prob)
    for n in range(3):
        qkv_s[n] = qkv[n]
    send("qkv", qkv_s)
    resid_s[...] = resid
    send("resid", resid_s)
    unit, spread = normalise(resid)
    normed = (unit * gains[1:2, :]).astype(HALF)
    upward = dot(normed, have["wup"][...])
    below, slope = gelu_parts(upward)
    slope_s[...] = slope.astype(HALF)
    send("slope", slope_s)
    active = (upward * below).astype(HALF)
    result = (resid + dot_nt(active, have["wdown"][...])).astype(HALF)
    blocks[...] = (dot(have["out_first"][...], result) + ready).astype(HALF)
    send("send", blocks.at[pl.ds(192, 192)])
    for n in range(4):
        send("keep" + str(n), blocks.at[pl.ds(n * 48, 48)])
    for copy in sent:
        copy.wait()


def second_bias(tbl, after, bias, table, xs, cols):
    fill_columns(cols)
    table_rows(tbl, 1, table)
    build_bias(table, cols, xs, bias, (flag("section"), flag("lat")))


def second_kernel(*refs):
    parts, rest = refs[:4], refs[4:]
    gains, wqkv, wproj, wup, wdown, bias, into, out_of, send_o = rest[:9]
    keep, stack, prob = rest[9:13], rest[13], rest[14]
    for n in range(4):
        stack[n * 96 : n * 96 + 96, :] = parts[n][...]
    both = dot(into[...], stack[...])
    x, dflat = both[:CELLS], both[CELLS:].astype(HALF)
    gains, wqkv, wproj, wup, wdown = (w.at[1] for w in (gains, wqkv, wproj, wup, wdown))
    qkv, resid = forward_half(x, gains, wqkv, wproj, bias, prob)
    unit, spread = normalise(resid)
    normed = (unit * gains[1:2, :]).astype(HALF)
    upward = dot(normed, wup[...])
    slope = gelu_parts(upward)[1]
    dx = backward(dflat, x, qkv, prob, resid, slope, gains, wqkv, wproj, wup, wdown)
    moved = dot(out_of[...], dx.astype(HALF)).astype(HALF)
    send_o[...] = moved[128:]
    for n in range(4):
        keep[n][...] = moved[n * 32 : n * 32 + 32]


def third_kernel(*refs):
    parts, rest = refs[:4], refs[4:]
    gains, wqkv, wproj, wup, wdown, patch, x_i, qkv_i, prob, resid, slope, into, out_of = rest[:13]
    grad_o, mine_o, other_o, stack, terms = rest[13:]
    for n in range(4):
        stack[n * 64 : n * 64 + 64, :] = parts[n][...]
    dflat = dot(into[...], stack[...]).astype(HALF)
    qkv = tuple(qkv_i[n] for n in range(3))
    gains, wqkv, wproj, wup, wdown = (w.at[0] for w in (gains, wqkv, wproj, wup, wdown))
    dx = backward(
        dflat, x_i[...].astype(FULL), qkv, prob, resid[...], slope[...].astype(FULL),
        gains, wqkv, wproj, wup, wdown,
    )
    grad = dx.astype(HALF)
    moved = dot(out_of[...], grad).astype(HALF)
    for z in range(2):
        for a in range(6):
            grad_o[z, a] = moved[(z * 6 + a) * 16 : (z * 6 + a) * 16 + 12]
    total = dot_tn(patch[...], grad)
    terms[0:224, :] = total[:224, :128]
    terms[224:336, :] = jnp.concatenate((total[:112, 128:], total[112:224, 128:]), 1)
    place = lax.axis_index("section") % 2
    mine_o[...] = terms[pl.ds(pl.multiple_of(place * 168, 8), 168), :].astype(HALF)
    other_o[...] = terms[pl.ds(pl.multiple_of(168 - place * 168, 8), 168), :].astype(HALF)


vmem = pl.BlockSpec(memory_space=pltpu.VMEM)
hbm = pl.BlockSpec(memory_space=pltpu.HBM)


def call(kernel, outs, scratch, *args, spec=vmem, out=vmem, room=30, size=1):
    return pl.pallas_call(
        kernel,
        out_shape=outs,
        in_specs=[spec for a in args],
        out_specs=jax.tree.map(lambda _: out, outs),
        scratch_shapes=scratch,
        compiler_params=pltpu.CompilerParams(vmem_limit_bytes=room * 2**20),
        cost_estimate=pl.CostEstimate(flops=1000000, bytes_accessed=size * 1000000, transcendentals=0),
    )(*args)


def shape(dims, dtype=HALF):
    return jax.ShapeDtypeStruct(dims, dtype)


def fetch(block, steps):
    names = ("lon", "lat", "section")
    axes = [name for name in names if steps.get(name, 0)]
    if not axes:
        return block
    sizes = [lax.axis_size(name) for name in axes]
    pairs = []
    for place in np.ndindex(*sizes):
        source = [(p + steps[name]) % n for p, name, n in zip(place, axes, sizes)]
        pairs.append(
            (int(np.ravel_multi_index(source, sizes)), int(np.ravel_multi_index(place, sizes)))
        )
    return lax.ppermute(block, tuple(axes), pairs)


def exchange(keep, got, way):
    pitch = got.shape[0] // 4
    blocks = []
    for n in range(4):
        block = jnp.concatenate((keep[n], got[n * pitch : (n + 1) * pitch]), 0)
        blocks.append(fetch(block, {"lat": way * (n // 2), "lon": way * (n % 2)}))
    return blocks


def swap(block, flips):
    names = ("lon", "lat", "section")
    axes = [name for name in names if flips.get(name, 0)]
    sizes = [lax.axis_size(name) for name in axes]
    pairs = []
    for place in np.ndindex(*sizes):
        source = [p ^ flips[name] for p, name in zip(place, axes)]
        pairs.append(
            (int(np.ravel_multi_index(source, sizes)), int(np.ravel_multi_index(place, sizes)))
        )
    return lax.ppermute(block, tuple(axes), pairs)


def add_up(mine, other):
    total = (mine.astype(FULL) + swap(other, {"section": 1}).astype(FULL)).astype(HALF)
    bits = []
    for name in ("section", "lat", "lon"):
        size = lax.axis_size(name)
        if size & (size - 1) or size < 2:
            raise ValueError("axis size")
        bits += [(name, 1 << n) for n in range(name == "section", size.bit_length() - 1)]
    for n in range(0, len(bits), 2):
        pair = [{name: bit} for name, bit in bits[n : n + 2]]
        if len(pair) == 1:
            total = total.astype(FULL) + swap(total, pair[0]).astype(FULL)
        else:
            one, two = pair
            three = dict(one)
            for name, bit in two.items():
                three[name] = three.get(name, 0) | bit
            near, far, last = (swap(total, step).astype(FULL) for step in (one, two, three))
            total = (total.astype(FULL) + near) + (far + last)
        total = total.astype(HALF)
    return total, swap(total, {"section": 1})


def last_kernel(scale, mine, other, upper_o, surface_o, halves, both, sems):
    place = lax.axis_index("section") % 2
    halves[pl.ds(pl.multiple_of(place * 168, 8), 168), :] = mine[...].astype(FULL) * scale
    halves[pl.ds(pl.multiple_of(168 - place * 168, 8), 168), :] = other[...].astype(FULL) * scale
    both[:, 0:128] = halves[0:224, :]
    last = halves[224:336, :]
    both[0:112, 128:192] = last[:, :64]
    both[112:224, 128:192] = last[:, 64:]
    copies = [
        pltpu.make_async_copy(both.at[pl.ds(0, 160)], upper_o, sems.at[0]),
        pltpu.make_async_copy(both.at[pl.ds(160, 64)], surface_o, sems.at[1]),
    ]
    for copy in copies:
        copy.start()
    for copy in copies:
        copy.wait()


def on_device(
    upper_fields,
    surface_fields,
    upper_embed,
    surface_embed,
    norm_gains,
    qkv_weight,
    proj_weight,
    up_weight,
    down_weight,
    earth_bias,
    out_grad,
):
    sections, bands = lax.axis_size("section"), lax.axis_size("lat")
    levels, rows, columns, width = out_grad.shape
    positions = earth_bias.shape[-1]
    table = earth_bias.transpose(0, 1, 3, 2, 4).reshape(2 * HEADS, 1, positions)
    weights = (norm_gains, qkv_weight, proj_weight, up_weight, down_weight.transpose(0, 2, 1))

    def from_cot(z, a, o):
        return (a * 12 + o) * 2 + z

    operands = (
        table, upper_fields, surface_fields, jnp.asarray(natural_to_inner()), upper_embed,
        surface_embed, *weights, out_grad.transpose(1, 2, 0, 3),
        jnp.asarray(octants_out(48, 0, True, inner_row)),
        jnp.asarray(octants_out(48, 18, True, from_cot)),
    )
    local = [
        pltpu.VMEM(v.shape[1:] if 7 <= n < 11 else v.shape, v.dtype) for n, v in enumerate(operands)
    ]
    local[0] = pltpu.VMEM((HEADS, 1, positions), FULL)
    local[4] = local[5] = pltpu.VMEM((16, 128), HALF)
    scratch_bias = [pltpu.VMEM((8, 3328), FULL), pltpu.VMEM((4, CELLS, 128), FULL)]
    scratch_cols = pltpu.VMEM((2, 256, 384), HALF)
    held = [
        shape((CELLS, 256)),
        shape((CELLS, WIDTH)),
        shape((3, CELLS, WIDTH)),
        shape((HEADS * CELLS, CELLS)),
        shape((CELLS, WIDTH), FULL),
        shape((CELLS, 4 * WIDTH)),
    ]
    patch, x, qkv, prob, resid, slope, send, *keep = call(
        first_kernel,
        held + [shape((192, WIDTH))] + [shape((48, WIDTH))] * 4,
        local
        + [pltpu.VMEM(v.shape, v.dtype) for v in held]
        + [
            pltpu.VMEM((384, WIDTH), HALF),
            pltpu.VMEM((576, 128), FULL),
            pltpu.VMEM((288, 128), FULL),
            pltpu.VMEM((256, WIDTH), HALF),
            pltpu.VMEM((CELLS, WIDTH), FULL),
        ]
        + scratch_bias
        + [
            pltpu.VMEM((HEADS * CELLS, CELLS), FULL),
            scratch_cols,
            pltpu.VMEM((512, 512), HALF),
            pltpu.SemaphoreType.DMA((len(operands) + 11,)),
        ],
        *operands,
        spec=hbm,
        out=hbm,
        room=60,
    )
    bias_shape = shape((HEADS * CELLS, CELLS), FULL)
    got = fetch(send, {"section": 1})
    bias = call(second_bias, bias_shape, [*scratch_bias, scratch_cols], table, got)
    into = np.concatenate((octants_in(48, 0, False), octants_in(48, 18, False)), 0)
    send, *keep = call(
        second_kernel,
        [shape((128, WIDTH))] + [shape((32, WIDTH))] * 4,
        [pltpu.VMEM((8 * 48, WIDTH), HALF), pltpu.VMEM((HEADS * CELLS, CELLS), HALF)],
        *exchange(keep, got, 1), *weights, bias,
        jnp.asarray(into), jnp.asarray(octants_out(32, 0, False, inner_row)),
    )
    latent_grad, mine, other = call(
        third_kernel,
        [shape((2, 6, 12, WIDTH)), shape((168, 128)), shape((168, 128))],
        [pltpu.VMEM((8 * 32, WIDTH), HALF), pltpu.VMEM((336, 128), FULL)],
        *exchange(keep, fetch(send, {"section": -1}), -1), *weights, patch, x, qkv, prob, resid, slope,
        jnp.asarray(octants_in(32, 0, True)), jnp.asarray(inner_to_padded()),
    )
    scale = float(levels * sections * rows * bands * columns * lax.axis_size("lon")) ** (-0.5)
    upper_grad, surface_grad = call(
        functools.partial(last_kernel, scale),
        [shape((160, WIDTH), FULL), shape((64, WIDTH), FULL)],
        [
            pltpu.VMEM((336, 128), FULL),
            pltpu.VMEM((224, WIDTH), FULL),
            pltpu.SemaphoreType.DMA((2,)),
        ],
        *add_up(mine, other),
        out=hbm,
    )
    return (latent_grad, upper_grad, surface_grad)


def solution(mesh):
    placed = (
        P(None, None, "lat", "lon"),
        P(None, "lat", "lon"),
        P(),
        P(),
        P(),
        P(),
        P(),
        P(),
        P(),
        P(None, "lat", "section", None, None),
        P("section", "lat", "lon", None),
    )
    return jax.shard_map(
        on_device,
        mesh=mesh,
        in_specs=placed,
        out_specs=(P("section", "lat", "lon", None), P(), P()),
        check_vma=False,
    )
```

```python
import functools

import jax
import jax.numpy as jnp
import ml_dtypes
import numpy as np
from jax import lax
from jax.experimental import pallas as pl
from jax.experimental.pallas import tpu as pltpu
from jax.sharding import PartitionSpec as P

neg_fill = -1e30
norm_eps = 1e-05
HEADS = 6
HEAD = 32
CELLS = 144
WIDTH = 192
FULL = jnp.float32
HALF = jnp.bfloat16


def inner_row(z, a, o):
    return o * 12 + z * 6 + a


def octant_of(z, a, o):
    return (z * 4 + (a // 3) * 2 + o // 6, (a % 3) * 6 + o % 6)


def as_half(array):
    return array.astype(ml_dtypes.bfloat16)


def cells():
    return [(z, a, o) for z in range(2) for a in range(6) for o in range(12)]


def natural_to_inner():
    move = np.zeros((CELLS, CELLS), np.float32)
    for z, a, o in cells():
        move[inner_row(z, a, o), (z * 6 + a) * 12 + o] = 1
    return as_half(move)


def inner_to_padded():
    move = np.zeros((192, CELLS), np.float32)
    for z, a, o in cells():
        move[(z * 6 + a) * 16 + o, inner_row(z, a, o)] = 1
    return as_half(move)


def octants_out(pitch, first, flip, source):
    move = np.zeros((8 * pitch, CELLS), np.float32)
    for z, a, o in cells():
        part, place = octant_of(z, a, o)
        move[(7 - part if flip else part) * pitch + first + place, source(z, a, o)] = 1
    return as_half(move)


def octants_in(pitch, first, flip):
    move = np.zeros((CELLS, 8 * pitch), np.float32)
    for z, a, o in cells():
        part, place = octant_of(z, a, o)
        part = 7 - part if flip else part
        block = (part % 4) * 2 + part // 4
        move[inner_row(z, a, o), block * pitch + first + place] = 1
    return as_half(move)


def whole_part(v, size):
    return jnp.floor((v + 0.5) * (1.0 / size))


def one_hot(target, lanes):
    lane = lax.broadcasted_iota(jnp.int32, (1, lanes), 1).astype(FULL)
    return jnp.where(lane == target, 1.0, 0.0).astype(HALF)


def fill_columns(cols):
    row = lax.broadcasted_iota(jnp.int32, (256, 1), 0).astype(FULL)
    a = whole_part(row, 23)
    k = row - 23.0 * a
    for z in range(2):
        target = (22.0 - k) * 12.0 + (z * 6.0) + a
        cols[z] = one_hot(jnp.where(row < 138.0, target, -1.0), 384)


def fill_select(select):
    row = lax.broadcasted_iota(jnp.int32, (128, 1), 0).astype(FULL)
    b = whole_part(row, 32)
    slot = row - 32.0 * b
    layer = whole_part(slot, 5)
    z = whole_part(layer, 2)
    upper = z * 256.0 + (slot - 5.0 * layer) * 32.0 + (layer - 2.0 * z) * 16.0
    surface = 160.0 + (slot - 20.0) * 16.0
    target = jnp.where(slot < 20.0, upper, surface) + b * 4.0
    for c in range(4):
        select[c * 128 : c * 128 + 128, :] = one_hot(
            jnp.where(slot < 24.0, target + float(c), -1.0), 512
        )


def dot(a, b):
    return jnp.dot(a, b, preferred_element_type=FULL)


def dot_nt(a, b):
    return lax.dot_general(a, b, (((1,), (1,)), ((), ())), preferred_element_type=FULL)


def dot_tn(a, b):
    return lax.dot_general(a, b, (((0,), (0,)), ((), ())), preferred_element_type=FULL)


def normalise(v):
    mean = jnp.mean(v, -1, keepdims=True)
    centred = v - mean
    spread = lax.rsqrt(jnp.mean(centred * centred, -1, keepdims=True) + norm_eps)
    return centred * spread, spread


def normalise_back(dy, unit, spread, gain):
    dunit = dy * gain
    inner = jnp.mean(dunit * unit, -1, keepdims=True)
    return spread * (dunit - jnp.mean(dunit, -1, keepdims=True) - unit * inner)


def head_lanes(h):
    lane = lax.broadcasted_iota(jnp.int32, (1, WIDTH), 1)
    return (lane >= h * HEAD) & (lane < (h + 1) * HEAD)


def head_mask(h):
    return jnp.where(head_lanes(h), 1.0, 0.0).astype(HALF)


def build_bias(tbl, cols, xs, bias, edges):
    for z in range(2):
        for a in range(6):
            for zu in range(2):
                start = ((z * 2 + zu) * 6 + a) * 138
                piece = tbl[0:HEADS, start : start + 138]
                piece = jnp.concatenate((piece, jnp.zeros((HEADS, 118), FULL)), 1)
                for p in range(2):
                    for half in range(2):
                        xs[zu * 2 + half, pl.ds(p * 12 + z * 6 + a, HEADS, stride=24), :] = piece[
                            :, half * 128 : half * 128 + 128
                        ]
    total = None
    for zu in range(2):
        x = jnp.concatenate((xs[zu * 2], xs[zu * 2 + 1]), 1)
        high = x.astype(HALF)
        left = x - high.astype(FULL)
        mid = left.astype(HALF)
        low = (left - mid.astype(FULL)).astype(HALF)
        term = dot(jnp.concatenate((high, mid, low), 0), cols[zu])
        total = term if total is None else total + term
    table = total[:CELLS] + total[CELLS : 2 * CELLS] + total[2 * CELLS :]
    row = lax.broadcasted_iota(jnp.int32, (CELLS, 1), 0).astype(FULL)
    lane = lax.broadcasted_iota(jnp.int32, (1, CELLS), 1).astype(FULL)

    part = whole_part
    even = part(row, 12) - 2.0 * part(part(row, 12), 2) == 0.0
    table = jnp.where(even, pltpu.roll(table, 384 - 12, 1), table)
    if edges is not None:
        last_section, last_band = edges
        row12, lane12 = row - 12.0 * part(row, 12), lane - 12.0 * part(lane, 12)
        row_z, lane_z = part(row12, 6), part(lane12, 6)
        row_a, lane_a = part(row12 - 6.0 * row_z, 3), part(lane12 - 6.0 * lane_z, 3)
        apart = jnp.abs(row_z - lane_z) * last_section + jnp.abs(row_a - lane_a) * last_band
        blocked = apart > 0.5
    for j in range(6):
        shift = (10 - 2 * j) * 12
        moved = pltpu.roll(table, 384 - shift, 1) if shift else table
        moved = moved[:, :CELLS]
        if edges is not None:
            moved = jnp.where(blocked, neg_fill, moved)
        for h in range(HEADS):
            bias[h * CELLS + j * 24 : h * CELLS + j * 24 + 24, :] = moved[h * 24 : h * 24 + 24, :]


def attend(q, k, v, bias, prob):
    mixed = jnp.zeros((CELLS, WIDTH), FULL)
    for h in range(HEADS):
        rows = slice(h * CELLS, (h + 1) * CELLS)
        score = dot_nt(q * head_mask(h), k) * HEAD ** (-0.5) + bias[rows, :]
        expo = jnp.exp(score - jnp.max(score, -1, keepdims=True))
        weights = (expo * (1.0 / jnp.sum(expo, -1, keepdims=True))).astype(HALF)
        prob[rows, :] = weights
        mixed = jnp.where(head_lanes(h), dot(weights, v), mixed)
    return mixed.astype(HALF)


def attend_back(dmixed, q, k, v, prob):
    dq = jnp.zeros((CELLS, WIDTH), FULL)
    dk = jnp.zeros((CELLS, WIDTH), FULL)
    dv = jnp.zeros((CELLS, WIDTH), FULL)
    for h in range(HEADS):
        rows = slice(h * CELLS, (h + 1) * CELLS)
        weights = prob[rows, :]
        dhead = dmixed * head_mask(h)
        full = weights.astype(FULL)
        dweights = dot_nt(dhead, v)
        inner = jnp.sum(dweights * full, -1, keepdims=True)
        dscore = (full * (dweights - inner) * HEAD ** (-0.5)).astype(HALF)
        dv = dv + dot_tn(weights, dhead)
        dq = jnp.where(head_lanes(h), dot(dscore, k), dq)
        dk = dk + dot_tn(dscore, q * head_mask(h))
    return dq.astype(HALF), dk.astype(HALF), dv.astype(HALF)


def gelu_parts(u):
    below = 0.5 * (1.0 + lax.erf(u * (0.5**0.5)))
    slope = below + u * (jnp.exp(-0.5 * u * u) * (2.0 * np.pi) ** (-0.5))
    return below, slope


def forward_half(x, gains, wqkv, wproj, bias, prob):
    unit, spread = normalise(x)
    hidden = (unit * gains[0:1, :]).astype(HALF)
    qkv = dot(hidden, wqkv[...]).astype(HALF)
    q, k, v = (qkv[:, n * WIDTH : (n + 1) * WIDTH] for n in range(3))
    mixed = attend(q, k, v, bias, prob)
    return (q, k, v), x + dot(mixed, wproj[...])


def backward(dflat, x, qkv, prob, resid, slope, gains, wqkv, wproj, wup, wdown):
    q, k, v = qkv
    dactive = dot(dflat, wdown[...])
    dupward = (dactive * slope).astype(HALF)
    dnormed = dot_nt(dupward, wup[...])
    unit, spread = normalise(resid)
    dresid = dflat.astype(FULL) + normalise_back(dnormed, unit, spread, gains[1:2, :])
    dmixed = dot_nt(dresid.astype(HALF), wproj[...]).astype(HALF)
    dq, dk, dv = attend_back(dmixed, q, k, v, prob)
    dhidden = dot_nt(dq, wqkv[:, :WIDTH])
    dhidden = dhidden + dot_nt(dk, wqkv[:, WIDTH : 2 * WIDTH])
    dhidden = dhidden + dot_nt(dv, wqkv[:, 2 * WIDTH :])
    unit, spread = normalise(x)
    return dresid + normalise_back(dhidden, unit, spread, gains[0:1, :])


def gather_patches(upper, surface, section, select, ff, ft):
    base = 4 * section - 2
    for z in range(2):
        for a in range(2):
            level = jnp.maximum(base + 2 * z + a, 0)
            for v in range(5):
                field = upper[v, level].astype(FULL)
                if z == 0:
                    field = jnp.where(section == 0, 0.0, field)
                slot = (z * 2 + a) * 5 + v
                ff[slot * 24 : slot * 24 + 24, 0:48] = field
    for v in range(4):
        field = jnp.where(section == 0, surface[v].astype(FULL), 0.0)
        ff[(20 + v) * 24 : (21 + v) * 24, 0:48] = field
    pad = jnp.zeros((8, 128), FULL)
    for i in range(6):
        pieces = []
        for b in range(4):
            pieces += [ff[pl.ds(4 * i + b, 24, stride=24), :], pad]
        ft[i * 48 : i * 48 + 48, :] = jnp.concatenate(pieces, 0).T[:48]
    raw = [ft[pl.ds(c, 72, stride=4), :].astype(HALF) for c in range(4)]
    both = dot(jnp.concatenate(raw, 1), select[...])
    return jnp.concatenate((both[:, :256], both[:, 256:]), 0).astype(HALF)


def flag(axis):
    last = lax.axis_index(axis) == lax.axis_size(axis) - 1
    return jnp.where(last, 1.0, 0.0)


def table_rows(tbl, block, table):
    for h in range(HEADS):
        table[h : h + 1, 0 : tbl.shape[-1]] = tbl[block * HEADS + h]


def first_kernel(*refs):
    names = (
        "tbl", "upper", "surface", "to_inner", "uembed", "sembed", "gains",
        "wqkv", "wproj", "wup", "wdown", "cot", "out_first", "out_cot",
    )
    count = len(names)
    source, refs = refs[:count], refs[count:]
    patch_o, x_o, qkv_o, prob, resid_o, slope_o, send_o, *keep_o = refs[:11]
    refs = refs[11:]
    local, refs = refs[:count], refs[count:]
    ff, ft, emb, cots, table, xs, bias, cols, select, sems = refs
    copies = {}
    for n, name in enumerate(names):
        start, end = source[n], local[n]
        if name[0] == "w":
            start = start.at[0]
        elif name == "tbl":
            start = start.at[pl.ds(0, HEADS)]
        elif name == "uembed":
            end = emb.at[pl.ds(0, 160)]
        elif name == "sembed":
            end = emb.at[pl.ds(160, 64)]
        copies[name] = pltpu.make_async_copy(start, end, sems.at[n])
        copies[name].start()
    have = dict(zip(names, local))

    def wait(*which):
        for name in which:
            copies[name].wait()

    emb[224:256, :] = jnp.zeros((32, WIDTH), HALF)
    fill_columns(cols)
    fill_select(select)
    wait("tbl")
    table_rows(have["tbl"], 0, table)
    build_bias(table, cols, xs, bias, None)
    wait("upper", "surface", "to_inner", "uembed", "sembed", "gains", "wqkv")
    section = lax.axis_index("section")
    patch = gather_patches(have["upper"], have["surface"], section, select, ff, ft)
    patch = dot(have["to_inner"][...], patch).astype(HALF)
    patch_o[...] = patch
    latent = dot(patch, emb[...]).astype(HALF)
    x_o[...] = latent
    x = latent.astype(FULL)
    gains = have["gains"].at[0]
    wait("wproj", "wup", "wdown", "cot", "out_first", "out_cot")
    cot = have["cot"]
    for a in range(6):
        for o in range(12):
            cots[(a * 12 + o) * 2 : (a * 12 + o) * 2 + 2, :] = cot[a, o].astype(FULL)
    ready = dot(have["out_cot"][...], cots[...].astype(HALF))
    qkv, resid = forward_half(x, gains, have["wqkv"], have["wproj"], bias, prob)
    for n in range(3):
        qkv_o[n] = qkv[n]
    resid_o[...] = resid
    unit, spread = normalise(resid)
    normed = (unit * gains[1:2, :]).astype(HALF)
    upward = dot(normed, have["wup"][...])
    below, slope = gelu_parts(upward)
    slope_o[...] = slope.astype(HALF)
    active = (upward * below).astype(HALF)
    result = (resid + dot_nt(active, have["wdown"][...])).astype(HALF)
    moved = (dot(have["out_first"][...], result) + ready).astype(HALF)
    send_o[...] = moved[192:]
    for n in range(4):
        keep_o[n][...] = moved[n * 48 : n * 48 + 48]


def second_bias(tbl, after, bias, table, xs, cols):
    fill_columns(cols)
    table_rows(tbl, 1, table)
    build_bias(table, cols, xs, bias, (flag("section"), flag("lat")))


def second_kernel(*refs):
    parts, rest = refs[:4], refs[4:]
    gains, wqkv, wproj, wup, wdown, bias, into, out_of, send_o = rest[:9]
    keep, stack, prob = rest[9:13], rest[13], rest[14]
    for n in range(4):
        stack[n * 96 : n * 96 + 96, :] = parts[n][...]
    both = dot(into[...], stack[...])
    x, dflat = both[:CELLS], both[CELLS:].astype(HALF)
    gains, wqkv, wproj, wup, wdown = (w.at[1] for w in (gains, wqkv, wproj, wup, wdown))
    qkv, resid = forward_half(x, gains, wqkv, wproj, bias, prob)
    unit, spread = normalise(resid)
    normed = (unit * gains[1:2, :]).astype(HALF)
    upward = dot(normed, wup[...])
    slope = gelu_parts(upward)[1]
    dx = backward(dflat, x, qkv, prob, resid, slope, gains, wqkv, wproj, wup, wdown)
    moved = dot(out_of[...], dx.astype(HALF)).astype(HALF)
    send_o[...] = moved[128:]
    for n in range(4):
        keep[n][...] = moved[n * 32 : n * 32 + 32]


def third_kernel(*refs):
    parts, rest = refs[:4], refs[4:]
    gains, wqkv, wproj, wup, wdown, patch, x_i, qkv_i, prob, resid, slope, into, out_of = rest[:13]
    grad_o, mine_o, other_o, stack, terms = rest[13:]
    for n in range(4):
        stack[n * 64 : n * 64 + 64, :] = parts[n][...]
    dflat = dot(into[...], stack[...]).astype(HALF)
    qkv = tuple(qkv_i[n] for n in range(3))
    gains, wqkv, wproj, wup, wdown = (w.at[0] for w in (gains, wqkv, wproj, wup, wdown))
    dx = backward(
        dflat, x_i[...].astype(FULL), qkv, prob, resid[...], slope[...].astype(FULL),
        gains, wqkv, wproj, wup, wdown,
    )
    grad = dx.astype(HALF)
    moved = dot(out_of[...], grad).astype(HALF)
    for z in range(2):
        for a in range(6):
            grad_o[z, a] = moved[(z * 6 + a) * 16 : (z * 6 + a) * 16 + 12]
    total = dot_tn(patch[...], grad)
    terms[0:224, :] = total[:224, :128]
    terms[224:336, :] = jnp.concatenate((total[:112, 128:], total[112:224, 128:]), 1)
    place = lax.axis_index("section") % 2
    mine_o[...] = terms[pl.ds(pl.multiple_of(place * 168, 8), 168), :].astype(HALF)
    other_o[...] = terms[pl.ds(pl.multiple_of(168 - place * 168, 8), 168), :].astype(HALF)


vmem = pl.BlockSpec(memory_space=pltpu.VMEM)
hbm = pl.BlockSpec(memory_space=pltpu.HBM)


def call(kernel, outs, scratch, *args, spec=vmem, out=vmem, room=30, size=1):
    return pl.pallas_call(
        kernel,
        out_shape=outs,
        in_specs=[spec for a in args],
        out_specs=jax.tree.map(lambda _: out, outs),
        scratch_shapes=scratch,
        compiler_params=pltpu.CompilerParams(vmem_limit_bytes=room * 2**20),
        cost_estimate=pl.CostEstimate(flops=1000000, bytes_accessed=size * 1000000, transcendentals=0),
    )(*args)


def shape(dims, dtype=HALF):
    return jax.ShapeDtypeStruct(dims, dtype)


def fetch(block, steps):
    names = ("lon", "lat", "section")
    axes = [name for name in names if steps.get(name, 0)]
    if not axes:
        return block
    sizes = [lax.axis_size(name) for name in axes]
    pairs = []
    for place in np.ndindex(*sizes):
        source = [(p + steps[name]) % n for p, name, n in zip(place, axes, sizes)]
        pairs.append(
            (int(np.ravel_multi_index(source, sizes)), int(np.ravel_multi_index(place, sizes)))
        )
    return lax.ppermute(block, tuple(axes), pairs)


def exchange(keep, got, way):
    pitch = got.shape[0] // 4
    blocks = []
    for n in range(4):
        block = jnp.concatenate((keep[n], got[n * pitch : (n + 1) * pitch]), 0)
        blocks.append(fetch(block, {"lat": way * (n // 2), "lon": way * (n % 2)}))
    return blocks


def swap(block, flips):
    names = ("lon", "lat", "section")
    axes = [name for name in names if flips.get(name, 0)]
    sizes = [lax.axis_size(name) for name in axes]
    pairs = []
    for place in np.ndindex(*sizes):
        source = [p ^ flips[name] for p, name in zip(place, axes)]
        pairs.append(
            (int(np.ravel_multi_index(source, sizes)), int(np.ravel_multi_index(place, sizes)))
        )
    return lax.ppermute(block, tuple(axes), pairs)


def add_up(mine, other):
    total = (mine.astype(FULL) + swap(other, {"section": 1}).astype(FULL)).astype(HALF)
    bits = []
    for name in ("section", "lat", "lon"):
        size = lax.axis_size(name)
        if size & (size - 1) or size < 2:
            raise ValueError("axis size")
        bits += [(name, 1 << n) for n in range(name == "section", size.bit_length() - 1)]
    for n in range(0, len(bits), 2):
        pair = [{name: bit} for name, bit in bits[n : n + 2]]
        if len(pair) == 1:
            total = total.astype(FULL) + swap(total, pair[0]).astype(FULL)
        else:
            one, two = pair
            three = dict(one)
            for name, bit in two.items():
                three[name] = three.get(name, 0) | bit
            near, far, last = (swap(total, step).astype(FULL) for step in (one, two, three))
            total = (total.astype(FULL) + near) + (far + last)
        total = total.astype(HALF)
    return total, swap(total, {"section": 1})


def last_kernel(scale, mine, other, upper_o, surface_o, halves, both, sems):
    place = lax.axis_index("section") % 2
    halves[pl.ds(pl.multiple_of(place * 168, 8), 168), :] = mine[...].astype(FULL) * scale
    halves[pl.ds(pl.multiple_of(168 - place * 168, 8), 168), :] = other[...].astype(FULL) * scale
    both[:, 0:128] = halves[0:224, :]
    last = halves[224:336, :]
    both[0:112, 128:192] = last[:, :64]
    both[112:224, 128:192] = last[:, 64:]
    copies = [
        pltpu.make_async_copy(both.at[pl.ds(0, 160)], upper_o, sems.at[0]),
        pltpu.make_async_copy(both.at[pl.ds(160, 64)], surface_o, sems.at[1]),
    ]
    for copy in copies:
        copy.start()
    for copy in copies:
        copy.wait()


def on_device(
    upper_fields,
    surface_fields,
    upper_embed,
    surface_embed,
    norm_gains,
    qkv_weight,
    proj_weight,
    up_weight,
    down_weight,
    earth_bias,
    out_grad,
):
    sections, bands = lax.axis_size("section"), lax.axis_size("lat")
    levels, rows, columns, width = out_grad.shape
    positions = earth_bias.shape[-1]
    table = earth_bias.transpose(0, 1, 3, 2, 4).reshape(2 * HEADS, 1, positions)
    weights = (norm_gains, qkv_weight, proj_weight, up_weight, down_weight.transpose(0, 2, 1))

    def from_cot(z, a, o):
        return (a * 12 + o) * 2 + z

    operands = (
        table, upper_fields, surface_fields, jnp.asarray(natural_to_inner()), upper_embed,
        surface_embed, *weights, out_grad.transpose(1, 2, 0, 3),
        jnp.asarray(octants_out(48, 0, True, inner_row)),
        jnp.asarray(octants_out(48, 18, True, from_cot)),
    )
    local = [
        pltpu.VMEM(v.shape[1:] if 7 <= n < 11 else v.shape, v.dtype) for n, v in enumerate(operands)
    ]
    local[0] = pltpu.VMEM((HEADS, 1, positions), FULL)
    local[4] = local[5] = pltpu.VMEM((16, 128), HALF)
    scratch_bias = [pltpu.VMEM((8, 3328), FULL), pltpu.VMEM((4, CELLS, 128), FULL)]
    scratch_cols = pltpu.VMEM((2, 256, 384), HALF)
    held = [
        shape((CELLS, 256)),
        shape((CELLS, WIDTH)),
        shape((3, CELLS, WIDTH)),
        shape((HEADS * CELLS, CELLS)),
        shape((CELLS, WIDTH), FULL),
        shape((CELLS, 4 * WIDTH)),
    ]
    patch, x, qkv, prob, resid, slope, send, *keep = call(
        first_kernel,
        held + [shape((192, WIDTH))] + [shape((48, WIDTH))] * 4,
        local
        + [
            pltpu.VMEM((576, 128), FULL),
            pltpu.VMEM((288, 128), FULL),
            pltpu.VMEM((256, WIDTH), HALF),
            pltpu.VMEM((CELLS, WIDTH), FULL),
        ]
        + scratch_bias
        + [
            pltpu.VMEM((HEADS * CELLS, CELLS), FULL),
            scratch_cols,
            pltpu.VMEM((512, 512), HALF),
            pltpu.SemaphoreType.DMA((len(operands),)),
        ],
        *(pltpu.with_memory_space_constraint(v, pltpu.HBM) for v in operands),
        spec=hbm,
    )
    bias_shape = shape((HEADS * CELLS, CELLS), FULL)
    got = fetch(send, {"section": 1})
    bias = call(second_bias, bias_shape, [*scratch_bias, scratch_cols], table, got)
    into = np.concatenate((octants_in(48, 0, False), octants_in(48, 18, False)), 0)
    send, *keep = call(
        second_kernel,
        [shape((128, WIDTH))] + [shape((32, WIDTH))] * 4,
        [pltpu.VMEM((8 * 48, WIDTH), HALF), pltpu.VMEM((HEADS * CELLS, CELLS), HALF)],
        *exchange(keep, got, 1), *weights, bias,
        jnp.asarray(into), jnp.asarray(octants_out(32, 0, False, inner_row)),
    )
    latent_grad, mine, other = call(
        third_kernel,
        [shape((2, 6, 12, WIDTH)), shape((168, 128)), shape((168, 128))],
        [pltpu.VMEM((8 * 32, WIDTH), HALF), pltpu.VMEM((336, 128), FULL)],
        *exchange(keep, fetch(send, {"section": -1}), -1), *weights, patch, x, qkv, prob, resid, slope,
        jnp.asarray(octants_in(32, 0, True)), jnp.asarray(inner_to_padded()),
    )
    scale = float(levels * sections * rows * bands * columns * lax.axis_size("lon")) ** (-0.5)
    upper_grad, surface_grad = call(
        functools.partial(last_kernel, scale),
        [shape((160, WIDTH), FULL), shape((64, WIDTH), FULL)],
        [
            pltpu.VMEM((336, 128), FULL),
            pltpu.VMEM((224, WIDTH), FULL),
            pltpu.SemaphoreType.DMA((2,)),
        ],
        *add_up(mine, other),
        out=hbm,
    )
    return (latent_grad, upper_grad, surface_grad)


def solution(mesh):
    placed = (
        P(None, None, "lat", "lon"),
        P(None, "lat", "lon"),
        P(),
        P(),
        P(),
        P(),
        P(),
        P(),
        P(),
        P(None, "lat", "section", None, None),
        P("section", "lat", "lon", None),
    )
    return jax.shard_map(
        on_device,
        mesh=mesh,
        in_specs=placed,
        out_specs=(P("section", "lat", "lon", None), P(), P()),
        check_vma=False,
    )
```

```python
import functools

import jax
import jax.numpy as jnp
import ml_dtypes
import numpy as np
from jax import lax
from jax.experimental import pallas as pl
from jax.experimental.pallas import tpu as pltpu
from jax.sharding import PartitionSpec as P

neg_fill = -1e30
norm_eps = 1e-05
HEADS = 6
HEAD = 32
CELLS = 144
WIDTH = 192
FULL = jnp.float32
HALF = jnp.bfloat16


def inner_row(z, a, o):
    return o * 12 + z * 6 + a


def octant_of(z, a, o):
    return (z * 4 + (a // 3) * 2 + o // 6, (a % 3) * 6 + o % 6)


def as_half(array):
    return array.astype(ml_dtypes.bfloat16)


def cells():
    return [(z, a, o) for z in range(2) for a in range(6) for o in range(12)]


def natural_to_inner():
    move = np.zeros((CELLS, CELLS), np.float32)
    for z, a, o in cells():
        move[inner_row(z, a, o), (z * 6 + a) * 12 + o] = 1
    return as_half(move)


def inner_to_padded():
    move = np.zeros((192, CELLS), np.float32)
    for z, a, o in cells():
        move[(z * 6 + a) * 16 + o, inner_row(z, a, o)] = 1
    return as_half(move)


def octants_out(pitch, first, flip, source):
    move = np.zeros((8 * pitch, CELLS), np.float32)
    for z, a, o in cells():
        part, place = octant_of(z, a, o)
        move[(7 - part if flip else part) * pitch + first + place, source(z, a, o)] = 1
    return as_half(move)


def octants_in(pitch, first, flip):
    move = np.zeros((CELLS, 8 * pitch), np.float32)
    for z, a, o in cells():
        part, place = octant_of(z, a, o)
        part = 7 - part if flip else part
        block = (part % 4) * 2 + part // 4
        move[inner_row(z, a, o), block * pitch + first + place] = 1
    return as_half(move)


def whole_part(v, size):
    return jnp.floor((v + 0.5) * (1.0 / size))


def one_hot(target, lanes):
    lane = lax.broadcasted_iota(jnp.int32, (1, lanes), 1).astype(FULL)
    return jnp.where(lane == target, 1.0, 0.0).astype(HALF)


def fill_columns(cols):
    row = lax.broadcasted_iota(jnp.int32, (256, 1), 0).astype(FULL)
    a = whole_part(row, 23)
    k = row - 23.0 * a
    for z in range(2):
        target = (22.0 - k) * 12.0 + (z * 6.0) + a
        cols[z] = one_hot(jnp.where(row < 138.0, target, -1.0), 384)


def fill_select(select):
    row = lax.broadcasted_iota(jnp.int32, (128, 1), 0).astype(FULL)
    b = whole_part(row, 32)
    slot = row - 32.0 * b
    layer = whole_part(slot, 5)
    z = whole_part(layer, 2)
    upper = z * 256.0 + (slot - 5.0 * layer) * 32.0 + (layer - 2.0 * z) * 16.0
    surface = 160.0 + (slot - 20.0) * 16.0
    target = jnp.where(slot < 20.0, upper, surface) + b * 4.0
    for c in range(4):
        select[c * 128 : c * 128 + 128, :] = one_hot(
            jnp.where(slot < 24.0, target + float(c), -1.0), 512
        )


def dot(a, b):
    return jnp.dot(a, b, preferred_element_type=FULL)


def dot_nt(a, b):
    return lax.dot_general(a, b, (((1,), (1,)), ((), ())), preferred_element_type=FULL)


def dot_tn(a, b):
    return lax.dot_general(a, b, (((0,), (0,)), ((), ())), preferred_element_type=FULL)


def normalise(v):
    mean = jnp.mean(v, -1, keepdims=True)
    centred = v - mean
    spread = lax.rsqrt(jnp.mean(centred * centred, -1, keepdims=True) + norm_eps)
    return centred * spread, spread


def normalise_back(dy, unit, spread, gain):
    dunit = dy * gain
    inner = jnp.mean(dunit * unit, -1, keepdims=True)
    return spread * (dunit - jnp.mean(dunit, -1, keepdims=True) - unit * inner)


def head_lanes(h):
    lane = lax.broadcasted_iota(jnp.int32, (1, WIDTH), 1)
    return (lane >= h * HEAD) & (lane < (h + 1) * HEAD)


def head_mask(h):
    return jnp.where(head_lanes(h), 1.0, 0.0).astype(HALF)


def build_bias(tbl, cols, xs, bias, edges):
    for z in range(2):
        for a in range(6):
            for zu in range(2):
                start = ((z * 2 + zu) * 6 + a) * 138
                piece = tbl[0:HEADS, start : start + 138]
                piece = jnp.concatenate((piece, jnp.zeros((HEADS, 118), FULL)), 1)
                for p in range(2):
                    for half in range(2):
                        xs[zu * 2 + half, pl.ds(p * 12 + z * 6 + a, HEADS, stride=24), :] = piece[
                            :, half * 128 : half * 128 + 128
                        ]
    total = None
    for zu in range(2):
        x = jnp.concatenate((xs[zu * 2], xs[zu * 2 + 1]), 1)
        high = x.astype(HALF)
        left = x - high.astype(FULL)
        mid = left.astype(HALF)
        low = (left - mid.astype(FULL)).astype(HALF)
        term = dot(jnp.concatenate((high, mid, low), 0), cols[zu])
        total = term if total is None else total + term
    table = total[:CELLS] + total[CELLS : 2 * CELLS] + total[2 * CELLS :]
    row = lax.broadcasted_iota(jnp.int32, (CELLS, 1), 0).astype(FULL)
    lane = lax.broadcasted_iota(jnp.int32, (1, CELLS), 1).astype(FULL)

    part = whole_part
    even = part(row, 12) - 2.0 * part(part(row, 12), 2) == 0.0
    table = jnp.where(even, pltpu.roll(table, 384 - 12, 1), table)
    if edges is not None:
        last_section, last_band = edges
        row12, lane12 = row - 12.0 * part(row, 12), lane - 12.0 * part(lane, 12)
        row_z, lane_z = part(row12, 6), part(lane12, 6)
        row_a, lane_a = part(row12 - 6.0 * row_z, 3), part(lane12 - 6.0 * lane_z, 3)
        apart = jnp.abs(row_z - lane_z) * last_section + jnp.abs(row_a - lane_a) * last_band
        blocked = apart > 0.5
    for j in range(6):
        shift = (10 - 2 * j) * 12
        moved = pltpu.roll(table, 384 - shift, 1) if shift else table
        moved = moved[:, :CELLS]
        if edges is not None:
            moved = jnp.where(blocked, neg_fill, moved)
        for h in range(HEADS):
            bias[h * CELLS + j * 24 : h * CELLS + j * 24 + 24, :] = moved[h * 24 : h * 24 + 24, :]


def by_head(rows):
    return jnp.concatenate([rows * head_mask(h) for h in range(HEADS)], 0)


def attend(q, k, v, bias, prob):
    scores = dot_nt(by_head(q), k)
    for h in range(HEADS):
        rows = slice(h * CELLS, (h + 1) * CELLS)
        score = scores[rows] * HEAD ** (-0.5) + bias[rows, :]
        expo = jnp.exp(score - jnp.max(score, -1, keepdims=True))
        prob[rows, :] = (expo * (1.0 / jnp.sum(expo, -1, keepdims=True))).astype(HALF)
    mixed = jnp.zeros((CELLS, WIDTH), FULL)
    for h in range(HEADS):
        term = dot(prob[h * CELLS : (h + 1) * CELLS, :], v)
        mixed = jnp.where(head_lanes(h), term, mixed)
    return mixed.astype(HALF)


def attend_back(dmixed, q, k, v, prob):
    dheads = by_head(dmixed)
    dweights = dot_nt(dheads, v)
    dv = dot_tn(prob[...], dheads)
    dscores = []
    for h in range(HEADS):
        rows = slice(h * CELLS, (h + 1) * CELLS)
        full = prob[rows, :].astype(FULL)
        inner = jnp.sum(dweights[rows] * full, -1, keepdims=True)
        dscores.append((full * (dweights[rows] - inner) * HEAD ** (-0.5)).astype(HALF))
    dk = dot_tn(jnp.concatenate(dscores, 0), by_head(q))
    dq = jnp.zeros((CELLS, WIDTH), FULL)
    for h in range(HEADS):
        dq = jnp.where(head_lanes(h), dot(dscores[h], k), dq)
    return dq.astype(HALF), dk.astype(HALF), dv.astype(HALF)


def gelu_parts(u):
    below = 0.5 * (1.0 + lax.erf(u * (0.5**0.5)))
    slope = below + u * (jnp.exp(-0.5 * u * u) * (2.0 * np.pi) ** (-0.5))
    return below, slope


def forward_half(x, gains, wqkv, wproj, bias, prob):
    unit, spread = normalise(x)
    hidden = (unit * gains[0:1, :]).astype(HALF)
    qkv = dot(hidden, wqkv[...]).astype(HALF)
    q, k, v = (qkv[:, n * WIDTH : (n + 1) * WIDTH] for n in range(3))
    mixed = attend(q, k, v, bias, prob)
    return (q, k, v), x + dot(mixed, wproj[...])


def backward(dflat, x, qkv, prob, resid, slope, gains, wqkv, wproj, wup, wdown):
    q, k, v = qkv
    dactive = dot(dflat, wdown[...])
    dupward = (dactive * slope).astype(HALF)
    dnormed = dot_nt(dupward, wup[...])
    unit, spread = normalise(resid)
    dresid = dflat.astype(FULL) + normalise_back(dnormed, unit, spread, gains[1:2, :])
    dmixed = dot_nt(dresid.astype(HALF), wproj[...]).astype(HALF)
    dq, dk, dv = attend_back(dmixed, q, k, v, prob)
    dhidden = dot_nt(dq, wqkv[:, :WIDTH])
    dhidden = dhidden + dot_nt(dk, wqkv[:, WIDTH : 2 * WIDTH])
    dhidden = dhidden + dot_nt(dv, wqkv[:, 2 * WIDTH :])
    unit, spread = normalise(x)
    return dresid + normalise_back(dhidden, unit, spread, gains[0:1, :])


def gather_patches(upper, surface, section, select, ff, ft):
    base = 4 * section - 2
    for z in range(2):
        for a in range(2):
            level = jnp.maximum(base + 2 * z + a, 0)
            for v in range(5):
                field = upper[v, level].astype(FULL)
                if z == 0:
                    field = jnp.where(section == 0, 0.0, field)
                slot = (z * 2 + a) * 5 + v
                ff[slot * 24 : slot * 24 + 24, 0:48] = field
    for v in range(4):
        field = jnp.where(section == 0, surface[v].astype(FULL), 0.0)
        ff[(20 + v) * 24 : (21 + v) * 24, 0:48] = field
    pad = jnp.zeros((8, 128), FULL)
    for i in range(6):
        pieces = []
        for b in range(4):
            pieces += [ff[pl.ds(4 * i + b, 24, stride=24), :], pad]
        ft[i * 48 : i * 48 + 48, :] = jnp.concatenate(pieces, 0).T[:48]
    raw = [ft[pl.ds(c, 72, stride=4), :].astype(HALF) for c in range(4)]
    both = dot(jnp.concatenate(raw, 1), select[...])
    return jnp.concatenate((both[:, :256], both[:, 256:]), 0).astype(HALF)


def flag(axis):
    last = lax.axis_index(axis) == lax.axis_size(axis) - 1
    return jnp.where(last, 1.0, 0.0)


def table_rows(tbl, block, table):
    for h in range(HEADS):
        table[h : h + 1, 0 : tbl.shape[-1]] = tbl[block * HEADS + h]


def first_kernel(*refs):
    names = (
        "tbl", "upper", "surface", "to_inner", "uembed", "sembed", "gains",
        "wqkv", "wproj", "wup", "wdown", "cot", "out_first", "out_cot",
    )
    count = len(names)
    source, refs = refs[:count], refs[count:]
    patch_o, x_o, qkv_o, prob, resid_o, slope_o, send_o, *keep_o = refs[:11]
    refs = refs[11:]
    local, refs = refs[:count], refs[count:]
    ff, ft, emb, cots, table, xs, bias, cols, select, sems = refs
    copies = {}
    for n, name in enumerate(names):
        start, end = source[n], local[n]
        if name[0] == "w":
            start = start.at[0]
        elif name == "tbl":
            start = start.at[pl.ds(0, HEADS)]
        elif name == "uembed":
            end = emb.at[pl.ds(0, 160)]
        elif name == "sembed":
            end = emb.at[pl.ds(160, 64)]
        copies[name] = pltpu.make_async_copy(start, end, sems.at[n])
        copies[name].start()
    have = dict(zip(names, local))

    def wait(*which):
        for name in which:
            copies[name].wait()

    emb[224:256, :] = jnp.zeros((32, WIDTH), HALF)
    fill_columns(cols)
    fill_select(select)
    wait("tbl", "upper", "surface", "to_inner", "uembed", "sembed", "gains", "wqkv")
    table_rows(have["tbl"], 0, table)
    build_bias(table, cols, xs, bias, None)
    section = lax.axis_index("section")
    patch = gather_patches(have["upper"], have["surface"], section, select, ff, ft)
    patch = dot(have["to_inner"][...], patch).astype(HALF)
    patch_o[...] = patch
    latent = dot(patch, emb[...]).astype(HALF)
    x_o[...] = latent
    x = latent.astype(FULL)
    gains = have["gains"].at[0]
    wait("wproj", "wup", "wdown", "cot", "out_first", "out_cot")
    cot = have["cot"]
    for a in range(6):
        for o in range(12):
            cots[(a * 12 + o) * 2 : (a * 12 + o) * 2 + 2, :] = cot[a, o].astype(FULL)
    ready = dot(have["out_cot"][...], cots[...].astype(HALF))
    qkv, resid = forward_half(x, gains, have["wqkv"], have["wproj"], bias, prob)
    for n in range(3):
        qkv_o[n] = qkv[n]
    resid_o[...] = resid
    unit, spread = normalise(resid)
    normed = (unit * gains[1:2, :]).astype(HALF)
    upward = dot(normed, have["wup"][...])
    below, slope = gelu_parts(upward)
    slope_o[...] = slope.astype(HALF)
    active = (upward * below).astype(HALF)
    result = (resid + dot_nt(active, have["wdown"][...])).astype(HALF)
    moved = (dot(have["out_first"][...], result) + ready).astype(HALF)
    send_o[...] = moved[192:]
    for n in range(4):
        keep_o[n][...] = moved[n * 48 : n * 48 + 48]


def second_bias(tbl, after, bias, table, xs, cols):
    fill_columns(cols)
    table_rows(tbl, 1, table)
    build_bias(table, cols, xs, bias, (flag("section"), flag("lat")))


def second_kernel(*refs):
    parts, rest = refs[:4], refs[4:]
    gains, wqkv, wproj, wup, wdown, bias, into, out_of, send_o = rest[:9]
    keep, stack, prob = rest[9:13], rest[13], rest[14]
    for n in range(4):
        stack[n * 96 : n * 96 + 96, :] = parts[n][...]
    both = dot(into[...], stack[...])
    x, dflat = both[:CELLS], both[CELLS:].astype(HALF)
    gains, wqkv, wproj, wup, wdown = (w.at[1] for w in (gains, wqkv, wproj, wup, wdown))
    qkv, resid = forward_half(x, gains, wqkv, wproj, bias, prob)
    unit, spread = normalise(resid)
    normed = (unit * gains[1:2, :]).astype(HALF)
    upward = dot(normed, wup[...])
    slope = gelu_parts(upward)[1]
    dx = backward(dflat, x, qkv, prob, resid, slope, gains, wqkv, wproj, wup, wdown)
    moved = dot(out_of[...], dx.astype(HALF)).astype(HALF)
    send_o[...] = moved[128:]
    for n in range(4):
        keep[n][...] = moved[n * 32 : n * 32 + 32]


def third_kernel(*refs):
    parts, rest = refs[:4], refs[4:]
    gains, wqkv, wproj, wup, wdown, patch, x_i, qkv_i, prob, resid, slope, into, out_of = rest[:13]
    grad_o, mine_o, other_o, stack, terms = rest[13:]
    for n in range(4):
        stack[n * 64 : n * 64 + 64, :] = parts[n][...]
    dflat = dot(into[...], stack[...]).astype(HALF)
    qkv = tuple(qkv_i[n] for n in range(3))
    gains, wqkv, wproj, wup, wdown = (w.at[0] for w in (gains, wqkv, wproj, wup, wdown))
    dx = backward(
        dflat, x_i[...].astype(FULL), qkv, prob, resid[...], slope[...].astype(FULL),
        gains, wqkv, wproj, wup, wdown,
    )
    grad = dx.astype(HALF)
    moved = dot(out_of[...], grad).astype(HALF)
    for z in range(2):
        for a in range(6):
            grad_o[z, a] = moved[(z * 6 + a) * 16 : (z * 6 + a) * 16 + 12]
    total = dot_tn(patch[...], grad)
    terms[0:224, :] = total[:224, :128]
    terms[224:336, :] = jnp.concatenate((total[:112, 128:], total[112:224, 128:]), 1)
    place = lax.axis_index("section") % 2
    mine_o[...] = terms[pl.ds(pl.multiple_of(place * 168, 8), 168), :].astype(HALF)
    other_o[...] = terms[pl.ds(pl.multiple_of(168 - place * 168, 8), 168), :].astype(HALF)


vmem = pl.BlockSpec(memory_space=pltpu.VMEM)
hbm = pl.BlockSpec(memory_space=pltpu.HBM)


def call(kernel, outs, scratch, *args, spec=vmem, out=vmem, room=30, size=1):
    return pl.pallas_call(
        kernel,
        out_shape=outs,
        in_specs=[spec for a in args],
        out_specs=jax.tree.map(lambda _: out, outs),
        scratch_shapes=scratch,
        compiler_params=pltpu.CompilerParams(vmem_limit_bytes=room * 2**20),
        cost_estimate=pl.CostEstimate(flops=1000000, bytes_accessed=size * 1000000, transcendentals=0),
    )(*args)


def shape(dims, dtype=HALF):
    return jax.ShapeDtypeStruct(dims, dtype)


def fetch(block, steps):
    names = ("lon", "lat", "section")
    axes = [name for name in names if steps.get(name, 0)]
    if not axes:
        return block
    sizes = [lax.axis_size(name) for name in axes]
    pairs = []
    for place in np.ndindex(*sizes):
        source = [(p + steps[name]) % n for p, name, n in zip(place, axes, sizes)]
        pairs.append(
            (int(np.ravel_multi_index(source, sizes)), int(np.ravel_multi_index(place, sizes)))
        )
    return lax.ppermute(block, tuple(axes), pairs)


def exchange(keep, got, way):
    pitch = got.shape[0] // 4
    blocks = []
    for n in range(4):
        block = jnp.concatenate((keep[n], got[n * pitch : (n + 1) * pitch]), 0)
        blocks.append(fetch(block, {"lat": way * (n // 2), "lon": way * (n % 2)}))
    return blocks


def swap(block, flips):
    names = ("lon", "lat", "section")
    axes = [name for name in names if flips.get(name, 0)]
    sizes = [lax.axis_size(name) for name in axes]
    pairs = []
    for place in np.ndindex(*sizes):
        source = [p ^ flips[name] for p, name in zip(place, axes)]
        pairs.append(
            (int(np.ravel_multi_index(source, sizes)), int(np.ravel_multi_index(place, sizes)))
        )
    return lax.ppermute(block, tuple(axes), pairs)


def add_up(mine, other):
    total = (mine.astype(FULL) + swap(other, {"section": 1}).astype(FULL)).astype(HALF)
    bits = []
    for name in ("section", "lat", "lon"):
        size = lax.axis_size(name)
        if size & (size - 1) or size < 2:
            raise ValueError("axis size")
        bits += [(name, 1 << n) for n in range(name == "section", size.bit_length() - 1)]
    for n in range(0, len(bits), 2):
        pair = [{name: bit} for name, bit in bits[n : n + 2]]
        if len(pair) == 1:
            total = total.astype(FULL) + swap(total, pair[0]).astype(FULL)
        else:
            one, two = pair
            three = dict(one)
            for name, bit in two.items():
                three[name] = three.get(name, 0) | bit
            near, far, last = (swap(total, step).astype(FULL) for step in (one, two, three))
            total = (total.astype(FULL) + near) + (far + last)
        total = total.astype(HALF)
    return total, swap(total, {"section": 1})


def last_kernel(scale, mine, other, upper_o, surface_o, halves, both, sems):
    place = lax.axis_index("section") % 2
    halves[pl.ds(pl.multiple_of(place * 168, 8), 168), :] = mine[...].astype(FULL) * scale
    halves[pl.ds(pl.multiple_of(168 - place * 168, 8), 168), :] = other[...].astype(FULL) * scale
    both[:, 0:128] = halves[0:224, :]
    last = halves[224:336, :]
    both[0:112, 128:192] = last[:, :64]
    both[112:224, 128:192] = last[:, 64:]
    copies = [
        pltpu.make_async_copy(both.at[pl.ds(0, 160)], upper_o, sems.at[0]),
        pltpu.make_async_copy(both.at[pl.ds(160, 64)], surface_o, sems.at[1]),
    ]
    for copy in copies:
        copy.start()
    for copy in copies:
        copy.wait()


def on_device(
    upper_fields,
    surface_fields,
    upper_embed,
    surface_embed,
    norm_gains,
    qkv_weight,
    proj_weight,
    up_weight,
    down_weight,
    earth_bias,
    out_grad,
):
    sections, bands = lax.axis_size("section"), lax.axis_size("lat")
    levels, rows, columns, width = out_grad.shape
    positions = earth_bias.shape[-1]
    table = earth_bias.transpose(0, 1, 3, 2, 4).reshape(2 * HEADS, 1, positions)
    weights = (norm_gains, qkv_weight, proj_weight, up_weight, down_weight.transpose(0, 2, 1))

    def from_cot(z, a, o):
        return (a * 12 + o) * 2 + z

    operands = (
        table, upper_fields, surface_fields, jnp.asarray(natural_to_inner()), upper_embed,
        surface_embed, *weights, out_grad.transpose(1, 2, 0, 3),
        jnp.asarray(octants_out(48, 0, True, inner_row)),
        jnp.asarray(octants_out(48, 18, True, from_cot)),
    )
    local = [
        pltpu.VMEM(v.shape[1:] if 7 <= n < 11 else v.shape, v.dtype) for n, v in enumerate(operands)
    ]
    local[0] = pltpu.VMEM((HEADS, 1, positions), FULL)
    local[4] = local[5] = pltpu.VMEM((16, 128), HALF)
    scratch_bias = [pltpu.VMEM((8, 3328), FULL), pltpu.VMEM((4, CELLS, 128), FULL)]
    scratch_cols = pltpu.VMEM((2, 256, 384), HALF)
    held = [
        shape((CELLS, 256)),
        shape((CELLS, WIDTH)),
        shape((3, CELLS, WIDTH)),
        shape((HEADS * CELLS, CELLS)),
        shape((CELLS, WIDTH), FULL),
        shape((CELLS, 4 * WIDTH)),
    ]
    patch, x, qkv, prob, resid, slope, send, *keep = call(
        first_kernel,
        held + [shape((192, WIDTH))] + [shape((48, WIDTH))] * 4,
        local
        + [
            pltpu.VMEM((576, 128), FULL),
            pltpu.VMEM((288, 128), FULL),
            pltpu.VMEM((256, WIDTH), HALF),
            pltpu.VMEM((CELLS, WIDTH), FULL),
        ]
        + scratch_bias
        + [
            pltpu.VMEM((HEADS * CELLS, CELLS), FULL),
            scratch_cols,
            pltpu.VMEM((512, 512), HALF),
            pltpu.SemaphoreType.DMA((len(operands),)),
        ],
        *(pltpu.with_memory_space_constraint(v, pltpu.HBM) for v in operands),
        spec=hbm,
    )
    bias_shape = shape((HEADS * CELLS, CELLS), FULL)
    got = fetch(send, {"section": 1})
    bias = call(second_bias, bias_shape, [*scratch_bias, scratch_cols], table, got)
    into = np.concatenate((octants_in(48, 0, False), octants_in(48, 18, False)), 0)
    send, *keep = call(
        second_kernel,
        [shape((128, WIDTH))] + [shape((32, WIDTH))] * 4,
        [pltpu.VMEM((8 * 48, WIDTH), HALF), pltpu.VMEM((HEADS * CELLS, CELLS), HALF)],
        *exchange(keep, got, 1), *weights, bias,
        jnp.asarray(into), jnp.asarray(octants_out(32, 0, False, inner_row)),
    )
    latent_grad, mine, other = call(
        third_kernel,
        [shape((2, 6, 12, WIDTH)), shape((168, 128)), shape((168, 128))],
        [pltpu.VMEM((8 * 32, WIDTH), HALF), pltpu.VMEM((336, 128), FULL)],
        *exchange(keep, fetch(send, {"section": -1}), -1), *weights, patch, x, qkv, prob, resid, slope,
        jnp.asarray(octants_in(32, 0, True)), jnp.asarray(inner_to_padded()),
    )
    scale = float(levels * sections * rows * bands * columns * lax.axis_size("lon")) ** (-0.5)
    upper_grad, surface_grad = call(
        functools.partial(last_kernel, scale),
        [shape((160, WIDTH), FULL), shape((64, WIDTH), FULL)],
        [
            pltpu.VMEM((336, 128), FULL),
            pltpu.VMEM((224, WIDTH), FULL),
            pltpu.SemaphoreType.DMA((2,)),
        ],
        *add_up(mine, other),
        out=hbm,
    )
    return (latent_grad, upper_grad, surface_grad)


def solution(mesh):
    placed = (
        P(None, None, "lat", "lon"),
        P(None, "lat", "lon"),
        P(),
        P(),
        P(),
        P(),
        P(),
        P(),
        P(),
        P(None, "lat", "section", None, None),
        P("section", "lat", "lon", None),
    )
    return jax.shard_map(
        on_device,
        mesh=mesh,
        in_specs=placed,
        out_specs=(P("section", "lat", "lon", None), P(), P()),
        check_vma=False,
    )
```

```python
import functools

import jax
import jax.numpy as jnp
import ml_dtypes
import numpy as np
from jax import lax
from jax.experimental import pallas as pl
from jax.experimental.pallas import tpu as pltpu
from jax.sharding import PartitionSpec as P

neg_fill = -1e30
norm_eps = 1e-05
HEADS = 6
HEAD = 32
CELLS = 144
WIDTH = 192
FULL = jnp.float32
HALF = jnp.bfloat16


def inner_row(z, a, o):
    return o * 12 + z * 6 + a


def octant_of(z, a, o):
    return (z * 4 + (a // 3) * 2 + o // 6, (a % 3) * 6 + o % 6)


def as_half(array):
    return array.astype(ml_dtypes.bfloat16)


def cells():
    return [(z, a, o) for z in range(2) for a in range(6) for o in range(12)]


def natural_to_inner():
    move = np.zeros((CELLS, CELLS), np.float32)
    for z, a, o in cells():
        move[inner_row(z, a, o), (z * 6 + a) * 12 + o] = 1
    return as_half(move)


def inner_to_padded():
    move = np.zeros((192, CELLS), np.float32)
    for z, a, o in cells():
        move[(z * 6 + a) * 16 + o, inner_row(z, a, o)] = 1
    return as_half(move)


def octants_out(pitch, first, flip, source):
    move = np.zeros((8 * pitch, CELLS), np.float32)
    for z, a, o in cells():
        part, place = octant_of(z, a, o)
        move[(7 - part if flip else part) * pitch + first + place, source(z, a, o)] = 1
    return as_half(move)


def octants_in(pitch, first, flip):
    move = np.zeros((CELLS, 8 * pitch), np.float32)
    for z, a, o in cells():
        part, place = octant_of(z, a, o)
        part = 7 - part if flip else part
        block = (part % 4) * 2 + part // 4
        move[inner_row(z, a, o), block * pitch + first + place] = 1
    return as_half(move)


def whole_part(v, size):
    return jnp.floor((v + 0.5) * (1.0 / size))


def one_hot(target, lanes):
    lane = lax.broadcasted_iota(jnp.int32, (1, lanes), 1).astype(FULL)
    return jnp.where(lane == target, 1.0, 0.0).astype(HALF)


def fill_columns(cols):
    row = lax.broadcasted_iota(jnp.int32, (256, 1), 0).astype(FULL)
    a = whole_part(row, 23)
    k = row - 23.0 * a
    for z in range(2):
        target = (22.0 - k) * 12.0 + (z * 6.0) + a
        cols[z] = one_hot(jnp.where(row < 138.0, target, -1.0), 384)


def fill_select(select):
    row = lax.broadcasted_iota(jnp.int32, (128, 1), 0).astype(FULL)
    b = whole_part(row, 32)
    slot = row - 32.0 * b
    layer = whole_part(slot, 5)
    z = whole_part(layer, 2)
    upper = z * 256.0 + (slot - 5.0 * layer) * 32.0 + (layer - 2.0 * z) * 16.0
    surface = 160.0 + (slot - 20.0) * 16.0
    target = jnp.where(slot < 20.0, upper, surface) + b * 4.0
    for c in range(4):
        select[c * 128 : c * 128 + 128, :] = one_hot(
            jnp.where(slot < 24.0, target + float(c), -1.0), 512
        )


def dot(a, b):
    return jnp.dot(a, b, preferred_element_type=FULL)


def dot_nt(a, b):
    return lax.dot_general(a, b, (((1,), (1,)), ((), ())), preferred_element_type=FULL)


def dot_tn(a, b):
    return lax.dot_general(a, b, (((0,), (0,)), ((), ())), preferred_element_type=FULL)


def normalise(v):
    mean = jnp.mean(v, -1, keepdims=True)
    centred = v - mean
    spread = lax.rsqrt(jnp.mean(centred * centred, -1, keepdims=True) + norm_eps)
    return centred * spread, spread


def normalise_back(dy, unit, spread, gain):
    dunit = dy * gain
    inner = jnp.mean(dunit * unit, -1, keepdims=True)
    return spread * (dunit - jnp.mean(dunit, -1, keepdims=True) - unit * inner)


def head_lanes(h):
    lane = lax.broadcasted_iota(jnp.int32, (1, WIDTH), 1)
    return (lane >= h * HEAD) & (lane < (h + 1) * HEAD)


def head_mask(h):
    return jnp.where(head_lanes(h), 1.0, 0.0).astype(HALF)


def build_bias(tbl, cols, xs, bias, edges):
    for z in range(2):
        for a in range(6):
            for zu in range(2):
                start = ((z * 2 + zu) * 6 + a) * 138
                piece = tbl[0:HEADS, start : start + 138]
                piece = jnp.concatenate((piece, jnp.zeros((HEADS, 118), FULL)), 1)
                for p in range(2):
                    for half in range(2):
                        xs[zu * 2 + half, pl.ds(p * 12 + z * 6 + a, HEADS, stride=24), :] = piece[
                            :, half * 128 : half * 128 + 128
                        ]
    total = None
    for zu in range(2):
        x = jnp.concatenate((xs[zu * 2], xs[zu * 2 + 1]), 1)
        high = x.astype(HALF)
        left = x - high.astype(FULL)
        mid = left.astype(HALF)
        low = (left - mid.astype(FULL)).astype(HALF)
        term = dot(jnp.concatenate((high, mid, low), 0), cols[zu])
        total = term if total is None else total + term
    table = total[:CELLS] + total[CELLS : 2 * CELLS] + total[2 * CELLS :]
    row = lax.broadcasted_iota(jnp.int32, (CELLS, 1), 0).astype(FULL)
    lane = lax.broadcasted_iota(jnp.int32, (1, CELLS), 1).astype(FULL)

    part = whole_part
    even = part(row, 12) - 2.0 * part(part(row, 12), 2) == 0.0
    table = jnp.where(even, pltpu.roll(table, 384 - 12, 1), table)
    if edges is not None:
        last_section, last_band = edges
        row12, lane12 = row - 12.0 * part(row, 12), lane - 12.0 * part(lane, 12)
        row_z, lane_z = part(row12, 6), part(lane12, 6)
        row_a, lane_a = part(row12 - 6.0 * row_z, 3), part(lane12 - 6.0 * lane_z, 3)
        apart = jnp.abs(row_z - lane_z) * last_section + jnp.abs(row_a - lane_a) * last_band
        blocked = apart > 0.5
    for j in range(6):
        shift = (10 - 2 * j) * 12
        moved = pltpu.roll(table, 384 - shift, 1) if shift else table
        moved = moved[:, :CELLS]
        if edges is not None:
            moved = jnp.where(blocked, neg_fill, moved)
        for h in range(HEADS):
            bias[h * CELLS + j * 24 : h * CELLS + j * 24 + 24, :] = moved[h * 24 : h * 24 + 24, :]


def by_head(rows):
    return jnp.concatenate([rows * head_mask(h) for h in range(HEADS)], 0)


def attend(q, k, v, bias, prob):
    scores = dot_nt(by_head(q), k)
    for h in range(HEADS):
        rows = slice(h * CELLS, (h + 1) * CELLS)
        score = scores[rows] * HEAD ** (-0.5) + bias[rows, :]
        expo = jnp.exp(score - jnp.max(score, -1, keepdims=True))
        prob[rows, :] = (expo * (1.0 / jnp.sum(expo, -1, keepdims=True))).astype(HALF)
    mixed = jnp.zeros((CELLS, WIDTH), FULL)
    for h in range(HEADS):
        term = dot(prob[h * CELLS : (h + 1) * CELLS, :], v)
        mixed = jnp.where(head_lanes(h), term, mixed)
    return mixed.astype(HALF)


def attend_back(dmixed, q, k, v, prob):
    dheads = by_head(dmixed)
    dweights = dot_nt(dheads, v)
    dv = dot_tn(prob[...], dheads)
    dscores = []
    for h in range(HEADS):
        rows = slice(h * CELLS, (h + 1) * CELLS)
        full = prob[rows, :].astype(FULL)
        inner = jnp.sum(dweights[rows] * full, -1, keepdims=True)
        dscores.append((full * (dweights[rows] - inner) * HEAD ** (-0.5)).astype(HALF))
    dk = dot_tn(jnp.concatenate(dscores, 0), by_head(q))
    dq = jnp.zeros((CELLS, WIDTH), FULL)
    for h in range(HEADS):
        dq = jnp.where(head_lanes(h), dot(dscores[h], k), dq)
    return dq.astype(HALF), dk.astype(HALF), dv.astype(HALF)


def gelu_parts(u):
    below = 0.5 * (1.0 + lax.erf(u * (0.5**0.5)))
    slope = below + u * (jnp.exp(-0.5 * u * u) * (2.0 * np.pi) ** (-0.5))
    return below, slope


def forward_half(x, gains, wqkv, wproj, bias, prob):
    unit, spread = normalise(x)
    hidden = (unit * gains[0:1, :]).astype(HALF)
    qkv = dot(hidden, wqkv[...]).astype(HALF)
    q, k, v = (qkv[:, n * WIDTH : (n + 1) * WIDTH] for n in range(3))
    mixed = attend(q, k, v, bias, prob)
    return (q, k, v), x + dot(mixed, wproj[...])


def backward(dflat, x, qkv, prob, resid, slope, gains, wqkv, wproj, wup, wdown):
    q, k, v = qkv
    dactive = dot(dflat, wdown[...])
    dupward = (dactive * slope).astype(HALF)
    dnormed = dot_nt(dupward, wup[...])
    unit, spread = normalise(resid)
    dresid = dflat.astype(FULL) + normalise_back(dnormed, unit, spread, gains[1:2, :])
    dmixed = dot_nt(dresid.astype(HALF), wproj[...]).astype(HALF)
    dq, dk, dv = attend_back(dmixed, q, k, v, prob)
    dhidden = dot_nt(dq, wqkv[:, :WIDTH])
    dhidden = dhidden + dot_nt(dk, wqkv[:, WIDTH : 2 * WIDTH])
    dhidden = dhidden + dot_nt(dv, wqkv[:, 2 * WIDTH :])
    unit, spread = normalise(x)
    return dresid + normalise_back(dhidden, unit, spread, gains[0:1, :])


def gather_patches(upper, surface, section, select, ff, ft):
    base = 4 * section - 2
    for z in range(2):
        for a in range(2):
            level = jnp.maximum(base + 2 * z + a, 0)
            for v in range(5):
                field = upper[v, level].astype(FULL)
                if z == 0:
                    field = jnp.where(section == 0, 0.0, field)
                slot = (z * 2 + a) * 5 + v
                ff[slot * 24 : slot * 24 + 24, 0:48] = field
    for v in range(4):
        field = jnp.where(section == 0, surface[v].astype(FULL), 0.0)
        ff[(20 + v) * 24 : (21 + v) * 24, 0:48] = field
    pad = jnp.zeros((8, 128), FULL)
    for i in range(6):
        pieces = []
        for b in range(4):
            pieces += [ff[pl.ds(4 * i + b, 24, stride=24), :], pad]
        ft[i * 48 : i * 48 + 48, :] = jnp.concatenate(pieces, 0).T[:48]
    raw = [ft[pl.ds(c, 72, stride=4), :].astype(HALF) for c in range(4)]
    both = dot(jnp.concatenate(raw, 1), select[...])
    return jnp.concatenate((both[:, :256], both[:, 256:]), 0).astype(HALF)


def flag(axis):
    last = lax.axis_index(axis) == lax.axis_size(axis) - 1
    return jnp.where(last, 1.0, 0.0)


def table_rows(tbl, block, table):
    for h in range(HEADS):
        table[h : h + 1, 0 : tbl.shape[-1]] = tbl[block * HEADS + h]


def first_kernel(*refs):
    names = (
        "tbl", "upper", "surface", "to_inner", "uembed", "sembed", "gains",
        "wqkv", "wproj", "wup", "wdown", "cot", "out_first", "out_cot",
    )
    count = len(names)
    source, refs = refs[:count], refs[count:]
    patch_o, x_o, qkv_o, prob, resid_o, slope_o, send_o, *keep_o = refs[:11]
    refs = refs[11:]
    local, refs = refs[:count], refs[count:]
    ff, ft, emb, cots, table, xs, bias, cols, select, sems = refs
    copies = {}
    for n, name in enumerate(names):
        start, end = source[n], local[n]
        if name[0] == "w":
            start = start.at[0]
        elif name == "tbl":
            start = start.at[pl.ds(0, HEADS)]
        elif name == "uembed":
            end = emb.at[pl.ds(0, 160)]
        elif name == "sembed":
            end = emb.at[pl.ds(160, 64)]
        copies[name] = pltpu.make_async_copy(start, end, sems.at[n])
        copies[name].start()
    have = dict(zip(names, local))

    def wait(*which):
        for name in which:
            copies[name].wait()

    emb[224:256, :] = jnp.zeros((32, WIDTH), HALF)
    fill_columns(cols)
    fill_select(select)
    wait("tbl", "upper", "surface", "to_inner", "uembed", "sembed", "gains", "wqkv")
    table_rows(have["tbl"], 0, table)
    build_bias(table, cols, xs, bias, None)
    section = lax.axis_index("section")
    patch = gather_patches(have["upper"], have["surface"], section, select, ff, ft)
    patch = dot(have["to_inner"][...], patch).astype(HALF)
    patch_o[...] = patch
    latent = dot(patch, emb[...]).astype(HALF)
    x_o[...] = latent
    x = latent.astype(FULL)
    gains = have["gains"].at[0]
    wait("wproj", "wup", "wdown", "cot", "out_first", "out_cot")
    cot = have["cot"]
    for a in range(6):
        for o in range(12):
            cots[(a * 12 + o) * 2 : (a * 12 + o) * 2 + 2, :] = cot[a, o].astype(FULL)
    ready = dot(have["out_cot"][...], cots[...].astype(HALF))
    qkv, resid = forward_half(x, gains, have["wqkv"], have["wproj"], bias, prob)
    for n in range(3):
        qkv_o[n] = qkv[n]
    resid_o[...] = resid
    unit, spread = normalise(resid)
    normed = (unit * gains[1:2, :]).astype(HALF)
    upward = dot(normed, have["wup"][...])
    below, slope = gelu_parts(upward)
    slope_o[...] = slope.astype(HALF)
    active = (upward * below).astype(HALF)
    result = (resid + dot_nt(active, have["wdown"][...])).astype(HALF)
    moved = (dot(have["out_first"][...], result) + ready).astype(HALF)
    send_o[...] = moved[192:]
    for n in range(4):
        keep_o[n][...] = moved[n * 48 : n * 48 + 48]


def second_bias(tbl, after, bias, table, xs, cols):
    fill_columns(cols)
    table_rows(tbl, 1, table)
    build_bias(table, cols, xs, bias, (flag("section"), flag("lat")))


def second_kernel(*refs):
    parts, rest = refs[:4], refs[4:]
    gains, wqkv, wproj, wup, wdown, bias, into, out_of, send_o = rest[:9]
    keep, stack, prob = rest[9:13], rest[13], rest[14]
    for n, part in zip(order, parts):
        stack[n * 96 : n * 96 + 96, :] = part[...]
    both = dot(into[...], stack[...])
    x, dflat = both[:CELLS], both[CELLS:].astype(HALF)
    gains, wqkv, wproj, wup, wdown = (w.at[1] for w in (gains, wqkv, wproj, wup, wdown))
    qkv, resid = forward_half(x, gains, wqkv, wproj, bias, prob)
    unit, spread = normalise(resid)
    normed = (unit * gains[1:2, :]).astype(HALF)
    upward = dot(normed, wup[...])
    slope = gelu_parts(upward)[1]
    dx = backward(dflat, x, qkv, prob, resid, slope, gains, wqkv, wproj, wup, wdown)
    moved = dot(out_of[...], dx.astype(HALF)).astype(HALF)
    send_o[...] = moved[128:]
    for n in range(4):
        keep[n][...] = moved[n * 32 : n * 32 + 32]


def third_kernel(*refs):
    parts, rest = refs[:4], refs[4:]
    gains, wqkv, wproj, wup, wdown, patch, x_i, qkv_i, prob, resid, slope, into, out_of = rest[:13]
    grad_o, mine_o, other_o, stack, terms = rest[13:]
    for n, part in zip(order, parts):
        stack[n * 64 : n * 64 + 64, :] = part[...]
    dflat = dot(into[...], stack[...]).astype(HALF)
    qkv = tuple(qkv_i[n] for n in range(3))
    gains, wqkv, wproj, wup, wdown = (w.at[0] for w in (gains, wqkv, wproj, wup, wdown))
    dx = backward(
        dflat, x_i[...].astype(FULL), qkv, prob, resid[...], slope[...].astype(FULL),
        gains, wqkv, wproj, wup, wdown,
    )
    grad = dx.astype(HALF)
    moved = dot(out_of[...], grad).astype(HALF)
    for z in range(2):
        for a in range(6):
            grad_o[z, a] = moved[(z * 6 + a) * 16 : (z * 6 + a) * 16 + 12]
    total = dot_tn(patch[...], grad)
    terms[0:224, :] = total[:224, :128]
    terms[224:336, :] = jnp.concatenate((total[:112, 128:], total[112:224, 128:]), 1)
    place = lax.axis_index("section") % 2
    mine_o[...] = terms[pl.ds(pl.multiple_of(place * 168, 8), 168), :].astype(HALF)
    other_o[...] = terms[pl.ds(pl.multiple_of(168 - place * 168, 8), 168), :].astype(HALF)


vmem = pl.BlockSpec(memory_space=pltpu.VMEM)
hbm = pl.BlockSpec(memory_space=pltpu.HBM)


def call(kernel, outs, scratch, *args, spec=vmem, out=vmem, room=30, size=1):
    return pl.pallas_call(
        kernel,
        out_shape=outs,
        in_specs=[spec for a in args],
        out_specs=jax.tree.map(lambda _: out, outs),
        scratch_shapes=scratch,
        compiler_params=pltpu.CompilerParams(vmem_limit_bytes=room * 2**20),
        cost_estimate=pl.CostEstimate(flops=1000000, bytes_accessed=size * 1000000, transcendentals=0),
    )(*args)


def shape(dims, dtype=HALF):
    return jax.ShapeDtypeStruct(dims, dtype)


def fetch(block, steps):
    names = ("lon", "lat", "section")
    axes = [name for name in names if steps.get(name, 0)]
    if not axes:
        return block
    sizes = [lax.axis_size(name) for name in axes]
    pairs = []
    for place in np.ndindex(*sizes):
        source = [(p + steps[name]) % n for p, name, n in zip(place, axes, sizes)]
        pairs.append(
            (int(np.ravel_multi_index(source, sizes)), int(np.ravel_multi_index(place, sizes)))
        )
    return lax.ppermute(block, tuple(axes), pairs)


order = (3, 1, 2, 0)


def exchange(keep, got, way):
    pitch = got.shape[0] // 4
    blocks = []
    for n in order:
        block = jnp.concatenate((keep[n], got[n * pitch : (n + 1) * pitch]), 0)
        blocks.append(fetch(block, {"lat": way * (n // 2), "lon": way * (n % 2)}))
    return blocks


def swap(block, flips):
    names = ("lon", "lat", "section")
    axes = [name for name in names if flips.get(name, 0)]
    sizes = [lax.axis_size(name) for name in axes]
    pairs = []
    for place in np.ndindex(*sizes):
        source = [p ^ flips[name] for p, name in zip(place, axes)]
        pairs.append(
            (int(np.ravel_multi_index(source, sizes)), int(np.ravel_multi_index(place, sizes)))
        )
    return lax.ppermute(block, tuple(axes), pairs)


def add_up(mine, other):
    total = (mine.astype(FULL) + swap(other, {"section": 1}).astype(FULL)).astype(HALF)
    bits = []
    for name in ("section", "lat", "lon"):
        size = lax.axis_size(name)
        if size & (size - 1) or size < 2:
            raise ValueError("axis size")
        bits += [(name, 1 << n) for n in range(name == "section", size.bit_length() - 1)]
    for n in range(0, len(bits), 2):
        pair = [{name: bit} for name, bit in bits[n : n + 2]]
        if len(pair) == 1:
            total = total.astype(FULL) + swap(total, pair[0]).astype(FULL)
        else:
            one, two = pair
            three = dict(one)
            for name, bit in two.items():
                three[name] = three.get(name, 0) | bit
            near, far, last = (swap(total, step).astype(FULL) for step in (one, two, three))
            total = (total.astype(FULL) + near) + (far + last)
        total = total.astype(HALF)
    return total, swap(total, {"section": 1})


def last_kernel(scale, mine, other, upper_o, surface_o, halves, both, sems):
    place = lax.axis_index("section") % 2
    halves[pl.ds(pl.multiple_of(place * 168, 8), 168), :] = mine[...].astype(FULL) * scale
    halves[pl.ds(pl.multiple_of(168 - place * 168, 8), 168), :] = other[...].astype(FULL) * scale
    both[:, 0:128] = halves[0:224, :]
    last = halves[224:336, :]
    both[0:112, 128:192] = last[:, :64]
    both[112:224, 128:192] = last[:, 64:]
    copies = [
        pltpu.make_async_copy(both.at[pl.ds(0, 160)], upper_o, sems.at[0]),
        pltpu.make_async_copy(both.at[pl.ds(160, 64)], surface_o, sems.at[1]),
    ]
    for copy in copies:
        copy.start()
    for copy in copies:
        copy.wait()


def on_device(
    upper_fields,
    surface_fields,
    upper_embed,
    surface_embed,
    norm_gains,
    qkv_weight,
    proj_weight,
    up_weight,
    down_weight,
    earth_bias,
    out_grad,
):
    sections, bands = lax.axis_size("section"), lax.axis_size("lat")
    levels, rows, columns, width = out_grad.shape
    positions = earth_bias.shape[-1]
    table = earth_bias.transpose(0, 1, 3, 2, 4).reshape(2 * HEADS, 1, positions)
    weights = (norm_gains, qkv_weight, proj_weight, up_weight, down_weight.transpose(0, 2, 1))

    def from_cot(z, a, o):
        return (a * 12 + o) * 2 + z

    operands = (
        table, upper_fields, surface_fields, jnp.asarray(natural_to_inner()), upper_embed,
        surface_embed, *weights, out_grad.transpose(1, 2, 0, 3),
        jnp.asarray(octants_out(48, 0, True, inner_row)),
        jnp.asarray(octants_out(48, 18, True, from_cot)),
    )
    local = [
        pltpu.VMEM(v.shape[1:] if 7 <= n < 11 else v.shape, v.dtype) for n, v in enumerate(operands)
    ]
    local[0] = pltpu.VMEM((HEADS, 1, positions), FULL)
    local[4] = local[5] = pltpu.VMEM((16, 128), HALF)
    scratch_bias = [pltpu.VMEM((8, 3328), FULL), pltpu.VMEM((4, CELLS, 128), FULL)]
    scratch_cols = pltpu.VMEM((2, 256, 384), HALF)
    held = [
        shape((CELLS, 256)),
        shape((CELLS, WIDTH)),
        shape((3, CELLS, WIDTH)),
        shape((HEADS * CELLS, CELLS)),
        shape((CELLS, WIDTH), FULL),
        shape((CELLS, 4 * WIDTH)),
    ]
    patch, x, qkv, prob, resid, slope, send, *keep = call(
        first_kernel,
        held + [shape((192, WIDTH))] + [shape((48, WIDTH))] * 4,
        local
        + [
            pltpu.VMEM((576, 128), FULL),
            pltpu.VMEM((288, 128), FULL),
            pltpu.VMEM((256, WIDTH), HALF),
            pltpu.VMEM((CELLS, WIDTH), FULL),
        ]
        + scratch_bias
        + [
            pltpu.VMEM((HEADS * CELLS, CELLS), FULL),
            scratch_cols,
            pltpu.VMEM((512, 512), HALF),
            pltpu.SemaphoreType.DMA((len(operands),)),
        ],
        *(pltpu.with_memory_space_constraint(v, pltpu.HBM) for v in operands),
        spec=hbm,
    )
    bias_shape = shape((HEADS * CELLS, CELLS), FULL)
    got = fetch(send, {"section": 1})
    bias = call(second_bias, bias_shape, [*scratch_bias, scratch_cols], table, got)
    into = np.concatenate((octants_in(48, 0, False), octants_in(48, 18, False)), 0)
    send, *keep = call(
        second_kernel,
        [shape((128, WIDTH))] + [shape((32, WIDTH))] * 4,
        [pltpu.VMEM((8 * 48, WIDTH), HALF), pltpu.VMEM((HEADS * CELLS, CELLS), HALF)],
        *exchange(keep, got, 1), *weights, bias,
        jnp.asarray(into), jnp.asarray(octants_out(32, 0, False, inner_row)),
    )
    latent_grad, mine, other = call(
        third_kernel,
        [shape((2, 6, 12, WIDTH)), shape((168, 128)), shape((168, 128))],
        [pltpu.VMEM((8 * 32, WIDTH), HALF), pltpu.VMEM((336, 128), FULL)],
        *exchange(keep, fetch(send, {"section": -1}), -1), *weights, patch, x, qkv, prob, resid, slope,
        jnp.asarray(octants_in(32, 0, True)), jnp.asarray(inner_to_padded()),
    )
    scale = float(levels * sections * rows * bands * columns * lax.axis_size("lon")) ** (-0.5)
    upper_grad, surface_grad = call(
        functools.partial(last_kernel, scale),
        [shape((160, WIDTH), FULL), shape((64, WIDTH), FULL)],
        [
            pltpu.VMEM((336, 128), FULL),
            pltpu.VMEM((224, WIDTH), FULL),
            pltpu.SemaphoreType.DMA((2,)),
        ],
        *add_up(mine, other),
        out=hbm,
    )
    return (latent_grad, upper_grad, surface_grad)


def solution(mesh):
    placed = (
        P(None, None, "lat", "lon"),
        P(None, "lat", "lon"),
        P(),
        P(),
        P(),
        P(),
        P(),
        P(),
        P(),
        P(None, "lat", "section", None, None),
        P("section", "lat", "lon", None),
    )
    return jax.shard_map(
        on_device,
        mesh=mesh,
        in_specs=placed,
        out_specs=(P("section", "lat", "lon", None), P(), P()),
        check_vma=False,
    )
```

```python
import functools

import jax
import jax.numpy as jnp
import ml_dtypes
import numpy as np
from jax import lax
from jax.experimental import pallas as pl
from jax.experimental.pallas import tpu as pltpu
from jax.sharding import PartitionSpec as P

neg_fill = -1e30
norm_eps = 1e-05
HEADS = 6
HEAD = 32
CELLS = 144
WIDTH = 192
FULL = jnp.float32
HALF = jnp.bfloat16


def inner_row(z, a, o):
    return o * 12 + z * 6 + a


def octant_of(z, a, o):
    return (z * 4 + (a // 3) * 2 + o // 6, (a % 3) * 6 + o % 6)


def as_half(array):
    return array.astype(ml_dtypes.bfloat16)


def cells():
    return [(z, a, o) for z in range(2) for a in range(6) for o in range(12)]


def natural_to_inner():
    move = np.zeros((CELLS, CELLS), np.float32)
    for z, a, o in cells():
        move[inner_row(z, a, o), (z * 6 + a) * 12 + o] = 1
    return as_half(move)


def inner_to_padded():
    move = np.zeros((192, CELLS), np.float32)
    for z, a, o in cells():
        move[(z * 6 + a) * 16 + o, inner_row(z, a, o)] = 1
    return as_half(move)


def octants_out(pitch, first, flip, source):
    move = np.zeros((8 * pitch, CELLS), np.float32)
    for z, a, o in cells():
        part, place = octant_of(z, a, o)
        move[(7 - part if flip else part) * pitch + first + place, source(z, a, o)] = 1
    return as_half(move)


def octants_in(pitch, first, flip):
    move = np.zeros((CELLS, 8 * pitch), np.float32)
    for z, a, o in cells():
        part, place = octant_of(z, a, o)
        part = 7 - part if flip else part
        block = (part % 4) * 2 + part // 4
        move[inner_row(z, a, o), block * pitch + first + place] = 1
    return as_half(move)


def whole_part(v, size):
    return jnp.floor((v + 0.5) * (1.0 / size))


def one_hot(target, lanes):
    lane = lax.broadcasted_iota(jnp.int32, (1, lanes), 1).astype(FULL)
    return jnp.where(lane == target, 1.0, 0.0).astype(HALF)


def fill_columns(cols):
    row = lax.broadcasted_iota(jnp.int32, (256, 1), 0).astype(FULL)
    a = whole_part(row, 23)
    k = row - 23.0 * a
    for z in range(2):
        target = (22.0 - k) * 12.0 + (z * 6.0) + a
        cols[z] = one_hot(jnp.where(row < 138.0, target, -1.0), 384)


def fill_select(select):
    row = lax.broadcasted_iota(jnp.int32, (128, 1), 0).astype(FULL)
    b = whole_part(row, 32)
    slot = row - 32.0 * b
    layer = whole_part(slot, 5)
    z = whole_part(layer, 2)
    upper = z * 256.0 + (slot - 5.0 * layer) * 32.0 + (layer - 2.0 * z) * 16.0
    surface = 160.0 + (slot - 20.0) * 16.0
    target = jnp.where(slot < 20.0, upper, surface) + b * 4.0
    for c in range(4):
        select[c * 128 : c * 128 + 128, :] = one_hot(
            jnp.where(slot < 24.0, target + float(c), -1.0), 512
        )


def dot(a, b):
    return jnp.dot(a, b, preferred_element_type=FULL)


def dot_nt(a, b):
    return lax.dot_general(a, b, (((1,), (1,)), ((), ())), preferred_element_type=FULL)


def dot_tn(a, b):
    return lax.dot_general(a, b, (((0,), (0,)), ((), ())), preferred_element_type=FULL)


def normalise(v):
    mean = jnp.mean(v, -1, keepdims=True)
    centred = v - mean
    spread = lax.rsqrt(jnp.mean(centred * centred, -1, keepdims=True) + norm_eps)
    return centred * spread, spread


def normalise_back(dy, unit, spread, gain):
    dunit = dy * gain
    inner = jnp.mean(dunit * unit, -1, keepdims=True)
    return spread * (dunit - jnp.mean(dunit, -1, keepdims=True) - unit * inner)


def head_lanes(h):
    lane = lax.broadcasted_iota(jnp.int32, (1, WIDTH), 1)
    return (lane >= h * HEAD) & (lane < (h + 1) * HEAD)


def head_mask(h):
    return jnp.where(head_lanes(h), 1.0, 0.0).astype(HALF)


def build_bias(tbl, cols, xs, bias, edges):
    for z in range(2):
        for a in range(6):
            for zu in range(2):
                start = ((z * 2 + zu) * 6 + a) * 138
                piece = tbl[0:HEADS, start : start + 138]
                piece = jnp.concatenate((piece, jnp.zeros((HEADS, 118), FULL)), 1)
                for p in range(2):
                    for half in range(2):
                        xs[zu * 2 + half, pl.ds(p * 12 + z * 6 + a, HEADS, stride=24), :] = piece[
                            :, half * 128 : half * 128 + 128
                        ]
    total = None
    for zu in range(2):
        x = jnp.concatenate((xs[zu * 2], xs[zu * 2 + 1]), 1)
        high = x.astype(HALF)
        left = x - high.astype(FULL)
        mid = left.astype(HALF)
        low = (left - mid.astype(FULL)).astype(HALF)
        term = dot(jnp.concatenate((high, mid, low), 0), cols[zu])
        total = term if total is None else total + term
    table = total[:CELLS] + total[CELLS : 2 * CELLS] + total[2 * CELLS :]
    row = lax.broadcasted_iota(jnp.int32, (CELLS, 1), 0).astype(FULL)
    lane = lax.broadcasted_iota(jnp.int32, (1, CELLS), 1).astype(FULL)

    part = whole_part
    even = part(row, 12) - 2.0 * part(part(row, 12), 2) == 0.0
    table = jnp.where(even, pltpu.roll(table, 384 - 12, 1), table)
    if edges is not None:
        last_section, last_band = edges
        row12, lane12 = row - 12.0 * part(row, 12), lane - 12.0 * part(lane, 12)
        row_z, lane_z = part(row12, 6), part(lane12, 6)
        row_a, lane_a = part(row12 - 6.0 * row_z, 3), part(lane12 - 6.0 * lane_z, 3)
        apart = jnp.abs(row_z - lane_z) * last_section + jnp.abs(row_a - lane_a) * last_band
        blocked = apart > 0.5
    for j in range(6):
        shift = (10 - 2 * j) * 12
        moved = pltpu.roll(table, 384 - shift, 1) if shift else table
        moved = moved[:, :CELLS]
        if edges is not None:
            moved = jnp.where(blocked, neg_fill, moved)
        for h in range(HEADS):
            bias[h * CELLS + j * 24 : h * CELLS + j * 24 + 24, :] = moved[h * 24 : h * 24 + 24, :]


def by_head(rows):
    return jnp.concatenate([rows * head_mask(h) for h in range(HEADS)], 0)


def attend(q, k, v, bias, prob):
    scores = dot_nt(by_head(q), k)
    for h in range(HEADS):
        rows = slice(h * CELLS, (h + 1) * CELLS)
        score = scores[rows] * HEAD ** (-0.5) + bias[rows, :]
        expo = jnp.exp(score - jnp.max(score, -1, keepdims=True))
        prob[rows, :] = (expo * (1.0 / jnp.sum(expo, -1, keepdims=True))).astype(HALF)
    mixed = jnp.zeros((CELLS, WIDTH), FULL)
    for h in range(HEADS):
        term = dot(prob[h * CELLS : (h + 1) * CELLS, :], v)
        mixed = jnp.where(head_lanes(h), term, mixed)
    return mixed.astype(HALF)


def attend_back(dmixed, qheads, k, v, prob, turned):
    dheads = by_head(dmixed)
    dweights = dot_nt(dheads, v)
    dv = dot_tn(prob[...], dheads) if turned is None else dot(turned[...], dheads)
    dscores = []
    for h in range(HEADS):
        rows = slice(h * CELLS, (h + 1) * CELLS)
        full = prob[rows, :].astype(FULL)
        inner = jnp.sum(dweights[rows] * full, -1, keepdims=True)
        dscores.append((full * (dweights[rows] - inner) * HEAD ** (-0.5)).astype(HALF))
    dk = dot_tn(jnp.concatenate(dscores, 0), qheads)
    dq = jnp.zeros((CELLS, WIDTH), FULL)
    for h in range(HEADS):
        dq = jnp.where(head_lanes(h), dot(dscores[h], k), dq)
    return dq.astype(HALF), dk.astype(HALF), dv.astype(HALF)


def gelu_parts(u):
    below = 0.5 * (1.0 + lax.erf(u * (0.5**0.5)))
    slope = below + u * (jnp.exp(-0.5 * u * u) * (2.0 * np.pi) ** (-0.5))
    return below, slope


def forward_half(x, gains, wqkv, wproj, bias, prob):
    unit, spread = normalise(x)
    hidden = (unit * gains[0:1, :]).astype(HALF)
    qkv = dot(hidden, wqkv[...]).astype(HALF)
    q, k, v = (qkv[:, n * WIDTH : (n + 1) * WIDTH] for n in range(3))
    mixed = attend(q, k, v, bias, prob)
    return (unit, spread), (q, k, v), x + dot(mixed, wproj[...])


def backward(dflat, norms, heads, prob, turned, slope, gains, wqkv, wproj, wup, wdown):
    qheads, k, v = heads
    dactive = dot(dflat, wdown[...])
    dupward = (dactive * slope).astype(HALF)
    dnormed = dot_nt(dupward, wup[...])
    dresid = dflat.astype(FULL) + normalise_back(dnormed, *norms[1], gains[1:2, :])
    dmixed = dot_nt(dresid.astype(HALF), wproj[...]).astype(HALF)
    dq, dk, dv = attend_back(dmixed, qheads, k, v, prob, turned)
    dhidden = dot_nt(dq, wqkv[:, :WIDTH])
    dhidden = dhidden + dot_nt(dk, wqkv[:, WIDTH : 2 * WIDTH])
    dhidden = dhidden + dot_nt(dv, wqkv[:, 2 * WIDTH :])
    return dresid + normalise_back(dhidden, *norms[0], gains[0:1, :])


def gather_patches(upper, surface, section, select, ff, ft):
    base = 4 * section - 2
    for z in range(2):
        for a in range(2):
            level = jnp.maximum(base + 2 * z + a, 0)
            for v in range(5):
                field = upper[v, level].astype(FULL)
                if z == 0:
                    field = jnp.where(section == 0, 0.0, field)
                slot = (z * 2 + a) * 5 + v
                ff[slot * 24 : slot * 24 + 24, 0:48] = field
    for v in range(4):
        field = jnp.where(section == 0, surface[v].astype(FULL), 0.0)
        ff[(20 + v) * 24 : (21 + v) * 24, 0:48] = field
    pad = jnp.zeros((8, 128), FULL)
    for i in range(6):
        pieces = []
        for b in range(4):
            pieces += [ff[pl.ds(4 * i + b, 24, stride=24), :], pad]
        ft[i * 48 : i * 48 + 48, :] = jnp.concatenate(pieces, 0).T[:48]
    raw = [ft[pl.ds(c, 72, stride=4), :].astype(HALF) for c in range(4)]
    both = dot(jnp.concatenate(raw, 1), select[...])
    return jnp.concatenate((both[:, :256], both[:, 256:]), 0).astype(HALF)


def flag(axis):
    last = lax.axis_index(axis) == lax.axis_size(axis) - 1
    return jnp.where(last, 1.0, 0.0)


def table_rows(tbl, block, table):
    for h in range(HEADS):
        table[h : h + 1, 0 : tbl.shape[-1]] = tbl[block * HEADS + h]


def first_kernel(*refs):
    names = (
        "tbl", "upper", "surface", "to_inner", "uembed", "sembed", "gains",
        "wqkv", "wproj", "wup", "wdown", "cot", "out_first", "out_cot",
    )
    count = len(names)
    source, refs = refs[:count], refs[count:]
    patch_o, x_o, qkv_o, prob, resid_o, send_o, *keep_o = refs[:10]
    refs = refs[10:]
    local, refs = refs[:count], refs[count:]
    ff, ft, emb, cots, table, xs, bias, cols, select, sems = refs
    copies = {}
    for n, name in enumerate(names):
        start, end = source[n], local[n]
        if name[0] == "w":
            start = start.at[0]
        elif name == "tbl":
            start = start.at[pl.ds(0, HEADS)]
        elif name == "uembed":
            end = emb.at[pl.ds(0, 160)]
        elif name == "sembed":
            end = emb.at[pl.ds(160, 64)]
        copies[name] = pltpu.make_async_copy(start, end, sems.at[n])
        copies[name].start()
    have = dict(zip(names, local))

    def wait(*which):
        for name in which:
            copies[name].wait()

    emb[224:256, :] = jnp.zeros((32, WIDTH), HALF)
    fill_columns(cols)
    fill_select(select)
    wait("tbl", "upper", "surface", "to_inner", "uembed", "sembed", "gains", "wqkv")
    table_rows(have["tbl"], 0, table)
    build_bias(table, cols, xs, bias, None)
    section = lax.axis_index("section")
    patch = gather_patches(have["upper"], have["surface"], section, select, ff, ft)
    patch = dot(have["to_inner"][...], patch).astype(HALF)
    patch_o[...] = patch
    latent = dot(patch, emb[...]).astype(HALF)
    x_o[...] = latent
    x = latent.astype(FULL)
    gains = have["gains"].at[0]
    wait("wproj", "wup", "wdown", "cot", "out_first", "out_cot")
    cot = have["cot"]
    for a in range(6):
        for o in range(12):
            cots[(a * 12 + o) * 2 : (a * 12 + o) * 2 + 2, :] = cot[a, o].astype(FULL)
    ready = dot(have["out_cot"][...], cots[...].astype(HALF))
    _, qkv, resid = forward_half(x, gains, have["wqkv"], have["wproj"], bias, prob)
    for n in range(3):
        qkv_o[n] = qkv[n]
    resid_o[...] = resid
    unit, spread = normalise(resid)
    normed = (unit * gains[1:2, :]).astype(HALF)
    upward = dot(normed, have["wup"][...])
    active = (upward * gelu_parts(upward)[0]).astype(HALF)
    result = (resid + dot_nt(active, have["wdown"][...])).astype(HALF)
    moved = (dot(have["out_first"][...], result) + ready).astype(HALF)
    send_o[...] = moved[192:]
    for n in range(4):
        keep_o[n][...] = moved[n * 48 : n * 48 + 48]


def second_bias(tbl, after, bias, table, xs, cols):
    fill_columns(cols)
    table_rows(tbl, 1, table)
    build_bias(table, cols, xs, bias, (flag("section"), flag("lat")))


def between_kernel(after, x, qkv, prob, resid, gains, wup, *results):
    slope_o, unit_o, spread_o, heads_o, turned_o = results
    for n, values in enumerate((x[...].astype(FULL), resid[...])):
        unit, spread = normalise(values)
        unit_o[n] = unit
        spread_o[n] = spread
    upward = dot((unit * gains[0, 1:2, :]).astype(HALF), wup[0])
    slope_o[...] = gelu_parts(upward)[1].astype(HALF)
    heads_o[...] = by_head(qkv[0])
    turned_o[...] = prob[...].astype(FULL).T.astype(HALF)


def second_kernel(*refs):
    parts, rest = refs[:4], refs[4:]
    gains, wqkv, wproj, wup, wdown, bias, into, out_of, send_o = rest[:9]
    keep, stack, prob = rest[9:13], rest[13], rest[14]
    for n, part in zip(order, parts):
        stack[n * 96 : n * 96 + 96, :] = part[...]
    both = dot(into[...], stack[...])
    x, dflat = both[:CELLS], both[CELLS:].astype(HALF)
    gains, wqkv, wproj, wup, wdown = (w.at[1] for w in (gains, wqkv, wproj, wup, wdown))
    first, (q, k, v), resid = forward_half(x, gains, wqkv, wproj, bias, prob)
    last = normalise(resid)
    upward = dot((last[0] * gains[1:2, :]).astype(HALF), wup[...])
    slope = gelu_parts(upward)[1]
    heads = (by_head(q), k, v)
    dx = backward(
        dflat, (first, last), heads, prob, None, slope, gains, wqkv, wproj, wup, wdown
    )
    moved = dot(out_of[...], dx.astype(HALF)).astype(HALF)
    send_o[...] = moved[128:]
    for n in range(4):
        keep[n][...] = moved[n * 32 : n * 32 + 32]


def third_kernel(*refs):
    parts, rest = refs[:4], refs[4:]
    gains, wqkv, wproj, wup, wdown, patch, qkv_i, prob, slope, unit, spread, heads, turned = rest[:13]
    into, out_of, grad_o, mine_o, other_o, stack, terms = rest[13:]
    for n, part in zip(order, parts):
        stack[n * 64 : n * 64 + 64, :] = part[...]
    dflat = dot(into[...], stack[...]).astype(HALF)
    gains, wqkv, wproj, wup, wdown = (w.at[0] for w in (gains, wqkv, wproj, wup, wdown))
    norms = tuple((unit[n], spread[n]) for n in range(2))
    dx = backward(
        dflat, norms, (heads[...], qkv_i[1], qkv_i[2]), prob, turned, slope[...].astype(FULL),
        gains, wqkv, wproj, wup, wdown,
    )
    grad = dx.astype(HALF)
    moved = dot(out_of[...], grad).astype(HALF)
    for z in range(2):
        for a in range(6):
            grad_o[z, a] = moved[(z * 6 + a) * 16 : (z * 6 + a) * 16 + 12]
    total = dot_tn(patch[...], grad)
    terms[0:224, :] = total[:224, :128]
    terms[224:336, :] = jnp.concatenate((total[:112, 128:], total[112:224, 128:]), 1)
    place = lax.axis_index("section") % 2
    mine_o[...] = terms[pl.ds(pl.multiple_of(place * 168, 8), 168), :].astype(HALF)
    other_o[...] = terms[pl.ds(pl.multiple_of(168 - place * 168, 8), 168), :].astype(HALF)


vmem = pl.BlockSpec(memory_space=pltpu.VMEM)
hbm = pl.BlockSpec(memory_space=pltpu.HBM)


def call(kernel, outs, scratch, *args, spec=vmem, out=vmem, room=30, size=1):
    return pl.pallas_call(
        kernel,
        out_shape=outs,
        in_specs=[spec for a in args],
        out_specs=jax.tree.map(lambda _: out, outs),
        scratch_shapes=scratch,
        compiler_params=pltpu.CompilerParams(vmem_limit_bytes=room * 2**20),
        cost_estimate=pl.CostEstimate(flops=1000000, bytes_accessed=size * 1000000, transcendentals=0),
    )(*args)


def shape(dims, dtype=HALF):
    return jax.ShapeDtypeStruct(dims, dtype)


def fetch(block, steps):
    names = ("lon", "lat", "section")
    axes = [name for name in names if steps.get(name, 0)]
    if not axes:
        return block
    sizes = [lax.axis_size(name) for name in axes]
    pairs = []
    for place in np.ndindex(*sizes):
        source = [(p + steps[name]) % n for p, name, n in zip(place, axes, sizes)]
        pairs.append(
            (int(np.ravel_multi_index(source, sizes)), int(np.ravel_multi_index(place, sizes)))
        )
    return lax.ppermute(block, tuple(axes), pairs)


order = (3, 1, 2, 0)


def exchange(keep, got, way):
    pitch = got.shape[0] // 4
    blocks = []
    for n in order:
        block = jnp.concatenate((keep[n], got[n * pitch : (n + 1) * pitch]), 0)
        blocks.append(fetch(block, {"lat": way * (n // 2), "lon": way * (n % 2)}))
    return blocks


def swap(block, flips):
    names = ("lon", "lat", "section")
    axes = [name for name in names if flips.get(name, 0)]
    sizes = [lax.axis_size(name) for name in axes]
    pairs = []
    for place in np.ndindex(*sizes):
        source = [p ^ flips[name] for p, name in zip(place, axes)]
        pairs.append(
            (int(np.ravel_multi_index(source, sizes)), int(np.ravel_multi_index(place, sizes)))
        )
    return lax.ppermute(block, tuple(axes), pairs)


def add_up(mine, other):
    total = (mine.astype(FULL) + swap(other, {"section": 1}).astype(FULL)).astype(HALF)
    bits = []
    for name in ("section", "lat", "lon"):
        size = lax.axis_size(name)
        if size & (size - 1) or size < 2:
            raise ValueError("axis size")
        bits += [(name, 1 << n) for n in range(name == "section", size.bit_length() - 1)]
    for n in range(0, len(bits), 2):
        pair = [{name: bit} for name, bit in bits[n : n + 2]]
        if len(pair) == 1:
            total = total.astype(FULL) + swap(total, pair[0]).astype(FULL)
        else:
            one, two = pair
            three = dict(one)
            for name, bit in two.items():
                three[name] = three.get(name, 0) | bit
            near, far, last = (swap(total, step).astype(FULL) for step in (one, two, three))
            total = (total.astype(FULL) + near) + (far + last)
        total = total.astype(HALF)
    return total, swap(total, {"section": 1})


def last_kernel(scale, mine, other, upper_o, surface_o, halves, both, sems):
    place = lax.axis_index("section") % 2
    halves[pl.ds(pl.multiple_of(place * 168, 8), 168), :] = mine[...].astype(FULL) * scale
    halves[pl.ds(pl.multiple_of(168 - place * 168, 8), 168), :] = other[...].astype(FULL) * scale
    both[:, 0:128] = halves[0:224, :]
    last = halves[224:336, :]
    both[0:112, 128:192] = last[:, :64]
    both[112:224, 128:192] = last[:, 64:]
    copies = [
        pltpu.make_async_copy(both.at[pl.ds(0, 160)], upper_o, sems.at[0]),
        pltpu.make_async_copy(both.at[pl.ds(160, 64)], surface_o, sems.at[1]),
    ]
    for copy in copies:
        copy.start()
    for copy in copies:
        copy.wait()


def on_device(
    upper_fields,
    surface_fields,
    upper_embed,
    surface_embed,
    norm_gains,
    qkv_weight,
    proj_weight,
    up_weight,
    down_weight,
    earth_bias,
    out_grad,
):
    sections, bands = lax.axis_size("section"), lax.axis_size("lat")
    levels, rows, columns, width = out_grad.shape
    positions = earth_bias.shape[-1]
    table = earth_bias.transpose(0, 1, 3, 2, 4).reshape(2 * HEADS, 1, positions)
    weights = (norm_gains, qkv_weight, proj_weight, up_weight, down_weight.transpose(0, 2, 1))

    def from_cot(z, a, o):
        return (a * 12 + o) * 2 + z

    operands = (
        table, upper_fields, surface_fields, jnp.asarray(natural_to_inner()), upper_embed,
        surface_embed, *weights, out_grad.transpose(1, 2, 0, 3),
        jnp.asarray(octants_out(48, 0, True, inner_row)),
        jnp.asarray(octants_out(48, 18, True, from_cot)),
    )
    local = [
        pltpu.VMEM(v.shape[1:] if 7 <= n < 11 else v.shape, v.dtype) for n, v in enumerate(operands)
    ]
    local[0] = pltpu.VMEM((HEADS, 1, positions), FULL)
    local[4] = local[5] = pltpu.VMEM((16, 128), HALF)
    scratch_bias = [pltpu.VMEM((8, 3328), FULL), pltpu.VMEM((4, CELLS, 128), FULL)]
    scratch_cols = pltpu.VMEM((2, 256, 384), HALF)
    held = [
        shape((CELLS, 256)),
        shape((CELLS, WIDTH)),
        shape((3, CELLS, WIDTH)),
        shape((HEADS * CELLS, CELLS)),
        shape((CELLS, WIDTH), FULL),
    ]
    patch, x, qkv, prob, resid, send, *keep = call(
        first_kernel,
        held + [shape((192, WIDTH))] + [shape((48, WIDTH))] * 4,
        local
        + [
            pltpu.VMEM((576, 128), FULL),
            pltpu.VMEM((288, 128), FULL),
            pltpu.VMEM((256, WIDTH), HALF),
            pltpu.VMEM((CELLS, WIDTH), FULL),
        ]
        + scratch_bias
        + [
            pltpu.VMEM((HEADS * CELLS, CELLS), FULL),
            scratch_cols,
            pltpu.VMEM((512, 512), HALF),
            pltpu.SemaphoreType.DMA((len(operands),)),
        ],
        *(pltpu.with_memory_space_constraint(v, pltpu.HBM) for v in operands),
        spec=hbm,
    )
    bias_shape = shape((HEADS * CELLS, CELLS), FULL)
    got = fetch(send, {"section": 1})
    bias = call(second_bias, bias_shape, [*scratch_bias, scratch_cols], table, got)
    slope, unit, spread, heads, turned = call(
        between_kernel,
        [
            shape((CELLS, 4 * WIDTH)),
            shape((2, CELLS, WIDTH), FULL),
            shape((2, CELLS, 1), FULL),
            shape((HEADS * CELLS, WIDTH)),
            shape((CELLS, HEADS * CELLS)),
        ],
        [],
        got, x, qkv, prob, resid, norm_gains, up_weight,
    )
    into = np.concatenate((octants_in(48, 0, False), octants_in(48, 18, False)), 0)
    send, *keep = call(
        second_kernel,
        [shape((128, WIDTH))] + [shape((32, WIDTH))] * 4,
        [pltpu.VMEM((8 * 48, WIDTH), HALF), pltpu.VMEM((HEADS * CELLS, CELLS), HALF)],
        *exchange(keep, got, 1), *weights, bias,
        jnp.asarray(into), jnp.asarray(octants_out(32, 0, False, inner_row)),
    )
    latent_grad, mine, other = call(
        third_kernel,
        [shape((2, 6, 12, WIDTH)), shape((168, 128)), shape((168, 128))],
        [pltpu.VMEM((8 * 32, WIDTH), HALF), pltpu.VMEM((336, 128), FULL)],
        *exchange(keep, fetch(send, {"section": -1}), -1), *weights, patch, qkv, prob,
        slope, unit, spread, heads, turned,
        jnp.asarray(octants_in(32, 0, True)), jnp.asarray(inner_to_padded()),
    )
    scale = float(levels * sections * rows * bands * columns * lax.axis_size("lon")) ** (-0.5)
    upper_grad, surface_grad = call(
        functools.partial(last_kernel, scale),
        [shape((160, WIDTH), FULL), shape((64, WIDTH), FULL)],
        [
            pltpu.VMEM((336, 128), FULL),
            pltpu.VMEM((224, WIDTH), FULL),
            pltpu.SemaphoreType.DMA((2,)),
        ],
        *add_up(mine, other),
        out=hbm,
    )
    return (latent_grad, upper_grad, surface_grad)


def solution(mesh):
    placed = (
        P(None, None, "lat", "lon"),
        P(None, "lat", "lon"),
        P(),
        P(),
        P(),
        P(),
        P(),
        P(),
        P(),
        P(None, "lat", "section", None, None),
        P("section", "lat", "lon", None),
    )
    return jax.shard_map(
        on_device,
        mesh=mesh,
        in_specs=placed,
        out_specs=(P("section", "lat", "lon", None), P(), P()),
        check_vma=False,
    )
```

```python
import functools

import jax
import jax.numpy as jnp
import ml_dtypes
import numpy as np
from jax import lax
from jax.experimental import pallas as pl
from jax.experimental.pallas import tpu as pltpu
from jax.sharding import PartitionSpec as P

neg_fill = -1e30
norm_eps = 1e-05
HEADS = 6
HEAD = 32
CELLS = 144
WIDTH = 192
FULL = jnp.float32
HALF = jnp.bfloat16


def inner_row(z, a, o):
    return o * 12 + z * 6 + a


def octant_of(z, a, o):
    return (z * 4 + (a // 3) * 2 + o // 6, (a % 3) * 6 + o % 6)


def as_half(array):
    return array.astype(ml_dtypes.bfloat16)


def cells():
    return [(z, a, o) for z in range(2) for a in range(6) for o in range(12)]


def natural_to_inner():
    move = np.zeros((CELLS, CELLS), np.float32)
    for z, a, o in cells():
        move[inner_row(z, a, o), (z * 6 + a) * 12 + o] = 1
    return as_half(move)


def inner_to_padded():
    move = np.zeros((192, CELLS), np.float32)
    for z, a, o in cells():
        move[(z * 6 + a) * 16 + o, inner_row(z, a, o)] = 1
    return as_half(move)


def octants_out(count, first, flip, source):
    pitch = -(-count // 8) * 8
    move = np.zeros((4 * pitch + 4 * count, CELLS), np.float32)
    for z, a, o in cells():
        part, place = octant_of(z, a, o)
        part = 7 - part if flip else part
        start = part * pitch if part < 4 else 4 * pitch + (part - 4) * count
        move[start + first + place, source(z, a, o)] = 1
    return as_half(move)


def octants_in(count, first, flip):
    pitch = -(-2 * count // 16) * 16
    move = np.zeros((CELLS, 4 * pitch), np.float32)
    for z, a, o in cells():
        part, place = octant_of(z, a, o)
        part = 7 - part if flip else part
        move[inner_row(z, a, o), part % 4 * pitch + part // 4 * count + first + place] = 1
    return as_half(move)


def whole_part(v, size):
    return jnp.floor((v + 0.5) * (1.0 / size))


def one_hot(target, lanes):
    lane = lax.broadcasted_iota(jnp.int32, (1, lanes), 1).astype(FULL)
    return jnp.where(lane == target, 1.0, 0.0).astype(HALF)


def fill_columns(cols):
    row = lax.broadcasted_iota(jnp.int32, (256, 1), 0).astype(FULL)
    a = whole_part(row, 23)
    k = row - 23.0 * a
    for z in range(2):
        target = (22.0 - k) * 12.0 + (z * 6.0) + a
        cols[z] = one_hot(jnp.where(row < 138.0, target, -1.0), 384)


def fill_select(select):
    row = lax.broadcasted_iota(jnp.int32, (128, 1), 0).astype(FULL)
    b = whole_part(row, 32)
    slot = row - 32.0 * b
    layer = whole_part(slot, 5)
    z = whole_part(layer, 2)
    upper = z * 256.0 + (slot - 5.0 * layer) * 32.0 + (layer - 2.0 * z) * 16.0
    surface = 160.0 + (slot - 20.0) * 16.0
    target = jnp.where(slot < 20.0, upper, surface) + b * 4.0
    for c in range(4):
        select[c * 128 : c * 128 + 128, :] = one_hot(
            jnp.where(slot < 24.0, target + float(c), -1.0), 512
        )


def dot(a, b):
    return jnp.dot(a, b, preferred_element_type=FULL)


def dot_nt(a, b):
    return lax.dot_general(a, b, (((1,), (1,)), ((), ())), preferred_element_type=FULL)


def dot_tn(a, b):
    return lax.dot_general(a, b, (((0,), (0,)), ((), ())), preferred_element_type=FULL)


def normalise(v):
    mean = jnp.mean(v, -1, keepdims=True)
    centred = v - mean
    spread = lax.rsqrt(jnp.mean(centred * centred, -1, keepdims=True) + norm_eps)
    return centred * spread, spread


def normalise_back(dy, unit, spread, gain):
    dunit = dy * gain
    inner = jnp.mean(dunit * unit, -1, keepdims=True)
    return spread * (dunit - jnp.mean(dunit, -1, keepdims=True) - unit * inner)


def head_lanes(h):
    lane = lax.broadcasted_iota(jnp.int32, (1, WIDTH), 1)
    return (lane >= h * HEAD) & (lane < (h + 1) * HEAD)


def head_mask(h):
    return jnp.where(head_lanes(h), 1.0, 0.0).astype(HALF)


def build_bias(tbl, cols, xs, bias, edges):
    for z in range(2):
        for a in range(6):
            for zu in range(2):
                start = ((z * 2 + zu) * 6 + a) * 138
                piece = tbl[0:HEADS, start : start + 138]
                piece = jnp.concatenate((piece, jnp.zeros((HEADS, 118), FULL)), 1)
                for p in range(2):
                    for half in range(2):
                        xs[zu * 2 + half, pl.ds(p * 12 + z * 6 + a, HEADS, stride=24), :] = piece[
                            :, half * 128 : half * 128 + 128
                        ]
    total = None
    for zu in range(2):
        x = jnp.concatenate((xs[zu * 2], xs[zu * 2 + 1]), 1)
        high = x.astype(HALF)
        left = x - high.astype(FULL)
        mid = left.astype(HALF)
        low = (left - mid.astype(FULL)).astype(HALF)
        term = dot(jnp.concatenate((high, mid, low), 0), cols[zu])
        total = term if total is None else total + term
    table = total[:CELLS] + total[CELLS : 2 * CELLS] + total[2 * CELLS :]
    row = lax.broadcasted_iota(jnp.int32, (CELLS, 1), 0).astype(FULL)
    lane = lax.broadcasted_iota(jnp.int32, (1, CELLS), 1).astype(FULL)

    part = whole_part
    even = part(row, 12) - 2.0 * part(part(row, 12), 2) == 0.0
    table = jnp.where(even, pltpu.roll(table, 384 - 12, 1), table)
    if edges is not None:
        last_section, last_band = edges
        row12, lane12 = row - 12.0 * part(row, 12), lane - 12.0 * part(lane, 12)
        row_z, lane_z = part(row12, 6), part(lane12, 6)
        row_a, lane_a = part(row12 - 6.0 * row_z, 3), part(lane12 - 6.0 * lane_z, 3)
        apart = jnp.abs(row_z - lane_z) * last_section + jnp.abs(row_a - lane_a) * last_band
        blocked = apart > 0.5
    for j in range(6):
        shift = (10 - 2 * j) * 12
        moved = pltpu.roll(table, 384 - shift, 1) if shift else table
        moved = moved[:, :CELLS]
        if edges is not None:
            moved = jnp.where(blocked, neg_fill, moved)
        for h in range(HEADS):
            bias[h * CELLS + j * 24 : h * CELLS + j * 24 + 24, :] = moved[h * 24 : h * 24 + 24, :]


def by_head(rows):
    return jnp.concatenate([rows * head_mask(h) for h in range(HEADS)], 0)


def attend(q, k, v, bias, prob):
    scores = dot_nt(by_head(q), k)
    for h in range(HEADS):
        rows = slice(h * CELLS, (h + 1) * CELLS)
        score = scores[rows] * HEAD ** (-0.5) + bias[rows, :]
        expo = jnp.exp(score - jnp.max(score, -1, keepdims=True))
        prob[rows, :] = (expo * (1.0 / jnp.sum(expo, -1, keepdims=True))).astype(HALF)
    mixed = jnp.zeros((CELLS, WIDTH), FULL)
    for h in range(HEADS):
        term = dot(prob[h * CELLS : (h + 1) * CELLS, :], v)
        mixed = jnp.where(head_lanes(h), term, mixed)
    return mixed.astype(HALF)


def attend_back(dmixed, q, k, v, prob):
    dheads = by_head(dmixed)
    dweights = dot_nt(dheads, v)
    dv = dot_tn(prob[...], dheads)
    dscores = []
    for h in range(HEADS):
        rows = slice(h * CELLS, (h + 1) * CELLS)
        full = prob[rows, :].astype(FULL)
        inner = jnp.sum(dweights[rows] * full, -1, keepdims=True)
        dscores.append((full * (dweights[rows] - inner) * HEAD ** (-0.5)).astype(HALF))
    dk = dot_tn(jnp.concatenate(dscores, 0), by_head(q))
    dq = jnp.zeros((CELLS, WIDTH), FULL)
    for h in range(HEADS):
        dq = jnp.where(head_lanes(h), dot(dscores[h], k), dq)
    return dq.astype(HALF), dk.astype(HALF), dv.astype(HALF)


def gelu_parts(u):
    below = 0.5 * (1.0 + lax.erf(u * (0.5**0.5)))
    slope = below + u * (jnp.exp(-0.5 * u * u) * (2.0 * np.pi) ** (-0.5))
    return below, slope


def forward_half(x, gains, wqkv, wproj, bias, prob):
    unit, spread = normalise(x)
    hidden = (unit * gains[0:1, :]).astype(HALF)
    qkv = dot(hidden, wqkv[...]).astype(HALF)
    q, k, v = (qkv[:, n * WIDTH : (n + 1) * WIDTH] for n in range(3))
    mixed = attend(q, k, v, bias, prob)
    return (q, k, v), x + dot(mixed, wproj[...])


def backward(dflat, x, qkv, prob, resid, slope, gains, wqkv, wproj, wup, wdown):
    q, k, v = qkv
    dactive = dot(dflat, wdown[...])
    dupward = (dactive * slope).astype(HALF)
    dnormed = dot_nt(dupward, wup[...])
    unit, spread = normalise(resid)
    dresid = dflat.astype(FULL) + normalise_back(dnormed, unit, spread, gains[1:2, :])
    dmixed = dot_nt(dresid.astype(HALF), wproj[...]).astype(HALF)
    dq, dk, dv = attend_back(dmixed, q, k, v, prob)
    dhidden = dot_nt(dq, wqkv[:, :WIDTH])
    dhidden = dhidden + dot_nt(dk, wqkv[:, WIDTH : 2 * WIDTH])
    dhidden = dhidden + dot_nt(dv, wqkv[:, 2 * WIDTH :])
    unit, spread = normalise(x)
    return dresid + normalise_back(dhidden, unit, spread, gains[0:1, :])


def gather_patches(upper, surface, section, select, ff, ft):
    base = 4 * section - 2
    for z in range(2):
        for a in range(2):
            level = jnp.maximum(base + 2 * z + a, 0)
            for v in range(5):
                field = upper[v, level].astype(FULL)
                if z == 0:
                    field = jnp.where(section == 0, 0.0, field)
                slot = (z * 2 + a) * 5 + v
                ff[slot * 24 : slot * 24 + 24, 0:48] = field
    for v in range(4):
        field = jnp.where(section == 0, surface[v].astype(FULL), 0.0)
        ff[(20 + v) * 24 : (21 + v) * 24, 0:48] = field
    pad = jnp.zeros((8, 128), FULL)
    for i in range(6):
        pieces = []
        for b in range(4):
            pieces += [ff[pl.ds(4 * i + b, 24, stride=24), :], pad]
        ft[i * 48 : i * 48 + 48, :] = jnp.concatenate(pieces, 0).T[:48]
    raw = [ft[pl.ds(c, 72, stride=4), :].astype(HALF) for c in range(4)]
    both = dot(jnp.concatenate(raw, 1), select[...])
    return jnp.concatenate((both[:, :256], both[:, 256:]), 0).astype(HALF)


def flag(axis):
    last = lax.axis_index(axis) == lax.axis_size(axis) - 1
    return jnp.where(last, 1.0, 0.0)


def table_rows(tbl, block, table):
    for h in range(HEADS):
        table[h : h + 1, 0 : tbl.shape[-1]] = tbl[block * HEADS + h]


def first_kernel(*refs):
    names = (
        "tbl", "upper", "surface", "to_inner", "uembed", "sembed", "gains",
        "wqkv", "wproj", "wup", "wdown", "cot", "out_first", "out_cot",
    )
    count = len(names)
    source, refs = refs[:count], refs[count:]
    patch_o, x_o, qkv_o, prob, resid_o, slope_o, send_o, *keep_o = refs[:11]
    refs = refs[11:]
    local, refs = refs[:count], refs[count:]
    ff, ft, emb, cots, table, xs, bias, cols, select, sems = refs
    copies = {}
    for n, name in enumerate(names):
        start, end = source[n], local[n]
        if name[0] == "w":
            start = start.at[0]
        elif name == "tbl":
            start = start.at[pl.ds(0, HEADS)]
        elif name == "uembed":
            end = emb.at[pl.ds(0, 160)]
        elif name == "sembed":
            end = emb.at[pl.ds(160, 64)]
        copies[name] = pltpu.make_async_copy(start, end, sems.at[n])
        copies[name].start()
    have = dict(zip(names, local))

    def wait(*which):
        for name in which:
            copies[name].wait()

    emb[224:256, :] = jnp.zeros((32, WIDTH), HALF)
    fill_columns(cols)
    fill_select(select)
    wait("tbl", "upper", "surface", "to_inner", "uembed", "sembed", "gains", "wqkv")
    table_rows(have["tbl"], 0, table)
    build_bias(table, cols, xs, bias, None)
    section = lax.axis_index("section")
    patch = gather_patches(have["upper"], have["surface"], section, select, ff, ft)
    patch = dot(have["to_inner"][...], patch).astype(HALF)
    patch_o[...] = patch
    latent = dot(patch, emb[...]).astype(HALF)
    x_o[...] = latent
    x = latent.astype(FULL)
    gains = have["gains"].at[0]
    wait("wproj", "wup", "wdown", "cot", "out_first", "out_cot")
    cot = have["cot"]
    for a in range(6):
        for o in range(12):
            cots[(a * 12 + o) * 2 : (a * 12 + o) * 2 + 2, :] = cot[a, o].astype(FULL)
    ready = dot(have["out_cot"][...], cots[...].astype(HALF))
    qkv, resid = forward_half(x, gains, have["wqkv"], have["wproj"], bias, prob)
    for n in range(3):
        qkv_o[n] = qkv[n]
    resid_o[...] = resid
    unit, spread = normalise(resid)
    normed = (unit * gains[1:2, :]).astype(HALF)
    upward = dot(normed, have["wup"][...])
    below, slope = gelu_parts(upward)
    slope_o[...] = slope.astype(HALF)
    active = (upward * below).astype(HALF)
    result = (resid + dot_nt(active, have["wdown"][...])).astype(HALF)
    moved = dot(have["out_first"][...], result) + ready
    send_o[...] = moved[160:].astype(HALF)
    for n in range(4):
        keep_o[n][...] = moved[n * 40 : n * 40 + 36].astype(HALF)


def second_bias(tbl, after, bias, table, xs, cols):
    fill_columns(cols)
    table_rows(tbl, 1, table)
    build_bias(table, cols, xs, bias, (flag("section"), flag("lat")))


def second_kernel(*refs):
    parts, rest = refs[:4], refs[4:]
    gains, wqkv, wproj, wup, wdown, bias, into, out_of, send_o = rest[:9]
    keep, stack, prob = rest[9:13], rest[13], rest[14]
    stack[...] = jnp.zeros_like(stack)
    for n, part in zip(order, parts):
        stack[n * 80 : n * 80 + 72, :] = part[...]
    both = dot(into[...], stack[...])
    x, dflat = both[:CELLS], both[CELLS:].astype(HALF)
    gains, wqkv, wproj, wup, wdown = (w.at[1] for w in (gains, wqkv, wproj, wup, wdown))
    qkv, resid = forward_half(x, gains, wqkv, wproj, bias, prob)
    unit, spread = normalise(resid)
    normed = (unit * gains[1:2, :]).astype(HALF)
    upward = dot(normed, wup[...])
    slope = gelu_parts(upward)[1]
    dx = backward(dflat, x, qkv, prob, resid, slope, gains, wqkv, wproj, wup, wdown)
    moved = dot(out_of[...], dx.astype(HALF))
    send_o[...] = moved[96:].astype(HALF)
    for n in range(4):
        keep[n][...] = moved[n * 24 : n * 24 + 18].astype(HALF)


def third_kernel(*refs):
    parts, rest = refs[:4], refs[4:]
    gains, wqkv, wproj, wup, wdown, patch, x_i, qkv_i, prob, resid, slope, into, out_of = rest[:13]
    grad_o, mine_o, other_o, stack, terms = rest[13:]
    stack[...] = jnp.zeros_like(stack)
    for n, part in zip(order, parts):
        stack[n * 48 : n * 48 + 36, :] = part[...]
    dflat = dot(into[...], stack[...]).astype(HALF)
    qkv = tuple(qkv_i[n] for n in range(3))
    gains, wqkv, wproj, wup, wdown = (w.at[0] for w in (gains, wqkv, wproj, wup, wdown))
    dx = backward(
        dflat, x_i[...].astype(FULL), qkv, prob, resid[...], slope[...].astype(FULL),
        gains, wqkv, wproj, wup, wdown,
    )
    grad = dx.astype(HALF)
    moved = dot(out_of[...], grad).astype(HALF)
    for z in range(2):
        for a in range(6):
            grad_o[z, a] = moved[(z * 6 + a) * 16 : (z * 6 + a) * 16 + 12]
    total = dot_tn(patch[...], grad)
    terms[0:224, :] = total[:224, :128]
    terms[224:336, :] = jnp.concatenate((total[:112, 128:], total[112:224, 128:]), 1)
    place = lax.axis_index("section") % 2
    mine_o[...] = terms[pl.ds(pl.multiple_of(place * 168, 8), 168), :].astype(HALF)
    other_o[...] = terms[pl.ds(pl.multiple_of(168 - place * 168, 8), 168), :].astype(HALF)


vmem = pl.BlockSpec(memory_space=pltpu.VMEM)
hbm = pl.BlockSpec(memory_space=pltpu.HBM)


def call(kernel, outs, scratch, *args, spec=vmem, out=vmem, room=30, size=1):
    return pl.pallas_call(
        kernel,
        out_shape=outs,
        in_specs=[spec for a in args],
        out_specs=jax.tree.map(lambda _: out, outs),
        scratch_shapes=scratch,
        compiler_params=pltpu.CompilerParams(vmem_limit_bytes=room * 2**20),
        cost_estimate=pl.CostEstimate(flops=1000000, bytes_accessed=size * 1000000, transcendentals=0),
    )(*args)


def shape(dims, dtype=HALF):
    return jax.ShapeDtypeStruct(dims, dtype)


def fetch(block, steps):
    names = ("lon", "lat", "section")
    axes = [name for name in names if steps.get(name, 0)]
    if not axes:
        return block
    sizes = [lax.axis_size(name) for name in axes]
    pairs = []
    for place in np.ndindex(*sizes):
        source = [(p + steps[name]) % n for p, name, n in zip(place, axes, sizes)]
        pairs.append(
            (int(np.ravel_multi_index(source, sizes)), int(np.ravel_multi_index(place, sizes)))
        )
    return lax.ppermute(block, tuple(axes), pairs)


order = (3, 1, 2, 0)


def exchange(keep, got, way):
    pitch = got.shape[0] // 4
    blocks = []
    for n in order:
        block = jnp.concatenate((keep[n], got[n * pitch : (n + 1) * pitch]), 0)
        blocks.append(fetch(block, {"lat": way * (n // 2), "lon": way * (n % 2)}))
    return blocks


def swap(block, flips):
    names = ("lon", "lat", "section")
    axes = [name for name in names if flips.get(name, 0)]
    sizes = [lax.axis_size(name) for name in axes]
    pairs = []
    for place in np.ndindex(*sizes):
        source = [p ^ flips[name] for p, name in zip(place, axes)]
        pairs.append(
            (int(np.ravel_multi_index(source, sizes)), int(np.ravel_multi_index(place, sizes)))
        )
    return lax.ppermute(block, tuple(axes), pairs)


def add_up(mine, other):
    total = (mine.astype(FULL) + swap(other, {"section": 1}).astype(FULL)).astype(HALF)
    bits = []
    for name in ("section", "lat", "lon"):
        size = lax.axis_size(name)
        if size & (size - 1) or size < 2:
            raise ValueError("axis size")
        bits += [(name, 1 << n) for n in range(name == "section", size.bit_length() - 1)]
    for n in range(0, len(bits), 2):
        pair = [{name: bit} for name, bit in bits[n : n + 2]]
        if len(pair) == 1:
            total = total.astype(FULL) + swap(total, pair[0]).astype(FULL)
        else:
            one, two = pair
            three = dict(one)
            for name, bit in two.items():
                three[name] = three.get(name, 0) | bit
            near, far, last = (swap(total, step).astype(FULL) for step in (one, two, three))
            total = (total.astype(FULL) + near) + (far + last)
        total = total.astype(HALF)
    return total, swap(total, {"section": 1})


def last_kernel(scale, mine, other, upper_o, surface_o, halves, both, sems):
    place = lax.axis_index("section") % 2
    halves[pl.ds(pl.multiple_of(place * 168, 8), 168), :] = mine[...].astype(FULL) * scale
    halves[pl.ds(pl.multiple_of(168 - place * 168, 8), 168), :] = other[...].astype(FULL) * scale
    both[:, 0:128] = halves[0:224, :]
    last = halves[224:336, :]
    both[0:112, 128:192] = last[:, :64]
    both[112:224, 128:192] = last[:, 64:]
    copies = [
        pltpu.make_async_copy(both.at[pl.ds(0, 160)], upper_o, sems.at[0]),
        pltpu.make_async_copy(both.at[pl.ds(160, 64)], surface_o, sems.at[1]),
    ]
    for copy in copies:
        copy.start()
    for copy in copies:
        copy.wait()


def on_device(
    upper_fields,
    surface_fields,
    upper_embed,
    surface_embed,
    norm_gains,
    qkv_weight,
    proj_weight,
    up_weight,
    down_weight,
    earth_bias,
    out_grad,
):
    sections, bands = lax.axis_size("section"), lax.axis_size("lat")
    levels, rows, columns, width = out_grad.shape
    positions = earth_bias.shape[-1]
    table = earth_bias.transpose(0, 1, 3, 2, 4).reshape(2 * HEADS, 1, positions)
    weights = (norm_gains, qkv_weight, proj_weight, up_weight, down_weight.transpose(0, 2, 1))

    def from_cot(z, a, o):
        return (a * 12 + o) * 2 + z

    operands = (
        table, upper_fields, surface_fields, jnp.asarray(natural_to_inner()), upper_embed,
        surface_embed, *weights, out_grad.transpose(1, 2, 0, 3),
        jnp.asarray(octants_out(36, 0, True, inner_row)),
        jnp.asarray(octants_out(36, 18, True, from_cot)),
    )
    local = [
        pltpu.VMEM(v.shape[1:] if 7 <= n < 11 else v.shape, v.dtype) for n, v in enumerate(operands)
    ]
    local[0] = pltpu.VMEM((HEADS, 1, positions), FULL)
    local[4] = local[5] = pltpu.VMEM((16, 128), HALF)
    scratch_bias = [pltpu.VMEM((8, 3328), FULL), pltpu.VMEM((4, CELLS, 128), FULL)]
    scratch_cols = pltpu.VMEM((2, 256, 384), HALF)
    held = [
        shape((CELLS, 256)),
        shape((CELLS, WIDTH)),
        shape((3, CELLS, WIDTH)),
        shape((HEADS * CELLS, CELLS)),
        shape((CELLS, WIDTH), FULL),
        shape((CELLS, 4 * WIDTH)),
    ]
    patch, x, qkv, prob, resid, slope, send, *keep = call(
        first_kernel,
        held + [shape((144, WIDTH))] + [shape((36, WIDTH))] * 4,
        local
        + [
            pltpu.VMEM((576, 128), FULL),
            pltpu.VMEM((288, 128), FULL),
            pltpu.VMEM((256, WIDTH), HALF),
            pltpu.VMEM((CELLS, WIDTH), FULL),
        ]
        + scratch_bias
        + [
            pltpu.VMEM((HEADS * CELLS, CELLS), FULL),
            scratch_cols,
            pltpu.VMEM((512, 512), HALF),
            pltpu.SemaphoreType.DMA((len(operands),)),
        ],
        *(pltpu.with_memory_space_constraint(v, pltpu.HBM) for v in operands),
        spec=hbm,
    )
    bias_shape = shape((HEADS * CELLS, CELLS), FULL)
    got = fetch(send, {"section": 1})
    bias = call(second_bias, bias_shape, [*scratch_bias, scratch_cols], table, got)
    into = np.concatenate((octants_in(36, 0, False), octants_in(36, 18, False)), 0)
    send, *keep = call(
        second_kernel,
        [shape((72, WIDTH))] + [shape((18, WIDTH))] * 4,
        [pltpu.VMEM((320, WIDTH), HALF), pltpu.VMEM((HEADS * CELLS, CELLS), HALF)],
        *exchange(keep, got, 1), *weights, bias,
        jnp.asarray(into), jnp.asarray(octants_out(18, 0, False, inner_row)),
    )
    latent_grad, mine, other = call(
        third_kernel,
        [shape((2, 6, 12, WIDTH)), shape((168, 128)), shape((168, 128))],
        [pltpu.VMEM((192, WIDTH), HALF), pltpu.VMEM((336, 128), FULL)],
        *exchange(keep, fetch(send, {"section": -1}), -1), *weights, patch, x, qkv, prob, resid, slope,
        jnp.asarray(octants_in(18, 0, True)), jnp.asarray(inner_to_padded()),
    )
    scale = float(levels * sections * rows * bands * columns * lax.axis_size("lon")) ** (-0.5)
    upper_grad, surface_grad = call(
        functools.partial(last_kernel, scale),
        [shape((160, WIDTH), FULL), shape((64, WIDTH), FULL)],
        [
            pltpu.VMEM((336, 128), FULL),
            pltpu.VMEM((224, WIDTH), FULL),
            pltpu.SemaphoreType.DMA((2,)),
        ],
        *add_up(mine, other),
        out=hbm,
    )
    return (latent_grad, upper_grad, surface_grad)


def solution(mesh):
    placed = (
        P(None, None, "lat", "lon"),
        P(None, "lat", "lon"),
        P(),
        P(),
        P(),
        P(),
        P(),
        P(),
        P(),
        P(None, "lat", "section", None, None),
        P("section", "lat", "lon", None),
    )
    return jax.shard_map(
        on_device,
        mesh=mesh,
        in_specs=placed,
        out_specs=(P("section", "lat", "lon", None), P(), P()),
        check_vma=False,
    )
```

```python
import functools

import jax
import jax.numpy as jnp
import ml_dtypes
import numpy as np
from jax import lax
from jax.experimental import pallas as pl
from jax.experimental.pallas import tpu as pltpu
from jax.sharding import PartitionSpec as P

neg_fill = -1e30
norm_eps = 1e-05
HEADS = 6
HEAD = 32
CELLS = 144
WIDTH = 192
FULL = jnp.float32
HALF = jnp.bfloat16


def inner_row(z, a, o):
    return o * 12 + z * 6 + a


def octant_of(z, a, o):
    return (z * 4 + (a // 3) * 2 + o // 6, (a % 3) * 6 + o % 6)


def as_half(array):
    return array.astype(ml_dtypes.bfloat16)


def cells():
    return [(z, a, o) for z in range(2) for a in range(6) for o in range(12)]


def natural_to_inner():
    move = np.zeros((CELLS, CELLS), np.float32)
    for z, a, o in cells():
        move[inner_row(z, a, o), (z * 6 + a) * 12 + o] = 1
    return as_half(move)


def inner_to_padded():
    move = np.zeros((192, CELLS), np.float32)
    for z, a, o in cells():
        move[(z * 6 + a) * 16 + o, inner_row(z, a, o)] = 1
    return as_half(move)


def octants_out(count, first, flip, source):
    pitch = -(-count // 8) * 8
    move = np.zeros((4 * pitch + 4 * count, CELLS), np.float32)
    for z, a, o in cells():
        part, place = octant_of(z, a, o)
        part = 7 - part if flip else part
        start = part * pitch if part < 4 else 4 * pitch + (part - 4) * count
        move[start + first + place, source(z, a, o)] = 1
    return as_half(move)


def octants_in(count, first, flip):
    pitch = -(-2 * count // 16) * 16
    move = np.zeros((CELLS, 4 * pitch), np.float32)
    for z, a, o in cells():
        part, place = octant_of(z, a, o)
        part = 7 - part if flip else part
        move[inner_row(z, a, o), part % 4 * pitch + part // 4 * count + first + place] = 1
    return as_half(move)


def whole_part(v, size):
    return jnp.floor((v + 0.5) * (1.0 / size))


def one_hot(target, lanes):
    lane = lax.broadcasted_iota(jnp.int32, (1, lanes), 1).astype(FULL)
    return jnp.where(lane == target, 1.0, 0.0).astype(HALF)


def fill_columns(cols):
    row = lax.broadcasted_iota(jnp.int32, (256, 1), 0).astype(FULL)
    a = whole_part(row, 23)
    k = row - 23.0 * a
    for z in range(2):
        target = (22.0 - k) * 12.0 + (z * 6.0) + a
        cols[z] = one_hot(jnp.where(row < 138.0, target, -1.0), 384)


def fill_select(select):
    row = lax.broadcasted_iota(jnp.int32, (128, 1), 0).astype(FULL)
    b = whole_part(row, 32)
    slot = row - 32.0 * b
    layer = whole_part(slot, 5)
    z = whole_part(layer, 2)
    upper = z * 256.0 + (slot - 5.0 * layer) * 32.0 + (layer - 2.0 * z) * 16.0
    surface = 160.0 + (slot - 20.0) * 16.0
    target = jnp.where(slot < 20.0, upper, surface) + b * 4.0
    for c in range(4):
        select[c * 128 : c * 128 + 128, :] = one_hot(
            jnp.where(slot < 24.0, target + float(c), -1.0), 512
        )


def dot(a, b):
    return jnp.dot(a, b, preferred_element_type=FULL)


def dot_nt(a, b):
    return lax.dot_general(a, b, (((1,), (1,)), ((), ())), preferred_element_type=FULL)


def dot_tn(a, b):
    return lax.dot_general(a, b, (((0,), (0,)), ((), ())), preferred_element_type=FULL)


def normalise(v):
    mean = jnp.mean(v, -1, keepdims=True)
    centred = v - mean
    spread = lax.rsqrt(jnp.mean(centred * centred, -1, keepdims=True) + norm_eps)
    return centred * spread, spread


def normalise_back(dy, unit, spread, gain):
    dunit = dy * gain
    inner = jnp.mean(dunit * unit, -1, keepdims=True)
    return spread * (dunit - jnp.mean(dunit, -1, keepdims=True) - unit * inner)


def head_lanes(h):
    lane = lax.broadcasted_iota(jnp.int32, (1, WIDTH), 1)
    return (lane >= h * HEAD) & (lane < (h + 1) * HEAD)


def head_mask(h):
    return jnp.where(head_lanes(h), 1.0, 0.0).astype(HALF)


def build_bias(tbl, cols, xs, bias, edges):
    for z in range(2):
        for a in range(6):
            for zu in range(2):
                start = ((z * 2 + zu) * 6 + a) * 138
                piece = tbl[0:HEADS, start : start + 138]
                piece = jnp.concatenate((piece, jnp.zeros((HEADS, 118), FULL)), 1)
                for p in range(2):
                    for half in range(2):
                        xs[zu * 2 + half, pl.ds(p * 12 + z * 6 + a, HEADS, stride=24), :] = piece[
                            :, half * 128 : half * 128 + 128
                        ]
    total = None
    for zu in range(2):
        x = jnp.concatenate((xs[zu * 2, :CELLS, :], xs[zu * 2 + 1, :CELLS, :]), 1)
        high = x.astype(HALF)
        left = x - high.astype(FULL)
        mid = left.astype(HALF)
        low = (left - mid.astype(FULL)).astype(HALF)
        term = dot(jnp.concatenate((high, mid, low), 0), cols[zu])
        total = term if total is None else total + term
    table = total[:CELLS] + total[CELLS : 2 * CELLS] + total[2 * CELLS :]
    row = lax.broadcasted_iota(jnp.int32, (CELLS, 1), 0).astype(FULL)
    lane = lax.broadcasted_iota(jnp.int32, (1, CELLS), 1).astype(FULL)

    part = whole_part
    even = part(row, 12) - 2.0 * part(part(row, 12), 2) == 0.0
    table = jnp.where(even, pltpu.roll(table, 384 - 12, 1), table)
    if edges is not None:
        last_section, last_band = edges
        row12, lane12 = row - 12.0 * part(row, 12), lane - 12.0 * part(lane, 12)
        row_z, lane_z = part(row12, 6), part(lane12, 6)
        row_a, lane_a = part(row12 - 6.0 * row_z, 3), part(lane12 - 6.0 * lane_z, 3)
        apart = jnp.abs(row_z - lane_z) * last_section + jnp.abs(row_a - lane_a) * last_band
        blocked = apart > 0.5
    for j in range(6):
        shift = (10 - 2 * j) * 12
        moved = pltpu.roll(table, 384 - shift, 1) if shift else table
        moved = moved[:, :CELLS]
        if edges is not None:
            moved = jnp.where(blocked, neg_fill, moved)
        for h in range(HEADS):
            bias[h * CELLS + j * 24 : h * CELLS + j * 24 + 24, :] = moved[h * 24 : h * 24 + 24, :]


def by_head(rows):
    return jnp.concatenate([rows * head_mask(h) for h in range(HEADS)], 0)


def attend(q, k, v, bias, prob):
    scores = dot_nt(by_head(q), k)
    for h in range(HEADS):
        rows = slice(h * CELLS, (h + 1) * CELLS)
        score = scores[rows] * HEAD ** (-0.5) + bias[rows, :]
        expo = jnp.exp(score - jnp.max(score, -1, keepdims=True))
        prob[rows, :] = (expo * (1.0 / jnp.sum(expo, -1, keepdims=True))).astype(HALF)
    mixed = jnp.zeros((CELLS, WIDTH), FULL)
    for h in range(HEADS):
        term = dot(prob[h * CELLS : (h + 1) * CELLS, :], v)
        mixed = jnp.where(head_lanes(h), term, mixed)
    return mixed.astype(HALF)


def attend_back(dmixed, q, k, v, prob):
    dheads = by_head(dmixed)
    dweights = dot_nt(dheads, v)
    dv = dot_tn(prob[...], dheads)
    dscores = []
    for h in range(HEADS):
        rows = slice(h * CELLS, (h + 1) * CELLS)
        full = prob[rows, :].astype(FULL)
        inner = jnp.sum(dweights[rows] * full, -1, keepdims=True)
        dscores.append((full * (dweights[rows] - inner) * HEAD ** (-0.5)).astype(HALF))
    dk = dot_tn(jnp.concatenate(dscores, 0), by_head(q))
    dq = jnp.zeros((CELLS, WIDTH), FULL)
    for h in range(HEADS):
        dq = jnp.where(head_lanes(h), dot(dscores[h], k), dq)
    return dq.astype(HALF), dk.astype(HALF), dv.astype(HALF)


def gelu_parts(u):
    below = 0.5 * (1.0 + lax.erf(u * (0.5**0.5)))
    slope = below + u * (jnp.exp(-0.5 * u * u) * (2.0 * np.pi) ** (-0.5))
    return below, slope


def forward_half(x, gains, wqkv, wproj, bias, prob):
    unit, spread = normalise(x)
    hidden = (unit * gains[0:1, :]).astype(HALF)
    qkv = dot(hidden, wqkv[...]).astype(HALF)
    q, k, v = (qkv[:, n * WIDTH : (n + 1) * WIDTH] for n in range(3))
    mixed = attend(q, k, v, bias, prob)
    return (q, k, v), x + dot(mixed, wproj[...])


def backward(dflat, x, qkv, prob, resid, slope, gains, wqkv, wproj, wup, wdown):
    q, k, v = qkv
    dactive = dot(dflat, wdown[...])
    dupward = (dactive * slope).astype(HALF)
    dnormed = dot_nt(dupward, wup[...])
    unit, spread = normalise(resid)
    dresid = dflat.astype(FULL) + normalise_back(dnormed, unit, spread, gains[1:2, :])
    dmixed = dot_nt(dresid.astype(HALF), wproj[...]).astype(HALF)
    dq, dk, dv = attend_back(dmixed, q, k, v, prob)
    dhidden = dot_nt(dq, wqkv[:, :WIDTH])
    dhidden = dhidden + dot_nt(dk, wqkv[:, WIDTH : 2 * WIDTH])
    dhidden = dhidden + dot_nt(dv, wqkv[:, 2 * WIDTH :])
    unit, spread = normalise(x)
    return dresid + normalise_back(dhidden, unit, spread, gains[0:1, :])


def gather_patches(upper, surface, section, select, ff, ft):
    base = 4 * section - 2
    for z in range(2):
        for a in range(2):
            level = jnp.maximum(base + 2 * z + a, 0)
            for v in range(5):
                field = upper[v, level].astype(FULL)
                if z == 0:
                    field = jnp.where(section == 0, 0.0, field)
                slot = (z * 2 + a) * 5 + v
                ff[slot * 24 : slot * 24 + 24, 0:48] = field
    for v in range(4):
        field = jnp.where(section == 0, surface[v].astype(FULL), 0.0)
        ff[(20 + v) * 24 : (21 + v) * 24, 0:48] = field
    pad = jnp.zeros((8, 128), FULL)
    for i in range(6):
        pieces = []
        for b in range(4):
            pieces += [ff[pl.ds(4 * i + b, 24, stride=24), :], pad]
        ft[i * 48 : i * 48 + 48, :] = jnp.concatenate(pieces, 0).T[:48]
    raw = [ft[pl.ds(c, 72, stride=4), :].astype(HALF) for c in range(4)]
    both = dot(jnp.concatenate(raw, 1), select[...])
    return jnp.concatenate((both[:, :256], both[:, 256:]), 0).astype(HALF)


def flag(axis):
    last = lax.axis_index(axis) == lax.axis_size(axis) - 1
    return jnp.where(last, 1.0, 0.0)


def table_rows(tbl, block, table):
    for h in range(HEADS):
        table[h : h + 1, 0 : tbl.shape[-1]] = tbl[block * HEADS + h]


def first_kernel(*refs):
    names = (
        "tbl", "upper", "surface", "to_inner", "uembed", "sembed", "gains",
        "wqkv", "wproj", "wup", "wdown", "cot", "out_first", "out_cot",
    )
    count = len(names)
    source, refs = refs[:count], refs[count:]
    patch_o, x_o, qkv_o, prob, resid_o, slope_o, send_o, *keep_o = refs[:11]
    refs = refs[11:]
    local, refs = refs[:count], refs[count:]
    ff, ft, emb, cots, table, xs, bias, cols, select, sems = refs
    copies = {}
    for n, name in enumerate(names):
        start, end = source[n], local[n]
        if name[0] == "w":
            start = start.at[0]
        elif name == "tbl":
            start = start.at[pl.ds(0, HEADS)]
        elif name == "uembed":
            end = emb.at[pl.ds(0, 160)]
        elif name == "sembed":
            end = emb.at[pl.ds(160, 64)]
        copies[name] = pltpu.make_async_copy(start, end, sems.at[n])
        copies[name].start()
    have = dict(zip(names, local))

    def wait(*which):
        for name in which:
            copies[name].wait()

    emb[224:256, :] = jnp.zeros((32, WIDTH), HALF)
    fill_columns(cols)
    fill_select(select)
    wait("tbl", "upper", "surface", "to_inner", "uembed", "sembed", "gains", "wqkv")
    table_rows(have["tbl"], 0, table)
    build_bias(table, cols, xs, bias, None)
    section = lax.axis_index("section")
    patch = gather_patches(have["upper"], have["surface"], section, select, ff, ft)
    patch = dot(have["to_inner"][...], patch).astype(HALF)
    patch_o[...] = patch
    latent = dot(patch, emb[...]).astype(HALF)
    x_o[...] = latent
    x = latent.astype(FULL)
    gains = have["gains"].at[0]
    wait("wproj", "wup", "wdown", "cot", "out_first", "out_cot")
    cot = have["cot"]
    for a in range(6):
        for o in range(12):
            cots[(a * 12 + o) * 2 : (a * 12 + o) * 2 + 2, :] = cot[a, o].astype(FULL)
    ready = dot(have["out_cot"][...], cots[:CELLS, :].astype(HALF))
    qkv, resid = forward_half(x, gains, have["wqkv"], have["wproj"], bias, prob)
    for n in range(3):
        qkv_o[n] = qkv[n]
    resid_o[...] = resid
    unit, spread = normalise(resid)
    normed = (unit * gains[1:2, :]).astype(HALF)
    upward = dot(normed, have["wup"][...])
    below, slope = gelu_parts(upward)
    slope_o[...] = slope.astype(HALF)
    active = (upward * below).astype(HALF)
    result = (resid + dot_nt(active, have["wdown"][...])).astype(HALF)
    moved = dot(have["out_first"][...], result) + ready
    send_o[...] = moved[160:].astype(HALF)
    for n in range(4):
        keep_o[n][...] = moved[n * 40 : n * 40 + 36].astype(HALF)


def second_bias(tbl, after, bias, table, xs, cols):
    fill_columns(cols)
    table_rows(tbl, 1, table)
    build_bias(table, cols, xs, bias, (flag("section"), flag("lat")))


def second_kernel(*refs):
    parts, rest = refs[:4], refs[4:]
    gains, wqkv, wproj, wup, wdown, bias, into, out_of, send_o = rest[:9]
    keep, stack, prob = rest[9:13], rest[13], rest[14]
    stack[...] = jnp.zeros_like(stack)
    for n, part in zip(order, parts):
        stack[n * 80 : n * 80 + 72, :] = part[...]
    both = dot(into[...], stack[...])
    x, dflat = both[:CELLS], both[CELLS:].astype(HALF)
    gains, wqkv, wproj, wup, wdown = (w.at[1] for w in (gains, wqkv, wproj, wup, wdown))
    qkv, resid = forward_half(x, gains, wqkv, wproj, bias, prob)
    unit, spread = normalise(resid)
    normed = (unit * gains[1:2, :]).astype(HALF)
    upward = dot(normed, wup[...])
    slope = gelu_parts(upward)[1]
    dx = backward(dflat, x, qkv, prob, resid, slope, gains, wqkv, wproj, wup, wdown)
    moved = dot(out_of[...], dx.astype(HALF))
    send_o[...] = moved[96:].astype(HALF)
    for n in range(4):
        keep[n][...] = moved[n * 24 : n * 24 + 18].astype(HALF)


def third_kernel(*refs):
    parts, rest = refs[:4], refs[4:]
    gains, wqkv, wproj, wup, wdown, patch, x_i, qkv_i, prob, resid, slope, into, out_of = rest[:13]
    grad_o, mine_o, other_o, stack, terms = rest[13:]
    stack[...] = jnp.zeros_like(stack)
    for n, part in zip(order, parts):
        stack[n * 48 : n * 48 + 36, :] = part[...]
    dflat = dot(into[...], stack[...]).astype(HALF)
    qkv = tuple(qkv_i[n] for n in range(3))
    gains, wqkv, wproj, wup, wdown = (w.at[0] for w in (gains, wqkv, wproj, wup, wdown))
    dx = backward(
        dflat, x_i[...].astype(FULL), qkv, prob, resid[...], slope[...].astype(FULL),
        gains, wqkv, wproj, wup, wdown,
    )
    grad = dx.astype(HALF)
    moved = dot(out_of[...], grad).astype(HALF)
    for z in range(2):
        for a in range(6):
            grad_o[z, a] = moved[(z * 6 + a) * 16 : (z * 6 + a) * 16 + 12]
    total = dot_tn(patch[...], grad)
    terms[0:224, :] = total[:224, :128]
    terms[224:336, :] = jnp.concatenate((total[:112, 128:], total[112:224, 128:]), 1)
    place = lax.axis_index("section") % 2
    mine_o[...] = terms[pl.ds(pl.multiple_of(place * 168, 8), 168), :].astype(HALF)
    other_o[...] = terms[pl.ds(pl.multiple_of(168 - place * 168, 8), 168), :].astype(HALF)


vmem = pl.BlockSpec(memory_space=pltpu.VMEM)
hbm = pl.BlockSpec(memory_space=pltpu.HBM)


def call(kernel, outs, scratch, *args, spec=vmem, out=vmem, room=30, size=1):
    return pl.pallas_call(
        kernel,
        out_shape=outs,
        in_specs=[spec for a in args],
        out_specs=jax.tree.map(lambda _: out, outs),
        scratch_shapes=scratch,
        compiler_params=pltpu.CompilerParams(vmem_limit_bytes=room * 2**20),
        cost_estimate=pl.CostEstimate(flops=1000000, bytes_accessed=size * 1000000, transcendentals=0),
    )(*args)


def shape(dims, dtype=HALF):
    return jax.ShapeDtypeStruct(dims, dtype)


def fetch(block, steps):
    names = ("lon", "lat", "section")
    axes = [name for name in names if steps.get(name, 0)]
    if not axes:
        return block
    sizes = [lax.axis_size(name) for name in axes]
    pairs = []
    for place in np.ndindex(*sizes):
        source = [(p + steps[name]) % n for p, name, n in zip(place, axes, sizes)]
        pairs.append(
            (int(np.ravel_multi_index(source, sizes)), int(np.ravel_multi_index(place, sizes)))
        )
    return lax.ppermute(block, tuple(axes), pairs)


order = (3, 1, 2, 0)


def exchange(keep, got, way):
    pitch = got.shape[0] // 4
    blocks = []
    for n in order:
        block = jnp.concatenate((keep[n], got[n * pitch : (n + 1) * pitch]), 0)
        blocks.append(fetch(block, {"lat": way * (n // 2), "lon": way * (n % 2)}))
    return blocks


def swap(block, flips):
    names = ("lon", "lat", "section")
    axes = [name for name in names if flips.get(name, 0)]
    sizes = [lax.axis_size(name) for name in axes]
    pairs = []
    for place in np.ndindex(*sizes):
        source = [p ^ flips[name] for p, name in zip(place, axes)]
        pairs.append(
            (int(np.ravel_multi_index(source, sizes)), int(np.ravel_multi_index(place, sizes)))
        )
    return lax.ppermute(block, tuple(axes), pairs)


def add_up(mine, other):
    total = (mine.astype(FULL) + swap(other, {"section": 1}).astype(FULL)).astype(HALF)
    bits = []
    for name in ("section", "lat", "lon"):
        size = lax.axis_size(name)
        if size & (size - 1) or size < 2:
            raise ValueError("axis size")
        bits += [(name, 1 << n) for n in range(name == "section", size.bit_length() - 1)]
    for n in range(0, len(bits), 2):
        pair = [{name: bit} for name, bit in bits[n : n + 2]]
        if len(pair) == 1:
            total = total.astype(FULL) + swap(total, pair[0]).astype(FULL)
        else:
            one, two = pair
            three = dict(one)
            for name, bit in two.items():
                three[name] = three.get(name, 0) | bit
            near, far, last = (swap(total, step).astype(FULL) for step in (one, two, three))
            total = (total.astype(FULL) + near) + (far + last)
        total = total.astype(HALF)
    return total, swap(total, {"section": 1})


def last_kernel(scale, mine, other, upper_o, surface_o, halves, both, sems):
    place = lax.axis_index("section") % 2
    halves[pl.ds(pl.multiple_of(place * 168, 8), 168), :] = mine[...].astype(FULL) * scale
    halves[pl.ds(pl.multiple_of(168 - place * 168, 8), 168), :] = other[...].astype(FULL) * scale
    both[:, 0:128] = halves[0:224, :]
    last = halves[224:336, :]
    both[0:112, 128:192] = last[:, :64]
    both[112:224, 128:192] = last[:, 64:]
    copies = [
        pltpu.make_async_copy(both.at[pl.ds(0, 160)], upper_o, sems.at[0]),
        pltpu.make_async_copy(both.at[pl.ds(160, 64)], surface_o, sems.at[1]),
    ]
    for copy in copies:
        copy.start()
    for copy in copies:
        copy.wait()


def on_device(
    upper_fields,
    surface_fields,
    upper_embed,
    surface_embed,
    norm_gains,
    qkv_weight,
    proj_weight,
    up_weight,
    down_weight,
    earth_bias,
    out_grad,
):
    sections, bands = lax.axis_size("section"), lax.axis_size("lat")
    levels, rows, columns, width = out_grad.shape
    positions = earth_bias.shape[-1]
    table = earth_bias.transpose(0, 1, 3, 2, 4).reshape(2 * HEADS, 1, positions)
    weights = (norm_gains, qkv_weight, proj_weight, up_weight, down_weight.transpose(0, 2, 1))

    def from_cot(z, a, o):
        return (a * 12 + o) * 2 + z

    operands = (
        table, upper_fields, surface_fields, jnp.asarray(natural_to_inner()), upper_embed,
        surface_embed, *weights, out_grad.transpose(1, 2, 0, 3),
        jnp.asarray(octants_out(36, 0, True, inner_row)),
        jnp.asarray(octants_out(36, 18, True, from_cot)),
    )
    local = [
        pltpu.VMEM(v.shape[1:] if 7 <= n < 11 else v.shape, v.dtype) for n, v in enumerate(operands)
    ]
    local[0] = pltpu.VMEM((HEADS, 1, positions), FULL)
    local[4] = local[5] = pltpu.VMEM((16, 128), HALF)
    scratch_bias = [pltpu.VMEM((8, 3328), FULL), pltpu.VMEM((4, 192, 128), FULL)]
    scratch_cols = pltpu.VMEM((2, 256, 384), HALF)
    held = [
        shape((CELLS, 256)),
        shape((CELLS, WIDTH)),
        shape((3, CELLS, WIDTH)),
        shape((HEADS * CELLS, CELLS)),
        shape((CELLS, WIDTH), FULL),
        shape((CELLS, 4 * WIDTH)),
    ]
    patch, x, qkv, prob, resid, slope, send, *keep = call(
        first_kernel,
        held + [shape((144, WIDTH))] + [shape((36, WIDTH))] * 4,
        local
        + [
            pltpu.VMEM((576, 128), FULL),
            pltpu.VMEM((288, 128), FULL),
            pltpu.VMEM((256, WIDTH), HALF),
            pltpu.VMEM((160, WIDTH), FULL),
        ]
        + scratch_bias
        + [
            pltpu.VMEM((HEADS * CELLS, CELLS), FULL),
            scratch_cols,
            pltpu.VMEM((512, 512), HALF),
            pltpu.SemaphoreType.DMA((len(operands),)),
        ],
        *(pltpu.with_memory_space_constraint(v, pltpu.HBM) for v in operands),
        spec=hbm,
    )
    bias_shape = shape((HEADS * CELLS, CELLS), FULL)
    got = fetch(send, {"section": 1})
    bias = call(second_bias, bias_shape, [*scratch_bias, scratch_cols], table, got)
    into = np.concatenate((octants_in(36, 0, False), octants_in(36, 18, False)), 0)
    send, *keep = call(
        second_kernel,
        [shape((72, WIDTH))] + [shape((18, WIDTH))] * 4,
        [pltpu.VMEM((320, WIDTH), HALF), pltpu.VMEM((HEADS * CELLS, CELLS), HALF)],
        *exchange(keep, got, 1), *weights, bias,
        jnp.asarray(into), jnp.asarray(octants_out(18, 0, False, inner_row)),
    )
    latent_grad, mine, other = call(
        third_kernel,
        [shape((2, 6, 12, WIDTH)), shape((168, 128)), shape((168, 128))],
        [pltpu.VMEM((192, WIDTH), HALF), pltpu.VMEM((336, 128), FULL)],
        *exchange(keep, fetch(send, {"section": -1}), -1), *weights, patch, x, qkv, prob, resid, slope,
        jnp.asarray(octants_in(18, 0, True)), jnp.asarray(inner_to_padded()),
    )
    scale = float(levels * sections * rows * bands * columns * lax.axis_size("lon")) ** (-0.5)
    upper_grad, surface_grad = call(
        functools.partial(last_kernel, scale),
        [shape((160, WIDTH), FULL), shape((64, WIDTH), FULL)],
        [
            pltpu.VMEM((336, 128), FULL),
            pltpu.VMEM((224, WIDTH), FULL),
            pltpu.SemaphoreType.DMA((2,)),
        ],
        *add_up(mine, other),
        out=hbm,
    )
    return (latent_grad, upper_grad, surface_grad)


def solution(mesh):
    placed = (
        P(None, None, "lat", "lon"),
        P(None, "lat", "lon"),
        P(),
        P(),
        P(),
        P(),
        P(),
        P(),
        P(),
        P(None, "lat", "section", None, None),
        P("section", "lat", "lon", None),
    )
    return jax.shard_map(
        on_device,
        mesh=mesh,
        in_specs=placed,
        out_specs=(P("section", "lat", "lon", None), P(), P()),
        check_vma=False,
    )
```
